32 devices in a mesh: beam: 2 (over y), sub: 8 (over z, x), tm: 2 (over core).
Axes of the slice: x: 2, y: 2, z: 4, core: 2. Of those that a mesh axis runs over, the one named last changes fastest.
Arguments:
- filterbank: bfloat16 [2048, 1024], P(('beam', 'sub'), 'tm'), parts along dimension 0, may hold values from -6 to 6
- bandpass: float32 [2048], P(('beam', 'sub')), parts along dimension 0, may hold values from 0.3 to 3
- local_delays: int32 [7, 1024], P(None, 'sub'), may hold values from 0 to 32, as said below
- cross_delays: int32 [3, 128], P(None, 'sub'), may hold values from 0 to 32, as said below
Outputs:
- dedispersed: float32 [256, 1024], P(('beam', 'sub'), 'tm'), parts along dimension 0
The draws below stay inside these ranges and needn't reach their ends.
There are 2 independent parts, one for each index of `beam`. The reference program is written for one: setup_inputs(seed, part) draws one part's arguments, and reference() takes and returns one part's arrays. A program takes and returns all parts, laid end to end along the dimension named above; an argument that names none is the same for every part. Nothing has to cross between parts.
Inputs may be any that keep to these rules, and one draw needn't show every extreme that they name: `local_delays`: whole samples; level m of the local levels reads its first entries of each block of 128. `cross_delays`: whole samples.
All inputs are finite; a program needn't handle non-finite values.
Results may differ from the reference program's by a relative error of at most 0.0003.
Values may be sent and summed in bfloat16 or wider, within the bound.
No kernel may reach another device: no remote copies, remote signals or barrier semaphores. Data moves between devices by JAX's collectives and lax.ppermute only.
A program may use at most 64 MiB of HBM per device.

```python
import math
import jax
import jax.numpy as jnp
from jax import lax

CH_DEV = 128
KD = 16
CHANNELS = 1024
SAMPLES = 1024
TRIALS = 128
LLEV = 7
XLEV = 3
SHIFT_MAX = 32
N_SUB = 8


def draw_local_delays(key, part):
    delays = jax.random.randint(key, (LLEV, CHANNELS), 0, SHIFT_MAX + 1, dtype=jnp.int32)
    return delays.at[0, 0].set(SHIFT_MAX)


def draw_cross_delays(key, part):
    delays = jax.random.randint(jax.random.fold_in(key, 7), (XLEV, TRIALS), 0, SHIFT_MAX + 1, dtype=jnp.int32)
    return delays.at[XLEV - 1, 0].set(SHIFT_MAX)


def level_of(own_key, dims, pieces, least, top_value):
    level, own = 1.0, jax.random.fold_in(own_key, 6)
    for axis_at, parts in pieces:
        draws = jnp.exp(jax.random.uniform(jax.random.fold_in(own, axis_at), (parts,), jnp.float32, least / len(pieces), top_value / len(pieces)))
        level = level * jnp.repeat(draws, dims[axis_at] // parts).reshape([-1 if axis == axis_at else 1 for axis in range(len(dims))])
    return level


def scatter_about(own_key, shape, width, bound, split=(), kind=jnp.bfloat16):
    factor_of = level_of(own_key, shape, split, -0.22, 0.18) if split else 1.0
    array = jax.random.normal(own_key, shape, jnp.float32) * width * factor_of
    return jnp.minimum(jnp.maximum(array, -bound), bound).astype(kind)


def setup_inputs(seed: int = 0, part: int = 0) -> dict:
    streams_of = jax.random.split(jax.random.key(seed), 5)
    own_keys = jax.random.split(jax.random.fold_in(streams_of[4], part), 5)
    filterbank = scatter_about(own_keys[0], (CHANNELS, SAMPLES), 1.0, 6.0, ((0, 8), (1, 2)))
    bandpass = jnp.clip(jnp.exp(math.log(3.0) - 2.3025851 * jax.random.uniform(own_keys[1], (CHANNELS,), jnp.float32) ** level_of(own_keys[1], (CHANNELS,), ((0, 8),), -0.2, 0.2)), 0.3, 3.0)
    local_delays = draw_local_delays(jax.random.fold_in(streams_of[4], 71), part)
    cross_delays = draw_cross_delays(jax.random.fold_in(streams_of[4], 71), part)
    return dict(filterbank=filterbank, bandpass=bandpass, local_delays=local_delays, cross_delays=cross_delays)


def delayed(upper, delays):
    padded = jnp.pad(upper, ((0, 0), (SHIFT_MAX, 0)))
    columns = lax.broadcasted_iota(jnp.int32, upper.shape, 1)
    offsets = columns + SHIFT_MAX - delays[:, None].astype(jnp.int32)
    return jnp.take_along_axis(padded, offsets, axis=1)

def reference(filterbank, bandpass, local_delays, cross_delays):
    corrected = filterbank.astype(jnp.float32) * bandpass[:, None]
    padded = jnp.pad(corrected, ((0, 0), (15, 15)))
    window_total = lax.reduce_window(padded, jnp.zeros((), padded.dtype), lax.add, (1, 31), (1, 1), 'VALID')
    current = corrected - window_total / 31.0
    trial_count = 1
    for level_index in range(LLEV):
        band_count = current.shape[0] // trial_count
        grouped = current.reshape(band_count // 2, 2, trial_count, SAMPLES)
        lower = grouped[:, 0]
        upper = grouped[:, 1]
        new_count = min(2 * trial_count, KD)
        if new_count > trial_count:
            lower = jnp.concatenate([lower, lower], axis=1)
            upper = jnp.concatenate([upper, upper], axis=1)
        per_device = band_count // 2 // N_SUB * new_count
        delays = local_delays[level_index].reshape(N_SUB, CH_DEV)[:, :per_device].reshape(-1)
        current = lower.reshape(-1, SAMPLES) + delayed(upper.reshape(-1, SAMPLES), delays)
        trial_count = new_count
    for level_index in range(XLEV):
        grouped = current.reshape(-1, 2, trial_count, SAMPLES)
        lower = jnp.concatenate([grouped[:, 0], grouped[:, 0]], axis=1)
        upper = jnp.concatenate([grouped[:, 1], grouped[:, 1]], axis=1)
        current = lower.reshape(-1, SAMPLES) + delayed(upper.reshape(-1, SAMPLES), cross_delays[level_index])
        trial_count = 2 * trial_count
    return current * (1.0 / math.sqrt(CHANNELS))
```

```python
import functools
import math

import jax
import jax.numpy as jnp
from jax import lax
from jax.experimental import pallas as pl
from jax.experimental.pallas import tpu as pltpu
from jax.sharding import PartitionSpec as P

LANES = 128
SUBLANES = 8
WINDOW = 31
HALF = WINDOW // 2


def iota(shape, axis):
    return lax.broadcasted_iota(jnp.int32, shape, axis)


def turned(x, index, axis):
    return jnp.take_along_axis(x, index, axis=axis, mode="promise_in_bounds")


def blocks_of(columns):
    return -(-columns // LANES)


def later(tiles, shift, count):
    lane = iota(shift.shape, 1)
    index = (lane - shift) & (LANES - 1)
    same = lane >= shift
    spun = [turned(tile, index, 1) for tile in tiles]
    zero = jnp.zeros(shift.shape, jnp.float32)
    got = []
    for block in range(count):
        here = spun[block] if block < len(spun) else zero
        prior = spun[block - 1] if 0 < block <= len(spun) else zero
        got.append(jnp.where(same, here, prior))
    return got


def folded(tiles):
    row = iota(tiles[0].shape, 0)
    reach = SUBLANES // 2
    while reach:
        first = row & reach == 0
        tiles = [
            jnp.where(
                first,
                a + pltpu.roll(a, SUBLANES - reach, 0),
                b + pltpu.roll(b, reach, 0),
            )
            for a, b in zip(tiles[:reach], tiles[reach:])
        ]
        reach //= 2
    return tiles[0]


def plane_kernel(shift_max, cross_count, fb_ref, bp_ref, ld_ref, cd_ref, out_ref, level_ref):
    rows, span = fb_ref.shape
    local_levels = ld_ref.shape[0]
    trials = cd_ref.shape[1]
    grow = trials.bit_length() - 1
    square = (rows, LANES)
    lane, row = iota(square, 1), iota(square, 0)
    inner, outer = row & (SUBLANES - 1), row >> 3

    pick = lane == inner * trials + outer
    parts = [jnp.where(pick, ld_ref[m : m + 1, :], 0).astype(jnp.bfloat16) for m in range(grow)]
    tail = jnp.zeros(square, jnp.int32)
    for m in range(grow, local_levels):
        bit = m - grow
        use = (lane == (inner >> (bit + 1)) * trials + outer) & (inner >> bit & 1 == 1)
        tail = tail + jnp.where(use, ld_ref[m : m + 1, :], 0)
    parts.append(tail.astype(jnp.float32).astype(jnp.bfloat16))
    rest = bp_ref[...]
    for _ in range(3):
        part = rest.astype(jnp.bfloat16)
        rest = rest - part.astype(jnp.float32)
        parts.append(jnp.where(pick, part.astype(jnp.float32), 0.0).astype(jnp.bfloat16))
    ones = jnp.ones((rows, LANES), jnp.bfloat16)
    spread = jnp.dot(jnp.concatenate(parts, axis=0), ones, preferred_element_type=jnp.float32)
    delays = spread[: (grow + 1) * rows].astype(jnp.int32)
    gain = spread[(grow + 1) * rows :]
    gain = (gain[:rows] + gain[rows : 2 * rows] + gain[2 * rows :]) * (1.0 / WINDOW)

    at = iota((2 * LANES, LANES), 0) - LANES
    to = iota((2 * LANES, LANES), 1) - HALF
    band = jnp.where(at == to, float(WINDOW), 0.0) - jnp.where(jnp.abs(at - to) <= HALF, 1.0, 0.0)
    band = band.astype(jnp.bfloat16)
    whole = span // LANES
    start_blocks = blocks_of(span + 2 * HALF)
    for block in range(start_blocks):
        low, high = max(block - 1, 0), min(block + 1, whole)
        part = band[(low - block + 1) * LANES : (high - block + 1) * LANES]
        level_ref[block * rows : (block + 1) * rows, :] = jnp.dot(
            fb_ref[:, low * LANES : high * LANES], part, preferred_element_type=jnp.float32
        )

    first_span = lax.axis_index("tm") == 0
    early = jnp.logical_and(iota((SUBLANES, LANES), 1) < HALF, first_span)
    bands = []
    for e in range(trials):
        scale = gain[e * SUBLANES : (e + 1) * SUBLANES]
        tiles = []
        for block in range(start_blocks):
            tile = level_ref[pl.ds(block * rows + e, SUBLANES, stride=trials), :] * scale
            tiles.append(jnp.where(early, 0.0, tile) if block == 0 else tile)
        bands.append(tiles)
    plane = [bands]
    for m in range(grow):
        count = blocks_of(span + 2 * HALF + (m + 1) * shift_max)
        old, plane = plane, []
        for c in range(2):
            for i, held in enumerate(old):
                j = c * len(old) + i
                new = []
                for e in range(len(held) // 2):
                    at_row = m * rows + (e * 2 * len(old) + j) * SUBLANES
                    moved = later(held[2 * e + 1], delays[at_row : at_row + SUBLANES], count)
                    base = held[2 * e]
                    new.append([base[b] + moved[b] if b < len(base) else moved[b] for b in range(count)])
                plane.append(new)
    count = blocks_of(span + 2 * HALF + local_levels * shift_max)
    row8 = iota((SUBLANES, LANES), 0)
    lane8 = iota((SUBLANES, LANES), 1)
    eye = iota((trials, trials), 0) == iota((trials, trials), 1)
    notes = [
        jnp.sum(jnp.where(eye, cd_ref[l : l + 1, :].astype(jnp.float32), 0.0), axis=1, keepdims=True)
        for l in range(cross_count)
    ]
    for j in range(trials):
        at_row = grow * rows + j * SUBLANES
        moved = later(plane[j][0], delays[at_row : at_row + SUBLANES], count)
        zero = jnp.zeros((SUBLANES, LANES), jnp.float32)
        tile = folded(moved + [zero] * (SUBLANES - count))
        for l in range(cross_count):
            tile = jnp.where((row8 == SUBLANES - 1) & (lane8 == l), notes[l][j : j + 1, :], tile)
        out_ref[j * SUBLANES : (j + 1) * SUBLANES, :] = tile


def merge_kernel(spans, span, plane_blocks, scale, in_ref, out_ref):
    devices = SUBLANES
    levels = devices.bit_length() - 1
    per_span = span // LANES
    out_blocks = spans * per_span
    tile_shape = (SUBLANES, LANES)
    lane, place = iota(tile_shape, 1), iota(tile_shape, 0)
    notes = in_ref[pl.ds(SUBLANES - 1, devices, stride=spans * SUBLANES), :]
    steps = [
        turned(notes, jnp.full(tile_shape, l, jnp.int32), 1).astype(jnp.int32) for l in range(levels)
    ]
    total = [jnp.zeros(tile_shape, jnp.float32) for _ in range(out_blocks)]
    zero = jnp.zeros(tile_shape, jnp.float32)
    kept = {}
    for q in range(devices):
        shift = jnp.zeros(tile_shape, jnp.int32)
        for l in range(levels):
            if q >> l & 1:
                high = q >> (l + 1) << (l + 1)
                if (l, high) not in kept:
                    low_mask = (1 << (l + 1)) - 1
                    kept[l, high] = turned(steps[l], high | (place & low_mask), 0)
                shift = shift + kept[l, high]
        source = lane + HALF - shift
        index = source & (LANES - 1)
        before, after = source < 0, source >= LANES
        spun = []
        for block in range(blocks_of(spans * span + HALF)):
            line = None
            for k in range(spans):
                own = block - k * per_span
                if 0 <= own < plane_blocks:
                    at_row = (q * spans + k) * SUBLANES + own
                    piece = in_ref[at_row : at_row + 1, :]
                    line = piece if line is None else line + piece
            spun.append(turned(jnp.broadcast_to(line, tile_shape), index, 1))
        for block in range(out_blocks):
            prior = spun[block - 1] if block else zero
            got = jnp.where(before, prior, jnp.where(after, spun[block + 1], spun[block]))
            total[block] = total[block] + got
    for block in range(out_blocks):
        out_ref[pl.ds(block, devices, stride=out_blocks), :] = total[block] * scale


def delayed(upper, delays):
    columns = lax.broadcasted_iota(jnp.int32, upper.shape, 1) - delays[:, None]
    moved = jnp.take_along_axis(upper, jnp.maximum(columns, 0), axis=1)
    return jnp.where(columns >= 0, moved, 0.0)


def shards(filterbank, bandpass, local_delays, cross_delays):
    rows, span = filterbank.shape
    trials = cross_delays.shape[1]
    subs, spans = lax.axis_size("sub"), lax.axis_size("tm")
    cross_levels = subs.bit_length() - 1
    local_levels = local_delays.shape[0]
    shift_max = span // 16
    merged = SUBLANES.bit_length() - 1
    plane_blocks = blocks_of(span + 2 * HALF + local_levels * shift_max)
    assert rows == trials * SUBLANES and trials == SUBLANES * spans
    assert plane_blocks < SUBLANES and rows == LANES

    vmem = pl.BlockSpec(memory_space=pltpu.VMEM)
    payload = pl.pallas_call(
        functools.partial(plane_kernel, shift_max, merged),
        out_shape=jax.ShapeDtypeStruct((trials * SUBLANES, LANES), jnp.float32),
        in_specs=[vmem] * 4,
        out_specs=vmem,
        scratch_shapes=[pltpu.VMEM((rows * blocks_of(span + 2 * HALF), LANES), jnp.float32)],
    )(filterbank, bandpass[None, :], local_delays, cross_delays)

    members = SUBLANES * spans
    groups = None
    if subs > SUBLANES:
        groups = [list(range(g, g + members)) for g in range(0, subs * spans, members)]
    exchange = functools.partial(
        lax.all_to_all,
        axis_name=("sub", "tm"),
        split_axis=0,
        concat_axis=0,
        axis_index_groups=groups,
        tiled=True,
    )
    inbox = exchange(payload.reshape(members, SUBLANES, LANES))
    norm = 1.0 / math.sqrt(rows * subs)
    per_span = span // LANES
    merged_rows = pl.pallas_call(
        functools.partial(merge_kernel, spans, span, plane_blocks, norm),
        out_shape=jax.ShapeDtypeStruct((members * per_span, LANES), jnp.float32),
        in_specs=[vmem],
        out_specs=vmem,
    )(inbox.reshape(members * SUBLANES, LANES))
    current = exchange(merged_rows.reshape(members, per_span, LANES)).reshape(trials, span)

    if cross_levels > merged:
        wide = lax.all_gather(current, "tm", axis=1, tiled=True)
        position = lax.axis_index("sub")
        for level in range(merged, cross_levels):
            partner = lax.ppermute(wide, "sub", [(i, i ^ 1 << level) for i in range(subs)])
            upper_side = position >> level & 1 == 1
            lower = jnp.where(upper_side, partner, wide)
            upper = jnp.where(upper_side, wide, partner)
            wide = lower + delayed(upper, cross_delays[level])
        current = lax.dynamic_slice_in_dim(wide, lax.axis_index("tm") * span, span, axis=1)
    return current


def solution(mesh):
    return jax.shard_map(
        shards,
        mesh=mesh,
        in_specs=(P(("beam", "sub"), "tm"), P(("beam", "sub")), P(None, "sub"), P(None, "sub")),
        out_specs=P(("beam", "sub"), "tm"),
        check_vma=False,
    )
```

```python
import functools
import math

import jax
import jax.numpy as jnp
from jax import lax
from jax.experimental import pallas as pl
from jax.experimental.pallas import tpu as pltpu
from jax.sharding import PartitionSpec as P

LANES = 128
SUBLANES = 8
WINDOW = 31
HALF = WINDOW // 2
LEAD = LANES


def iota(shape, axis):
    return lax.broadcasted_iota(jnp.int32, shape, axis)


def turned(x, index, axis):
    return jnp.take_along_axis(x, index, axis=axis, mode="promise_in_bounds")


def blocks_of(columns):
    return -(-columns // LANES)


def later(tiles, shift, count, far=False):
    source = iota(shift.shape, 1) - shift
    index = source & (LANES - 1)
    zero = jnp.zeros(shift.shape, jnp.float32)
    spun = [zero, zero] + [turned(tile, index, 1) for tile in tiles]
    spun += [zero] * (count + 2 - len(spun))
    got = []
    for b in range(count):
        prior = jnp.where(source >= -LANES, spun[b + 1], spun[b]) if far else spun[b + 1]
        got.append(jnp.where(source >= 0, spun[b + 2], prior))
    return got


def folded(tiles):
    row = iota(tiles[0].shape, 0)
    reach = SUBLANES // 2
    while reach:
        first = row & reach == 0
        tiles = [
            jnp.where(
                first,
                a + pltpu.roll(a, SUBLANES - reach, 0),
                b + pltpu.roll(b, reach, 0),
            )
            for a, b in zip(tiles[:reach], tiles[reach:])
        ]
        reach //= 2
    return tiles[0]


def plane_kernel(shift_max, fb_ref, bp_ref, ld_ref, cd_ref, plane_ref, edge_ref, level_ref):
    rows, span = fb_ref.shape
    local_levels = ld_ref.shape[0]
    trials = cd_ref.shape[1]
    grow = trials.bit_length() - 1
    square = (rows, LANES)
    lane, row = iota(square, 1), iota(square, 0)
    inner, outer = row & (SUBLANES - 1), row >> 3

    pick = lane == inner * trials + outer
    parts = [jnp.where(pick, ld_ref[m : m + 1, :], 0).astype(jnp.bfloat16) for m in range(grow)]
    tail = jnp.zeros(square, jnp.int32)
    for m in range(grow, local_levels):
        bit = m - grow
        use = (lane == (inner >> (bit + 1)) * trials + outer) & (inner >> bit & 1 == 1)
        tail = tail + jnp.where(use, ld_ref[m : m + 1, :], 0)
    parts.append(tail.astype(jnp.float32).astype(jnp.bfloat16))
    rest = bp_ref[...]
    for _ in range(3):
        part = rest.astype(jnp.bfloat16)
        rest = rest - part.astype(jnp.float32)
        parts.append(jnp.where(pick, part.astype(jnp.float32), 0.0).astype(jnp.bfloat16))
    ones = jnp.ones((rows, LANES), jnp.bfloat16)
    spread = jnp.dot(jnp.concatenate(parts, axis=0), ones, preferred_element_type=jnp.float32)
    delays = spread[: (grow + 1) * rows].astype(jnp.int32)
    gain = spread[(grow + 1) * rows :]
    gain = (gain[:rows] + gain[rows : 2 * rows] + gain[2 * rows :]) * (1.0 / WINDOW)

    at = iota((2 * LANES, LANES), 0) - LANES
    to = iota((2 * LANES, LANES), 1) - HALF
    band = jnp.where(at == to, float(WINDOW), 0.0) - jnp.where(jnp.abs(at - to) <= HALF, 1.0, 0.0)
    band = band.astype(jnp.bfloat16)
    whole = span // LANES
    start_blocks = blocks_of(span + 2 * HALF)
    for block in range(start_blocks):
        low, high = max(block - 1, 0), min(block + 1, whole)
        part = band[(low - block + 1) * LANES : (high - block + 1) * LANES]
        level_ref[block * rows : (block + 1) * rows, :] = jnp.dot(
            fb_ref[:, low * LANES : high * LANES], part, preferred_element_type=jnp.float32
        )

    first_span = lax.axis_index("tm") == 0
    early = jnp.logical_and(iota((SUBLANES, LANES), 1) < HALF, first_span)
    bands = []
    for e in range(trials):
        scale = gain[e * SUBLANES : (e + 1) * SUBLANES]
        tiles = []
        for block in range(start_blocks):
            tile = level_ref[pl.ds(block * rows + e, SUBLANES, stride=trials), :] * scale
            tiles.append(jnp.where(early, 0.0, tile) if block == 0 else tile)
        bands.append(tiles)
    plane = [bands]
    for m in range(grow):
        count = blocks_of(span + 2 * HALF + (m + 1) * shift_max)
        old, plane = plane, []
        for c in range(2):
            for i, held in enumerate(old):
                j = c * len(old) + i
                new = []
                for e in range(len(held) // 2):
                    at_row = m * rows + (e * 2 * len(old) + j) * SUBLANES
                    moved = later(held[2 * e + 1], delays[at_row : at_row + SUBLANES], count)
                    base = held[2 * e]
                    new.append([base[b] + moved[b] if b < len(base) else moved[b] for b in range(count)])
                plane.append(new)
    count = blocks_of(span + LEAD + HALF + local_levels * shift_max)
    zero = jnp.zeros((SUBLANES, LANES), jnp.float32)
    for j in range(trials):
        at_row = grow * rows + j * SUBLANES
        shift = delays[at_row : at_row + SUBLANES] + (LEAD - HALF)
        moved = later(plane[j][0], shift, count, far=True)
        level_ref[pl.ds(j, SUBLANES, stride=trials), :] = folded(moved + [zero] * (SUBLANES - count))
    own = plane_ref.shape[0] // trials
    plane_ref[...] = level_ref[: own * trials, :]
    past = span // LANES
    width = edge_ref.shape[0] // trials
    edge_ref[...] = jnp.where(
        first_span,
        level_ref[past * trials : (past + width) * trials, :],
        level_ref[: width * trials, :],
    )


def joined(plane_ref, edge_ref, span, trials, block):
    past = span // LANES
    here = plane_ref[block * trials : (block + 1) * trials, :]
    width = edge_ref.shape[0] // trials
    first_span = lax.axis_index("tm") == 0
    if block < width:
        there = edge_ref[block * trials : (block + 1) * trials, :]
        here = here + jnp.where(first_span, 0.0, there)
    if block == past:
        here = here + jnp.where(first_span, edge_ref[:trials, :], 0.0)
    return here


def delayed(upper, delays):
    columns = lax.broadcasted_iota(jnp.int32, upper.shape, 1) - delays[:, None]
    moved = jnp.take_along_axis(upper, jnp.maximum(columns, 0), axis=1)
    return jnp.where(columns >= 0, moved, 0.0)


def noted_kernel(span, levels, plane_ref, edge_ref, cd_ref, out_ref):
    trials = cd_ref.shape[1]
    blocks = plane_ref.shape[0] // trials
    for block in range(blocks):
        out_ref[block * trials : (block + 1) * trials, :] = joined(plane_ref, edge_ref, span, trials, block)
    eye = iota((trials, trials), 0) == iota((trials, trials), 1)
    lane = iota((trials, LANES), 1)
    note = jnp.zeros((trials, LANES), jnp.float32)
    for l in range(levels):
        own = jnp.where(eye, cd_ref[l : l + 1, :].astype(jnp.float32), 0.0)
        note = jnp.where(lane == l, jnp.sum(own, axis=1, keepdims=True), note)
    out_ref[blocks * trials :, :] = note


def merge_kernel(levels, trials, scale, in_ref, out_ref):
    devices = 1 << levels
    stride = in_ref.shape[0] // devices
    blocks = stride // trials - 1
    place = lax.axis_index("sub") & (devices - 1)
    for half in range(trials // SUBLANES):
        base = half * SUBLANES
        total = None
        for q in range(devices):
            shift = jnp.zeros((SUBLANES, LANES), jnp.int32)
            for l in range(levels):
                if q >> l & 1:
                    source = (q >> (l + 1) << (l + 1)) | (place & ((1 << (l + 1)) - 1))
                    at_row = pl.multiple_of(source * stride + blocks * trials + base, SUBLANES)
                    note = in_ref[pl.ds(at_row, SUBLANES), :]
                    shift = shift + turned(note, jnp.full(note.shape, l, jnp.int32), 1).astype(jnp.int32)
            tiles = [
                in_ref[q * stride + b * trials + base : q * stride + b * trials + base + SUBLANES, :]
                for b in range(blocks)
            ]
            moved = later(tiles, shift, blocks)[1:] if q else tiles[1:]
            total = moved if total is None else [a + b for a, b in zip(total, moved)]
        for b, tile in enumerate(total):
            out_ref[base : base + SUBLANES, b * LANES : (b + 1) * LANES] = tile * scale


def shards(filterbank, bandpass, local_delays, cross_delays):
    rows, span = filterbank.shape
    trials = cross_delays.shape[1]
    subs, spans = lax.axis_size("sub"), lax.axis_size("tm")
    cross_levels = subs.bit_length() - 1
    local_levels = local_delays.shape[0]
    shift_max = span // 16
    merged = min(cross_levels, (LANES - 1) // shift_max)
    own = (LEAD + span) // LANES
    width = blocks_of(LEAD + HALF + local_levels * shift_max)
    assert rows == LANES == trials * SUBLANES and spans == 2

    vmem = pl.BlockSpec(memory_space=pltpu.VMEM)
    tiled = lambda count: jax.ShapeDtypeStruct((count * trials, LANES), jnp.float32)
    start_rows = rows * blocks_of(span + 2 * HALF)
    plane, edge = pl.pallas_call(
        functools.partial(plane_kernel, shift_max),
        out_shape=(tiled(own), tiled(width)),
        in_specs=[vmem] * 4,
        out_specs=(vmem, vmem),
        scratch_shapes=[pltpu.VMEM((start_rows, LANES), jnp.float32)],
    )(filterbank, bandpass[None, :], local_delays, cross_delays)
    edge = lax.ppermute(edge, "tm", [(0, 1), (1, 0)])
    noted = pl.pallas_call(
        functools.partial(noted_kernel, span, merged),
        out_shape=tiled(own + 1),
        in_specs=[vmem] * 3,
        out_specs=vmem,
    )(plane, edge, cross_delays)

    members = 1 << merged
    groups = None
    if subs > members:
        groups = [list(range(g, g + members)) for g in range(0, subs, members)]
    planes = lax.all_gather(noted, "sub", axis=0, tiled=True, axis_index_groups=groups)
    current = pl.pallas_call(
        functools.partial(merge_kernel, merged, trials, 1.0 / math.sqrt(rows * subs)),
        out_shape=jax.ShapeDtypeStruct((trials, span), jnp.float32),
        in_specs=[vmem],
        out_specs=vmem,
    )(planes)

    if cross_levels > merged:
        wide = lax.all_gather(current, "tm", axis=1, tiled=True)
        position = lax.axis_index("sub")
        for level in range(merged, cross_levels):
            partner = lax.ppermute(wide, "sub", [(i, i ^ 1 << level) for i in range(subs)])
            upper_side = position >> level & 1 == 1
            lower = jnp.where(upper_side, partner, wide)
            upper = jnp.where(upper_side, wide, partner)
            wide = lower + delayed(upper, cross_delays[level])
        current = lax.dynamic_slice_in_dim(wide, lax.axis_index("tm") * span, span, axis=1)
    return current


def solution(mesh):
    return jax.shard_map(
        shards,
        mesh=mesh,
        in_specs=(P(("beam", "sub"), "tm"), P(("beam", "sub")), P(None, "sub"), P(None, "sub")),
        out_specs=P(("beam", "sub"), "tm"),
        check_vma=False,
    )
```

```python
import functools
import math

import jax
import jax.numpy as jnp
from jax import lax
from jax.experimental import pallas as pl
from jax.experimental.pallas import tpu as pltpu
from jax.sharding import PartitionSpec as P

LANES = 128
SUBLANES = 8
WINDOW = 31
HALF = WINDOW // 2


def iota(shape, axis):
    return lax.broadcasted_iota(jnp.int32, shape, axis)


def turned(x, index, axis):
    return jnp.take_along_axis(x, index, axis=axis, mode="promise_in_bounds")


def blocks_of(columns):
    return -(-columns // LANES)


def later(tiles, shift, count, far=False):
    source = iota(shift.shape, 1) - shift
    index = source & (LANES - 1)
    zero = jnp.zeros(shift.shape, jnp.float32)
    spun = [zero, zero] + [turned(tile, index, 1) for tile in tiles]
    spun += [zero] * (count + 2 - len(spun))
    got = []
    for b in range(count):
        prior = jnp.where(source >= -LANES, spun[b + 1], spun[b]) if far else spun[b + 1]
        got.append(jnp.where(source >= 0, spun[b + 2], prior))
    return got


def folded(tiles):
    row = iota(tiles[0].shape, 0)
    reach = SUBLANES // 2
    while reach:
        first = row & reach == 0
        tiles = [
            jnp.where(
                first,
                a + pltpu.roll(a, SUBLANES - reach, 0),
                b + pltpu.roll(b, reach, 0),
            )
            for a, b in zip(tiles[:reach], tiles[reach:])
        ]
        reach //= 2
    return tiles[0]


def plane_kernel(shift_max, lead, fb_ref, bp_ref, ld_ref, cd_ref, plane_ref, edge_ref, steps_ref, level_ref):
    rows, span = fb_ref.shape
    local_levels = ld_ref.shape[0]
    trials = cd_ref.shape[1]
    grow = trials.bit_length() - 1
    square = (rows, LANES)
    lane, row = iota(square, 1), iota(square, 0)
    inner, outer = row & (SUBLANES - 1), row >> 3

    pick = lane == inner * trials + outer
    parts = [jnp.where(pick, ld_ref[m : m + 1, :], 0).astype(jnp.bfloat16) for m in range(grow)]
    tail = jnp.zeros(square, jnp.int32)
    for m in range(grow, local_levels):
        bit = m - grow
        use = (lane == (inner >> (bit + 1)) * trials + outer) & (inner >> bit & 1 == 1)
        tail = tail + jnp.where(use, ld_ref[m : m + 1, :], 0)
    parts.append(tail.astype(jnp.float32).astype(jnp.bfloat16))
    rest = bp_ref[...]
    for _ in range(3):
        part = rest.astype(jnp.bfloat16)
        rest = rest - part.astype(jnp.float32)
        parts.append(jnp.where(pick, part.astype(jnp.float32), 0.0).astype(jnp.bfloat16))
    ones = jnp.ones((rows, LANES), jnp.bfloat16)
    spread = jnp.dot(jnp.concatenate(parts, axis=0), ones, preferred_element_type=jnp.float32)
    delays = spread[: (grow + 1) * rows].astype(jnp.int32)
    gain = spread[(grow + 1) * rows :]
    gain = (gain[:rows] + gain[rows : 2 * rows] + gain[2 * rows :]) * (1.0 / WINDOW)

    at = iota((2 * LANES, LANES), 0) - LANES
    to = iota((2 * LANES, LANES), 1) - HALF
    band = jnp.where(at == to, float(WINDOW), 0.0) - jnp.where(jnp.abs(at - to) <= HALF, 1.0, 0.0)
    band = band.astype(jnp.bfloat16)
    whole = span // LANES
    start_blocks = blocks_of(span + 2 * HALF)
    for block in range(start_blocks):
        low, high = max(block - 1, 0), min(block + 1, whole)
        part = band[(low - block + 1) * LANES : (high - block + 1) * LANES]
        level_ref[block * rows : (block + 1) * rows, :] = jnp.dot(
            fb_ref[:, low * LANES : high * LANES], part, preferred_element_type=jnp.float32
        )

    first_span = lax.axis_index("tm") == 0
    early = jnp.logical_and(iota((SUBLANES, LANES), 1) < HALF, first_span)
    bands = []
    for e in range(trials):
        scale = gain[e * SUBLANES : (e + 1) * SUBLANES]
        tiles = []
        for block in range(start_blocks):
            tile = level_ref[pl.ds(block * rows + e, SUBLANES, stride=trials), :] * scale
            tiles.append(jnp.where(early, 0.0, tile) if block == 0 else tile)
        bands.append(tiles)
    plane = [bands]
    for m in range(grow):
        count = blocks_of(span + 2 * HALF + (m + 1) * shift_max)
        old, plane = plane, []
        for c in range(2):
            for i, held in enumerate(old):
                j = c * len(old) + i
                new = []
                for e in range(len(held) // 2):
                    at_row = m * rows + (e * 2 * len(old) + j) * SUBLANES
                    moved = later(held[2 * e + 1], delays[at_row : at_row + SUBLANES], count)
                    base = held[2 * e]
                    new.append([base[b] + moved[b] if b < len(base) else moved[b] for b in range(count)])
                plane.append(new)
    count = blocks_of(span + HALF + local_levels * shift_max) + lead
    zero = jnp.zeros((SUBLANES, LANES), jnp.float32)
    for j in range(trials):
        at_row = grow * rows + j * SUBLANES
        shift = delays[at_row : at_row + SUBLANES] + (LANES - HALF)
        moved = later([zero] * (lead - 1) + plane[j][0], shift, count, far=True)
        level_ref[pl.ds(j, SUBLANES, stride=trials), :] = folded(moved + [zero] * (SUBLANES - count))
    eye = iota((trials, trials), 0) == iota((trials, trials), 1)
    for l in range(cd_ref.shape[0]):
        step = jnp.sum(jnp.where(eye, cd_ref[l : l + 1, :].astype(jnp.float32), 0.0), axis=1, keepdims=True)
        steps_ref[l * trials : (l + 1) * trials, :] = jnp.broadcast_to(step, (trials, LANES)).astype(jnp.int32)
    own = plane_ref.shape[0] // trials
    plane_ref[...] = level_ref[: own * trials, :]
    past = span // LANES
    width = edge_ref.shape[0] // trials
    edge_ref[...] = jnp.where(
        first_span,
        level_ref[past * trials : (past + width) * trials, :],
        level_ref[: width * trials, :],
    )


def join_kernel(past, lead, trials, plane_ref, edge_ref, out_ref):
    first_span = lax.axis_index("tm") == 0
    for block in range(plane_ref.shape[0] // trials):
        rows = slice(block * trials, (block + 1) * trials)
        here = plane_ref[rows, :]
        if rows.stop <= edge_ref.shape[0]:
            here = here + jnp.where(first_span, 0.0, edge_ref[rows, :])
        if block == past + lead - 1:
            there = edge_ref[(lead - 1) * trials : lead * trials, :]
            here = here + jnp.where(first_span, there, 0.0)
        out_ref[rows, :] = here


def merge_kernel(level, trials, own_ref, there_ref, steps_ref, out_ref, lead=0, scale=None):
    is_upper = lax.axis_index("sub") >> level & 1 == 1
    blocks = own_ref.shape[0] // trials
    shift = steps_ref[level * trials : (level + 1) * trials, :]
    lower, upper = [], []
    for block in range(blocks):
        rows = slice(block * trials, (block + 1) * trials)
        own, there = own_ref[rows, :], there_ref[rows, :]
        lower.append(jnp.where(is_upper, there, own))
        upper.append(jnp.where(is_upper, own, there))
    moved = later(upper, shift, blocks)
    for block in range(lead, blocks):
        new = lower[block] + moved[block]
        if scale is None:
            out_ref[block * trials : (block + 1) * trials, :] = new
        else:
            out_ref[:, (block - lead) * LANES : (block - lead + 1) * LANES] = new * scale


def shards(filterbank, bandpass, local_delays, cross_delays):
    rows, span = filterbank.shape
    cross_levels, trials = cross_delays.shape
    subs = lax.axis_size("sub")
    local_levels = local_delays.shape[0]
    shift_max = span // 16
    lead = blocks_of(cross_levels * shift_max)
    past = span // LANES
    width = blocks_of(lead * LANES + HALF + local_levels * shift_max)
    assert rows == LANES == trials * SUBLANES and lax.axis_size("tm") == 2

    vmem = pl.BlockSpec(memory_space=pltpu.VMEM)
    tiled = lambda count: jax.ShapeDtypeStruct((count * trials, LANES), jnp.float32)
    start_rows = rows * blocks_of(span + 2 * HALF)
    plane, edge, steps = pl.pallas_call(
        functools.partial(plane_kernel, shift_max, lead),
        out_shape=(
            tiled(lead + past),
            tiled(width),
            jax.ShapeDtypeStruct((cross_levels * trials, LANES), jnp.int32),
        ),
        in_specs=[vmem] * 4,
        out_specs=(vmem,) * 3,
        scratch_shapes=[pltpu.VMEM((start_rows, LANES), jnp.float32)],
    )(filterbank, bandpass[None, :], local_delays, cross_delays)
    edge = lax.ppermute(edge, "tm", [(0, 1), (1, 0)])
    plane = pl.pallas_call(
        functools.partial(join_kernel, past, lead, trials),
        out_shape=tiled(lead + past),
        in_specs=[vmem] * 2,
        out_specs=vmem,
    )(plane, edge)
    for level in range(cross_levels):
        there = lax.ppermute(plane, "sub", [(i, i ^ 1 << level) for i in range(subs)])
        body = functools.partial(merge_kernel, level, trials)
        shape = tiled(lead + past)
        if level == cross_levels - 1:
            body = functools.partial(body, lead=lead, scale=1.0 / math.sqrt(rows * subs))
            shape = jax.ShapeDtypeStruct((trials, span), jnp.float32)
        plane = pl.pallas_call(body, out_shape=shape, in_specs=[vmem] * 3, out_specs=vmem)(
            plane, there, steps
        )
    return plane


def solution(mesh):
    return jax.shard_map(
        shards,
        mesh=mesh,
        in_specs=(P(("beam", "sub"), "tm"), P(("beam", "sub")), P(None, "sub"), P(None, "sub")),
        out_specs=P(("beam", "sub"), "tm"),
        check_vma=False,
    )
```

```python
import functools
import math

import jax
import jax.numpy as jnp
from jax import lax
from jax.experimental import pallas as pl
from jax.experimental.pallas import tpu as pltpu
from jax.sharding import PartitionSpec as P

LANES = 128
SUBLANES = 8
WINDOW = 31
HALF = WINDOW // 2


def iota(shape, axis):
    return lax.broadcasted_iota(jnp.int32, shape, axis)


def turned(x, index, axis):
    return jnp.take_along_axis(x, index, axis=axis, mode="promise_in_bounds")


def blocks_of(columns):
    return -(-columns // LANES)


def later(tiles, shift, count, far=False):
    source = iota(shift.shape, 1) - shift
    index = source & (LANES - 1)
    zero = jnp.zeros(shift.shape, jnp.float32)
    spun = [zero, zero] + [turned(tile, index, 1) for tile in tiles]
    spun += [zero] * (count + 2 - len(spun))
    got = []
    for b in range(count):
        prior = jnp.where(source >= -LANES, spun[b + 1], spun[b]) if far else spun[b + 1]
        got.append(jnp.where(source >= 0, spun[b + 2], prior))
    return got


def folded(tiles):
    row = iota(tiles[0].shape, 0)
    reach = SUBLANES // 2
    while reach:
        first = row & reach == 0
        tiles = [
            jnp.where(
                first,
                a + pltpu.roll(a, SUBLANES - reach, 0),
                b + pltpu.roll(b, reach, 0),
            )
            for a, b in zip(tiles[:reach], tiles[reach:])
        ]
        reach //= 2
    return tiles[0]


def plane_kernel(shift_max, lead, fb_ref, bp_ref, ld_ref, cd_ref, plane_ref, edge_ref, steps_ref, level_ref):
    rows, span = fb_ref.shape
    local_levels = ld_ref.shape[0]
    trials = cd_ref.shape[1]
    grow = trials.bit_length() - 1
    square = (rows, LANES)
    lane, row = iota(square, 1), iota(square, 0)
    inner, outer = row & (SUBLANES - 1), row >> 3

    pick = lane == inner * trials + outer
    parts = [jnp.where(pick, ld_ref[m : m + 1, :], 0).astype(jnp.bfloat16) for m in range(grow)]
    tail = jnp.zeros(square, jnp.int32)
    for m in range(grow, local_levels):
        bit = m - grow
        use = (lane == (inner >> (bit + 1)) * trials + outer) & (inner >> bit & 1 == 1)
        tail = tail + jnp.where(use, ld_ref[m : m + 1, :], 0)
    parts.append(tail.astype(jnp.float32).astype(jnp.bfloat16))
    rest = bp_ref[...]
    for _ in range(3):
        part = rest.astype(jnp.bfloat16)
        rest = rest - part.astype(jnp.float32)
        parts.append(jnp.where(pick, part.astype(jnp.float32), 0.0).astype(jnp.bfloat16))
    ones = jnp.ones((rows, LANES), jnp.bfloat16)
    spread = jnp.dot(jnp.concatenate(parts, axis=0), ones, preferred_element_type=jnp.float32)
    delays = spread[: (grow + 1) * rows].astype(jnp.int32)
    gain = spread[(grow + 1) * rows :]
    gain = (gain[:rows] + gain[rows : 2 * rows] + gain[2 * rows :]) * (1.0 / WINDOW)

    at = iota((2 * LANES, LANES), 0) - LANES
    to = iota((2 * LANES, LANES), 1) - HALF
    band = jnp.where(at == to, float(WINDOW), 0.0) - jnp.where(jnp.abs(at - to) <= HALF, 1.0, 0.0)
    band = band.astype(jnp.bfloat16)
    whole = span // LANES
    start_blocks = blocks_of(span + 2 * HALF)
    for block in range(start_blocks):
        low, high = max(block - 1, 0), min(block + 1, whole)
        part = band[(low - block + 1) * LANES : (high - block + 1) * LANES]
        level_ref[block * rows : (block + 1) * rows, :] = jnp.dot(
            fb_ref[:, low * LANES : high * LANES], part, preferred_element_type=jnp.float32
        )

    first_span = lax.axis_index("tm") == 0
    early = jnp.logical_and(iota((SUBLANES, LANES), 1) < HALF, first_span)
    bands = []
    for e in range(trials):
        scale = gain[e * SUBLANES : (e + 1) * SUBLANES]
        tiles = []
        for block in range(start_blocks):
            tile = level_ref[pl.ds(block * rows + e, SUBLANES, stride=trials), :] * scale
            tiles.append(jnp.where(early, 0.0, tile) if block == 0 else tile)
        bands.append(tiles)
    plane = [bands]
    for m in range(grow):
        count = blocks_of(span + 2 * HALF + (m + 1) * shift_max)
        old, plane = plane, []
        for c in range(2):
            for i, held in enumerate(old):
                j = c * len(old) + i
                new = []
                for e in range(len(held) // 2):
                    at_row = m * rows + (e * 2 * len(old) + j) * SUBLANES
                    moved = later(held[2 * e + 1], delays[at_row : at_row + SUBLANES], count)
                    base = held[2 * e]
                    new.append([base[b] + moved[b] if b < len(base) else moved[b] for b in range(count)])
                plane.append(new)
    count = blocks_of(span + HALF + local_levels * shift_max) + lead
    zero = jnp.zeros((SUBLANES, LANES), jnp.float32)
    for j in range(trials):
        at_row = grow * rows + j * SUBLANES
        shift = delays[at_row : at_row + SUBLANES] + (LANES - HALF)
        moved = later([zero] * (lead - 1) + plane[j][0], shift, count, far=True)
        level_ref[pl.ds(j, SUBLANES, stride=trials), :] = folded(moved + [zero] * (SUBLANES - count))
    eye = iota((trials, trials), 0) == iota((trials, trials), 1)
    for l in range(cd_ref.shape[0]):
        step = jnp.sum(jnp.where(eye, cd_ref[l : l + 1, :].astype(jnp.float32), 0.0), axis=1, keepdims=True)
        steps_ref[l * trials : (l + 1) * trials, :] = jnp.broadcast_to(step, (trials, LANES)).astype(jnp.int32)
    own = plane_ref.shape[0] // trials
    plane_ref[...] = level_ref[: own * trials, :]
    past = span // LANES
    width = edge_ref.shape[0] // trials
    edge_ref[...] = jnp.where(
        first_span,
        level_ref[past * trials : (past + width) * trials, :],
        level_ref[: width * trials, :],
    )


def join_kernel(past, lead, trials, plane_ref, edge_ref, out_ref):
    first_span = lax.axis_index("tm") == 0
    for block in range(plane_ref.shape[0] // trials):
        rows = slice(block * trials, (block + 1) * trials)
        here = plane_ref[rows, :]
        if rows.stop <= edge_ref.shape[0]:
            here = here + jnp.where(first_span, 0.0, edge_ref[rows, :])
        if block == past + lead - 1:
            there = edge_ref[(lead - 1) * trials : lead * trials, :]
            here = here + jnp.where(first_span, there, 0.0)
        out_ref[rows, :] = here


def merge_kernel(level, trials, own_ref, there_ref, steps_ref, out_ref, lead=0, scale=None):
    is_upper = lax.axis_index("sub") >> level & 1 == 1
    blocks = own_ref.shape[0] // trials
    shift = steps_ref[level * trials : (level + 1) * trials, :]
    lower, upper = [], []
    for block in range(blocks):
        rows = slice(block * trials, (block + 1) * trials)
        own, there = own_ref[rows, :], there_ref[rows, :]
        lower.append(jnp.where(is_upper, there, own))
        upper.append(jnp.where(is_upper, own, there))
    moved = later(upper, shift, blocks)
    for block in range(lead, blocks):
        new = lower[block] + moved[block]
        if scale is None:
            out_ref[block * trials : (block + 1) * trials, :] = new
        else:
            out_ref[:, (block - lead) * LANES : (block - lead + 1) * LANES] = new * scale


def shards(filterbank, bandpass, local_delays, cross_delays):
    rows, span = filterbank.shape
    cross_levels, trials = cross_delays.shape
    subs = lax.axis_size("sub")
    local_levels = local_delays.shape[0]
    shift_max = span // 16
    lead = blocks_of(cross_levels * shift_max)
    past = span // LANES
    width = blocks_of(lead * LANES + HALF + local_levels * shift_max)
    assert rows == LANES == trials * SUBLANES and lax.axis_size("tm") == 2

    vmem = pl.BlockSpec(memory_space=pltpu.VMEM)
    tiled = lambda count: jax.ShapeDtypeStruct((count * trials, LANES), jnp.float32)
    start_rows = rows * blocks_of(span + 2 * HALF)
    plane, edge, steps = pl.pallas_call(
        functools.partial(plane_kernel, shift_max, lead),
        out_shape=(
            tiled(lead + past),
            tiled(width),
            jax.ShapeDtypeStruct((cross_levels * trials, LANES), jnp.int32),
        ),
        in_specs=[vmem] * 4,
        out_specs=(vmem,) * 3,
        scratch_shapes=[pltpu.VMEM((start_rows, LANES), jnp.float32)],
        compiler_params=pltpu.CompilerParams(vmem_limit_bytes=4 << 20),
    )(filterbank, bandpass[None, :], local_delays, cross_delays)
    edge = lax.ppermute(edge, "tm", [(0, 1), (1, 0)])
    plane = pl.pallas_call(
        functools.partial(join_kernel, past, lead, trials),
        out_shape=tiled(lead + past),
        in_specs=[vmem] * 2,
        out_specs=vmem,
        compiler_params=pltpu.CompilerParams(vmem_limit_bytes=1 << 20),
    )(plane, edge)
    for level in range(cross_levels):
        there = lax.ppermute(plane, "sub", [(i, i ^ 1 << level) for i in range(subs)])
        body = functools.partial(merge_kernel, level, trials)
        shape = tiled(lead + past)
        if level == cross_levels - 1:
            body = functools.partial(body, lead=lead, scale=1.0 / math.sqrt(rows * subs))
            shape = jax.ShapeDtypeStruct((trials, span), jnp.float32)
        plane = pl.pallas_call(
            body,
            out_shape=shape,
            in_specs=[vmem] * 3,
            out_specs=vmem,
            compiler_params=pltpu.CompilerParams(vmem_limit_bytes=1 << 20),
        )(plane, there, steps)
    return plane


def solution(mesh):
    return jax.shard_map(
        shards,
        mesh=mesh,
        in_specs=(P(("beam", "sub"), "tm"), P(("beam", "sub")), P(None, "sub"), P(None, "sub")),
        out_specs=P(("beam", "sub"), "tm"),
        check_vma=False,
    )
```

```python
import functools
import math

import jax
import jax.numpy as jnp
from jax import lax
from jax.experimental import pallas as pl
from jax.experimental.pallas import tpu as pltpu
from jax.sharding import PartitionSpec as P

LANES = 128
SUBLANES = 8
WINDOW = 31
HALF = WINDOW // 2


def iota(shape, axis):
    return lax.broadcasted_iota(jnp.int32, shape, axis)


def turned(x, index, axis):
    return jnp.take_along_axis(x, index, axis=axis, mode="promise_in_bounds")


def blocks_of(columns):
    return -(-columns // LANES)


def later(tiles, shift, count, far=False):
    source = iota(shift.shape, 1) - shift
    index = source & (LANES - 1)
    zero = jnp.zeros(shift.shape, jnp.float32)
    spun = [zero, zero] + [turned(tile, index, 1) for tile in tiles]
    spun += [zero] * (count + 2 - len(spun))
    got = []
    for b in range(count):
        prior = jnp.where(source >= -LANES, spun[b + 1], spun[b]) if far else spun[b + 1]
        got.append(jnp.where(source >= 0, spun[b + 2], prior))
    return got


def folded(tiles):
    row = iota(tiles[0].shape, 0)
    reach = SUBLANES // 2
    while reach:
        first = row & reach == 0
        tiles = [
            jnp.where(
                first,
                a + pltpu.roll(a, SUBLANES - reach, 0),
                b + pltpu.roll(b, reach, 0),
            )
            for a, b in zip(tiles[:reach], tiles[reach:])
        ]
        reach //= 2
    return tiles[0]


def plane_kernel(shift_max, lead, *refs):
    sources, (plane_ref, edge_ref, steps_ref, level_ref), held, sems = refs[:4], refs[4:8], refs[8:12], refs[12]
    copies = [pltpu.make_async_copy(a, b, sems.at[i]) for i, (a, b) in enumerate(zip(sources, held))]
    for copy in copies:
        copy.start()
    fb_ref, bp_ref, ld_ref, cd_ref = held
    for copy in copies[1:]:
        copy.wait()
    rows, span = fb_ref.shape
    local_levels = ld_ref.shape[0]
    trials = cd_ref.shape[1]
    grow = trials.bit_length() - 1
    square = (rows, LANES)
    lane, row = iota(square, 1), iota(square, 0)
    inner, outer = row & (SUBLANES - 1), row >> 3

    pick = lane == inner * trials + outer
    parts = [jnp.where(pick, ld_ref[m : m + 1, :], 0).astype(jnp.bfloat16) for m in range(grow)]
    tail = jnp.zeros(square, jnp.int32)
    for m in range(grow, local_levels):
        bit = m - grow
        use = (lane == (inner >> (bit + 1)) * trials + outer) & (inner >> bit & 1 == 1)
        tail = tail + jnp.where(use, ld_ref[m : m + 1, :], 0)
    parts.append(tail.astype(jnp.float32).astype(jnp.bfloat16))
    rest = bp_ref[...]
    for _ in range(3):
        part = rest.astype(jnp.bfloat16)
        rest = rest - part.astype(jnp.float32)
        parts.append(jnp.where(pick, part.astype(jnp.float32), 0.0).astype(jnp.bfloat16))
    ones = jnp.ones((rows, LANES), jnp.bfloat16)
    spread = jnp.dot(jnp.concatenate(parts, axis=0), ones, preferred_element_type=jnp.float32)
    delays = spread[: (grow + 1) * rows].astype(jnp.int32)
    gain = spread[(grow + 1) * rows :]
    gain = (gain[:rows] + gain[rows : 2 * rows] + gain[2 * rows :]) * (1.0 / WINDOW)

    at = iota((2 * LANES, LANES), 0) - LANES
    to = iota((2 * LANES, LANES), 1) - HALF
    band = jnp.where(at == to, float(WINDOW), 0.0) - jnp.where(jnp.abs(at - to) <= HALF, 1.0, 0.0)
    band = band.astype(jnp.bfloat16)
    whole = span // LANES
    start_blocks = blocks_of(span + 2 * HALF)
    copies[0].wait()
    for block in range(start_blocks):
        low, high = max(block - 1, 0), min(block + 1, whole)
        part = band[(low - block + 1) * LANES : (high - block + 1) * LANES]
        level_ref[block * rows : (block + 1) * rows, :] = jnp.dot(
            fb_ref[:, low * LANES : high * LANES], part, preferred_element_type=jnp.float32
        )

    first_span = lax.axis_index("tm") == 0
    early = jnp.logical_and(iota((SUBLANES, LANES), 1) < HALF, first_span)
    bands = []
    for e in range(trials):
        scale = gain[e * SUBLANES : (e + 1) * SUBLANES]
        tiles = []
        for block in range(start_blocks):
            tile = level_ref[pl.ds(block * rows + e, SUBLANES, stride=trials), :] * scale
            tiles.append(jnp.where(early, 0.0, tile) if block == 0 else tile)
        bands.append(tiles)
    plane = [bands]
    for m in range(grow):
        count = blocks_of(span + 2 * HALF + (m + 1) * shift_max)
        old, plane = plane, []
        for c in range(2):
            for i, held in enumerate(old):
                j = c * len(old) + i
                new = []
                for e in range(len(held) // 2):
                    at_row = m * rows + (e * 2 * len(old) + j) * SUBLANES
                    moved = later(held[2 * e + 1], delays[at_row : at_row + SUBLANES], count)
                    base = held[2 * e]
                    new.append([base[b] + moved[b] if b < len(base) else moved[b] for b in range(count)])
                plane.append(new)
    count = blocks_of(span + HALF + local_levels * shift_max) + lead
    zero = jnp.zeros((SUBLANES, LANES), jnp.float32)
    for j in range(trials):
        at_row = grow * rows + j * SUBLANES
        shift = delays[at_row : at_row + SUBLANES] + (LANES - HALF)
        moved = later([zero] * (lead - 1) + plane[j][0], shift, count, far=True)
        level_ref[pl.ds(j, SUBLANES, stride=trials), :] = folded(moved + [zero] * (SUBLANES - count))
    eye = iota((trials, trials), 0) == iota((trials, trials), 1)
    for l in range(cd_ref.shape[0]):
        step = jnp.sum(jnp.where(eye, cd_ref[l : l + 1, :].astype(jnp.float32), 0.0), axis=1, keepdims=True)
        steps_ref[l * trials : (l + 1) * trials, :] = jnp.broadcast_to(step, (trials, LANES)).astype(jnp.int32)
    own = plane_ref.shape[0] // trials
    plane_ref[...] = level_ref[: own * trials, :]
    past = span // LANES
    width = edge_ref.shape[0] // trials
    edge_ref[...] = jnp.where(
        first_span,
        level_ref[past * trials : (past + width) * trials, :],
        level_ref[: width * trials, :],
    )


def join_kernel(past, lead, trials, plane_ref, edge_ref, out_ref):
    first_span = lax.axis_index("tm") == 0
    for block in range(plane_ref.shape[0] // trials):
        rows = slice(block * trials, (block + 1) * trials)
        here = plane_ref[rows, :]
        if rows.stop <= edge_ref.shape[0]:
            here = here + jnp.where(first_span, 0.0, edge_ref[rows, :])
        if block == past + lead - 1:
            there = edge_ref[(lead - 1) * trials : lead * trials, :]
            here = here + jnp.where(first_span, there, 0.0)
        out_ref[rows, :] = here


def merge_kernel(level, trials, own_ref, there_ref, steps_ref, out_ref, lead=0, scale=None):
    is_upper = lax.axis_index("sub") >> level & 1 == 1
    blocks = own_ref.shape[0] // trials
    shift = steps_ref[level * trials : (level + 1) * trials, :]
    lower, upper = [], []
    for block in range(blocks):
        rows = slice(block * trials, (block + 1) * trials)
        own, there = own_ref[rows, :], there_ref[rows, :]
        lower.append(jnp.where(is_upper, there, own))
        upper.append(jnp.where(is_upper, own, there))
    moved = later(upper, shift, blocks)
    for block in range(lead, blocks):
        new = lower[block] + moved[block]
        if scale is None:
            out_ref[block * trials : (block + 1) * trials, :] = new
        else:
            out_ref[:, (block - lead) * LANES : (block - lead + 1) * LANES] = new * scale


def shards(filterbank, bandpass, local_delays, cross_delays):
    rows, span = filterbank.shape
    cross_levels, trials = cross_delays.shape
    subs = lax.axis_size("sub")
    local_levels = local_delays.shape[0]
    shift_max = span // 16
    lead = blocks_of(cross_levels * shift_max)
    past = span // LANES
    width = blocks_of(lead * LANES + HALF + local_levels * shift_max)
    assert rows == LANES == trials * SUBLANES and lax.axis_size("tm") == 2

    vmem = pl.BlockSpec(memory_space=pltpu.VMEM)
    tiled = lambda count: jax.ShapeDtypeStruct((count * trials, LANES), jnp.float32)
    start_rows = rows * blocks_of(span + 2 * HALF)
    args = (filterbank, bandpass[None, :], local_delays, cross_delays)
    plane, edge, steps = pl.pallas_call(
        functools.partial(plane_kernel, shift_max, lead),
        out_shape=(
            tiled(lead + past),
            tiled(width),
            jax.ShapeDtypeStruct((cross_levels * trials, LANES), jnp.int32),
        ),
        in_specs=[pl.BlockSpec(memory_space=pltpu.HBM)] * len(args),
        out_specs=(vmem,) * 3,
        scratch_shapes=[pltpu.VMEM((start_rows, LANES), jnp.float32)]
        + [pltpu.VMEM(a.shape, a.dtype) for a in args]
        + [pltpu.SemaphoreType.DMA((len(args),))],
        compiler_params=pltpu.CompilerParams(vmem_limit_bytes=4 << 20),
    )(*[pltpu.with_memory_space_constraint(a, pltpu.HBM) for a in args])
    edge = lax.ppermute(edge, "tm", [(0, 1), (1, 0)])
    plane = pl.pallas_call(
        functools.partial(join_kernel, past, lead, trials),
        out_shape=tiled(lead + past),
        in_specs=[vmem] * 2,
        out_specs=vmem,
        compiler_params=pltpu.CompilerParams(vmem_limit_bytes=1 << 20),
    )(plane, edge)
    for level in range(cross_levels):
        there = lax.ppermute(plane, "sub", [(i, i ^ 1 << level) for i in range(subs)])
        body = functools.partial(merge_kernel, level, trials)
        shape = tiled(lead + past)
        if level == cross_levels - 1:
            body = functools.partial(body, lead=lead, scale=1.0 / math.sqrt(rows * subs))
            shape = jax.ShapeDtypeStruct((trials, span), jnp.float32)
        plane = pl.pallas_call(
            body,
            out_shape=shape,
            in_specs=[vmem] * 3,
            out_specs=vmem,
            compiler_params=pltpu.CompilerParams(vmem_limit_bytes=1 << 20),
        )(plane, there, steps)
    return plane


def solution(mesh):
    return jax.shard_map(
        shards,
        mesh=mesh,
        in_specs=(P(("beam", "sub"), "tm"), P(("beam", "sub")), P(None, "sub"), P(None, "sub")),
        out_specs=P(("beam", "sub"), "tm"),
        check_vma=False,
    )
```

```python
import functools
import math

import jax
import jax.numpy as jnp
from jax import lax
from jax.experimental import pallas as pl
from jax.experimental.pallas import tpu as pltpu
from jax.sharding import PartitionSpec as P

LANES = 128
SUBLANES = 8
WINDOW = 31
HALF = WINDOW // 2


def iota(shape, axis):
    return lax.broadcasted_iota(jnp.int32, shape, axis)


def turned(x, index, axis):
    return jnp.take_along_axis(x, index, axis=axis, mode="promise_in_bounds")


def blocks_of(columns):
    return -(-columns // LANES)


def later(tiles, shift, count, far=False):
    source = iota(shift.shape, 1) - shift
    index = source & (LANES - 1)
    zero = jnp.zeros(shift.shape, jnp.float32)
    spun = [zero, zero] + [turned(tile, index, 1) for tile in tiles]
    spun += [zero] * (count + 2 - len(spun))
    got = []
    for b in range(count):
        prior = jnp.where(source >= -LANES, spun[b + 1], spun[b]) if far else spun[b + 1]
        got.append(jnp.where(source >= 0, spun[b + 2], prior))
    return got


def folded(tiles):
    row = iota(tiles[0].shape, 0)
    reach = SUBLANES // 2
    while reach:
        first = row & reach == 0
        tiles = [
            jnp.where(
                first,
                a + pltpu.roll(a, SUBLANES - reach, 0),
                b + pltpu.roll(b, reach, 0),
            )
            for a, b in zip(tiles[:reach], tiles[reach:])
        ]
        reach //= 2
    return tiles[0]


def plane_kernel(shift_max, *refs):
    sources, (head_ref, body_ref, steps_ref, level_ref), held, sems = refs[:4], refs[4:8], refs[8:12], refs[12]
    copies = [pltpu.make_async_copy(a, b, sems.at[i]) for i, (a, b) in enumerate(zip(sources, held))]
    for copy in copies:
        copy.start()
    fb_ref, bp_ref, ld_ref, cd_ref = held
    for copy in copies[1:]:
        copy.wait()
    rows, span = fb_ref.shape
    local_levels = ld_ref.shape[0]
    trials = cd_ref.shape[1]
    grow = trials.bit_length() - 1
    square = (rows, LANES)
    lane, row = iota(square, 1), iota(square, 0)
    inner, outer = row & (SUBLANES - 1), row >> 3

    pick = lane == inner * trials + outer
    parts = [jnp.where(pick, ld_ref[m : m + 1, :], 0).astype(jnp.bfloat16) for m in range(grow)]
    tail = jnp.zeros(square, jnp.int32)
    for m in range(grow, local_levels):
        bit = m - grow
        use = (lane == (inner >> (bit + 1)) * trials + outer) & (inner >> bit & 1 == 1)
        tail = tail + jnp.where(use, ld_ref[m : m + 1, :], 0)
    parts.append(tail.astype(jnp.float32).astype(jnp.bfloat16))
    rest = bp_ref[...]
    for _ in range(3):
        part = rest.astype(jnp.bfloat16)
        rest = rest - part.astype(jnp.float32)
        parts.append(jnp.where(pick, part.astype(jnp.float32), 0.0).astype(jnp.bfloat16))
    ones = jnp.ones((rows, LANES), jnp.bfloat16)
    spread = jnp.dot(jnp.concatenate(parts, axis=0), ones, preferred_element_type=jnp.float32)
    delays = spread[: (grow + 1) * rows].astype(jnp.int32)
    gain = spread[(grow + 1) * rows :]
    gain = (gain[:rows] + gain[rows : 2 * rows] + gain[2 * rows :]) * (1.0 / WINDOW)

    at = iota((2 * LANES, LANES), 0) - LANES
    to = iota((2 * LANES, LANES), 1) - HALF
    band = jnp.where(at == to, float(WINDOW), 0.0) - jnp.where(jnp.abs(at - to) <= HALF, 1.0, 0.0)
    band = band.astype(jnp.bfloat16)
    whole = span // LANES
    start_blocks = blocks_of(span + 2 * HALF)
    copies[0].wait()
    for block in range(start_blocks):
        low, high = max(block - 1, 0), min(block + 1, whole)
        part = band[(low - block + 1) * LANES : (high - block + 1) * LANES]
        level_ref[block * rows : (block + 1) * rows, :] = jnp.dot(
            fb_ref[:, low * LANES : high * LANES], part, preferred_element_type=jnp.float32
        )

    first_span = lax.axis_index("tm") == 0
    early = jnp.logical_and(iota((SUBLANES, LANES), 1) < HALF, first_span)
    bands = []
    for e in range(trials):
        scale = gain[e * SUBLANES : (e + 1) * SUBLANES]
        tiles = []
        for block in range(start_blocks):
            tile = level_ref[pl.ds(block * rows + e, SUBLANES, stride=trials), :] * scale
            tiles.append(jnp.where(early, 0.0, tile) if block == 0 else tile)
        bands.append(tiles)
    plane = [bands]
    for m in range(grow):
        count = blocks_of(span + 2 * HALF + (m + 1) * shift_max)
        old, plane = plane, []
        for c in range(2):
            for i, held in enumerate(old):
                j = c * len(old) + i
                new = []
                for e in range(len(held) // 2):
                    at_row = m * rows + (e * 2 * len(old) + j) * SUBLANES
                    moved = later(held[2 * e + 1], delays[at_row : at_row + SUBLANES], count)
                    base = held[2 * e]
                    new.append([base[b] + moved[b] if b < len(base) else moved[b] for b in range(count)])
                plane.append(new)
    count = blocks_of(span + HALF + local_levels * shift_max) + 1
    zero = jnp.zeros((SUBLANES, LANES), jnp.float32)
    for j in range(trials):
        at_row = grow * rows + j * SUBLANES
        shift = delays[at_row : at_row + SUBLANES] + (LANES - HALF)
        moved = later(plane[j][0], shift, count, far=True)
        level_ref[pl.ds(j, SUBLANES, stride=trials), :] = folded(moved + [zero] * (SUBLANES - count))
    eye = iota((trials, trials), 0) == iota((trials, trials), 1)
    for l in range(cd_ref.shape[0]):
        step = jnp.sum(jnp.where(eye, cd_ref[l : l + 1, :].astype(jnp.float32), 0.0), axis=1, keepdims=True)
        steps_ref[l * trials : (l + 1) * trials, :] = jnp.broadcast_to(step, (trials, LANES)).astype(jnp.int32)
    head_ref[...] = level_ref[trials : count * trials, :]
    body_ref[...] = level_ref[: body_ref.shape[0], :]


def join_kernel(trials, past, head_ref, body_ref, out_ref):
    for block in range(out_ref.shape[0] // trials):
        rows = slice(block * trials, (block + 1) * trials)
        parts = []
        if rows.stop <= head_ref.shape[0]:
            parts.append(head_ref[rows, :])
        if block >= past - 1:
            at_row = (block - past + 1) * trials
            parts.append(body_ref[at_row : at_row + trials, :])
        out_ref[rows, :] = sum(parts[1:], parts[0])


def merge_kernel(level, trials, scale, own_ref, there_ref, steps_ref, *out_refs):
    is_upper = lax.axis_index("sub") >> level & 1 == 1
    blocks = own_ref.shape[0] // trials
    shift = steps_ref[level * trials : (level + 1) * trials, :]
    lower, upper = [], []
    for block in range(blocks):
        rows = slice(block * trials, (block + 1) * trials)
        own, there = own_ref[rows, :], there_ref[rows, :]
        lower.append(jnp.where(is_upper, there, own))
        upper.append(jnp.where(is_upper, own, there))
    moved = later(upper, shift, blocks)
    per_ref = blocks // len(out_refs)
    for block in range(blocks):
        new = lower[block] + moved[block]
        at_row = block % per_ref * trials
        out_refs[block // per_ref][at_row : at_row + trials, :] = new if scale is None else new * scale


def last_kernel(trials, holder, own_ref, sent_ref, out_ref):
    is_holder = lax.axis_index("tm") == holder
    for block in range(own_ref.shape[0] // trials):
        rows = slice(block * trials, (block + 1) * trials)
        out_ref[:, block * LANES : (block + 1) * LANES] = jnp.where(is_holder, own_ref[rows, :], sent_ref[rows, :])


def shards(filterbank, bandpass, local_delays, cross_delays):
    rows, span = filterbank.shape
    cross_levels, trials = cross_delays.shape
    subs, spans = lax.axis_size("sub"), lax.axis_size("tm")
    local_levels = local_delays.shape[0]
    shift_max = span // 16
    past = span // LANES
    head = blocks_of(span + HALF + local_levels * shift_max)
    assert rows == LANES == trials * SUBLANES and spans == 2 and head <= spans * past

    vmem = pl.BlockSpec(memory_space=pltpu.VMEM)
    tiled = lambda count: jax.ShapeDtypeStruct((count * trials, LANES), jnp.float32)
    small = pltpu.CompilerParams(vmem_limit_bytes=1 << 20)
    args = (filterbank, bandpass[None, :], local_delays, cross_delays)
    start_rows = rows * blocks_of(span + 2 * HALF)
    head_part, body_part, steps = pl.pallas_call(
        functools.partial(plane_kernel, shift_max),
        out_shape=(
            tiled(head),
            tiled(past + 1),
            jax.ShapeDtypeStruct((cross_levels * trials, LANES), jnp.int32),
        ),
        in_specs=[pl.BlockSpec(memory_space=pltpu.HBM)] * len(args),
        out_specs=(vmem,) * 3,
        scratch_shapes=[pltpu.VMEM((start_rows, LANES), jnp.float32)]
        + [pltpu.VMEM(a.shape, a.dtype) for a in args]
        + [pltpu.SemaphoreType.DMA((len(args),))],
        compiler_params=pltpu.CompilerParams(vmem_limit_bytes=4 << 20),
    )(*[pltpu.with_memory_space_constraint(a, pltpu.HBM) for a in args])

    holder = 1
    head_part = lax.ppermute(head_part, "tm", [(0, 1)])
    plane = pl.pallas_call(
        functools.partial(join_kernel, trials, past),
        out_shape=tiled(spans * past),
        in_specs=[vmem] * 2,
        out_specs=vmem,
        compiler_params=small,
    )(head_part, body_part)
    for level in range(cross_levels):
        last = level == cross_levels - 1
        routes = [
            [(i * spans + holder, (i ^ apart) * spans + 1 - holder) for i in range(subs)]
            for apart in (1 << level, 0)
        ]
        there, own = [lax.ppermute(plane, ("sub", "tm"), route) for route in routes]
        holder = 1 - holder
        scale = 1.0 / math.sqrt(rows * subs) if last else None
        plane = pl.pallas_call(
            functools.partial(merge_kernel, level, trials, scale),
            out_shape=(tiled(past),) * spans if last else tiled(spans * past),
            in_specs=[vmem] * 3,
            out_specs=(vmem,) * spans if last else vmem,
            compiler_params=small,
        )(own, there, steps)
    sent = lax.ppermute(plane[1 - holder], "tm", [(holder, 1 - holder)])
    return pl.pallas_call(
        functools.partial(last_kernel, trials, holder),
        out_shape=jax.ShapeDtypeStruct((trials, span), jnp.float32),
        in_specs=[vmem] * 2,
        out_specs=vmem,
        compiler_params=small,
    )(plane[holder], sent)


def solution(mesh):
    return jax.shard_map(
        shards,
        mesh=mesh,
        in_specs=(P(("beam", "sub"), "tm"), P(("beam", "sub")), P(None, "sub"), P(None, "sub")),
        out_specs=P(("beam", "sub"), "tm"),
        check_vma=False,
    )
```

```python
import functools
import math

import jax
import jax.numpy as jnp
from jax import lax
from jax.experimental import pallas as pl
from jax.experimental.pallas import tpu as pltpu
from jax.sharding import PartitionSpec as P

LANES = 128
SUBLANES = 8
WINDOW = 31
HALF = WINDOW // 2


def iota(shape, axis):
    return lax.broadcasted_iota(jnp.int32, shape, axis)


def turned(x, index, axis):
    return jnp.take_along_axis(x, index, axis=axis, mode="promise_in_bounds")


def blocks_of(columns):
    return -(-columns // LANES)


def later(tiles, shift, count, far=False):
    source = iota(shift.shape, 1) - shift
    index = source & (LANES - 1)
    zero = jnp.zeros(shift.shape, jnp.float32)
    spun = [zero, zero] + [turned(tile, index, 1) for tile in tiles]
    spun += [zero] * (count + 2 - len(spun))
    got = []
    for b in range(count):
        prior = jnp.where(source >= -LANES, spun[b + 1], spun[b]) if far else spun[b + 1]
        got.append(jnp.where(source >= 0, spun[b + 2], prior))
    return got


def folded(tiles):
    row = iota(tiles[0].shape, 0)
    reach = SUBLANES // 2
    while reach:
        first = row & reach == 0
        tiles = [
            jnp.where(
                first,
                a + pltpu.roll(a, SUBLANES - reach, 0),
                b + pltpu.roll(b, reach, 0),
            )
            for a, b in zip(tiles[:reach], tiles[reach:])
        ]
        reach //= 2
    return tiles[0]


def plane_kernel(shift_max, *refs):
    sources, (head_ref, body_ref, steps_ref, level_ref), held, sems = refs[:4], refs[4:8], refs[8:12], refs[12]
    copies = [pltpu.make_async_copy(a, b, sems.at[i]) for i, (a, b) in enumerate(zip(sources, held))]
    for copy in copies:
        copy.start()
    fb_ref, bp_ref, ld_ref, cd_ref = held
    for copy in copies[1:]:
        copy.wait()
    rows, span = fb_ref.shape
    local_levels = ld_ref.shape[0]
    trials = cd_ref.shape[1]
    grow = trials.bit_length() - 1
    square = (rows, LANES)
    lane, row = iota(square, 1), iota(square, 0)
    inner, outer = row & (SUBLANES - 1), row >> 3

    pick = lane == inner * trials + outer
    parts = [jnp.where(pick, ld_ref[m : m + 1, :], 0).astype(jnp.bfloat16) for m in range(grow)]
    tail = jnp.zeros(square, jnp.int32)
    for m in range(grow, local_levels):
        bit = m - grow
        use = (lane == (inner >> (bit + 1)) * trials + outer) & (inner >> bit & 1 == 1)
        tail = tail + jnp.where(use, ld_ref[m : m + 1, :], 0)
    parts.append(tail.astype(jnp.float32).astype(jnp.bfloat16))
    rest = bp_ref[...]
    for _ in range(3):
        part = rest.astype(jnp.bfloat16)
        rest = rest - part.astype(jnp.float32)
        parts.append(jnp.where(pick, part.astype(jnp.float32), 0.0).astype(jnp.bfloat16))
    ones = jnp.ones((rows, LANES), jnp.bfloat16)
    spread = jnp.dot(jnp.concatenate(parts, axis=0), ones, preferred_element_type=jnp.float32)
    delays = spread[: (grow + 1) * rows].astype(jnp.int32)
    gain = spread[(grow + 1) * rows :]
    gain = (gain[:rows] + gain[rows : 2 * rows] + gain[2 * rows :]) * (1.0 / WINDOW)

    at = iota((2 * LANES, LANES), 0) - LANES
    to = iota((2 * LANES, LANES), 1) - HALF
    band = jnp.where(at == to, float(WINDOW), 0.0) - jnp.where(jnp.abs(at - to) <= HALF, 1.0, 0.0)
    band = band.astype(jnp.bfloat16)
    whole = span // LANES
    start_blocks = blocks_of(span + 2 * HALF)
    copies[0].wait()
    for block in range(start_blocks):
        low, high = max(block - 1, 0), min(block + 1, whole)
        part = band[(low - block + 1) * LANES : (high - block + 1) * LANES]
        level_ref[block * rows : (block + 1) * rows, :] = jnp.dot(
            fb_ref[:, low * LANES : high * LANES], part, preferred_element_type=jnp.float32
        )

    first_span = lax.axis_index("tm") == 0
    early = jnp.logical_and(iota((SUBLANES, LANES), 1) < HALF, first_span)
    bands = []
    for e in range(trials):
        scale = gain[e * SUBLANES : (e + 1) * SUBLANES]
        tiles = []
        for block in range(start_blocks):
            tile = level_ref[pl.ds(block * rows + e, SUBLANES, stride=trials), :] * scale
            tiles.append(jnp.where(early, 0.0, tile) if block == 0 else tile)
        bands.append(tiles)
    plane = [bands]
    for m in range(grow):
        count = blocks_of(span + 2 * HALF + (m + 1) * shift_max)
        old, plane = plane, []
        for c in range(2):
            for i, held in enumerate(old):
                j = c * len(old) + i
                new = []
                for e in range(len(held) // 2):
                    at_row = m * rows + (e * 2 * len(old) + j) * SUBLANES
                    moved = later(held[2 * e + 1], delays[at_row : at_row + SUBLANES], count)
                    base = held[2 * e]
                    new.append([base[b] + moved[b] if b < len(base) else moved[b] for b in range(count)])
                plane.append(new)
    count = blocks_of(span + HALF + local_levels * shift_max) + 1
    zero = jnp.zeros((SUBLANES, LANES), jnp.float32)
    for j in range(trials):
        at_row = grow * rows + j * SUBLANES
        shift = delays[at_row : at_row + SUBLANES] + (LANES - HALF)
        moved = later(plane[j][0], shift, count, far=True)
        level_ref[pl.ds(j, SUBLANES, stride=trials), :] = folded(moved + [zero] * (SUBLANES - count))
    eye = iota((trials, trials), 0) == iota((trials, trials), 1)
    for l in range(cd_ref.shape[0]):
        step = jnp.sum(jnp.where(eye, cd_ref[l : l + 1, :].astype(jnp.float32), 0.0), axis=1, keepdims=True)
        steps_ref[l * trials : (l + 1) * trials, :] = jnp.broadcast_to(step, (trials, LANES)).astype(jnp.int32)
    head_ref[...] = level_ref[trials : count * trials, :]
    body_ref[...] = level_ref[: body_ref.shape[0], :]


def join_kernel(trials, past, head_ref, body_ref, out_ref):
    for block in range(out_ref.shape[0] // trials):
        rows = slice(block * trials, (block + 1) * trials)
        parts = []
        if rows.stop <= head_ref.shape[0]:
            parts.append(head_ref[rows, :])
        if block >= past - 1:
            at_row = (block - past + 1) * trials
            parts.append(body_ref[at_row : at_row + trials, :])
        out_ref[rows, :] = sum(parts[1:], parts[0])


def merge_kernel(level, trials, scale, own_ref, there_ref, steps_ref, *out_refs):
    is_upper = lax.axis_index("sub") >> level & 1 == 1
    blocks = own_ref.shape[0] // trials
    shift = steps_ref[level * trials : (level + 1) * trials, :]
    lower, upper = [], []
    for block in range(blocks):
        rows = slice(block * trials, (block + 1) * trials)
        own, there = own_ref[rows, :], there_ref[rows, :]
        lower.append(jnp.where(is_upper, there, own))
        upper.append(jnp.where(is_upper, own, there))
    moved = later(upper, shift, blocks)
    per_ref = blocks // len(out_refs)
    for block in range(blocks):
        new = lower[block] + moved[block]
        at_row = block % per_ref * trials
        out_refs[block // per_ref][at_row : at_row + trials, :] = new if scale is None else new * scale


def last_kernel(trials, holder, own_ref, sent_ref, out_ref):
    is_holder = lax.axis_index("tm") == holder
    for block in range(own_ref.shape[0] // trials):
        rows = slice(block * trials, (block + 1) * trials)
        out_ref[:, block * LANES : (block + 1) * LANES] = jnp.where(is_holder, own_ref[rows, :], sent_ref[rows, :])


def shards(filterbank, bandpass, local_delays, cross_delays):
    rows, span = filterbank.shape
    cross_levels, trials = cross_delays.shape
    subs, spans = lax.axis_size("sub"), lax.axis_size("tm")
    local_levels = local_delays.shape[0]
    shift_max = span // 16
    past = span // LANES
    head = blocks_of(span + HALF + local_levels * shift_max)
    assert rows == LANES == trials * SUBLANES and spans == 2 and head <= spans * past

    vmem = pl.BlockSpec(memory_space=pltpu.VMEM)
    tiled = lambda count: jax.ShapeDtypeStruct((count * trials, LANES), jnp.float32)
    small = pltpu.CompilerParams(vmem_limit_bytes=1 << 20)
    args = (filterbank, bandpass[None, :], local_delays, cross_delays)
    start_rows = rows * blocks_of(span + 2 * HALF)
    head_part, body_part, steps = pl.pallas_call(
        functools.partial(plane_kernel, shift_max),
        out_shape=(
            tiled(head),
            tiled(past + 1),
            jax.ShapeDtypeStruct((cross_levels * trials, LANES), jnp.int32),
        ),
        in_specs=[pl.BlockSpec(memory_space=pltpu.HBM)] * len(args),
        out_specs=(vmem,) * 3,
        scratch_shapes=[pltpu.VMEM((start_rows, LANES), jnp.float32)]
        + [pltpu.VMEM(a.shape, a.dtype) for a in args]
        + [pltpu.SemaphoreType.DMA((len(args),))],
        compiler_params=pltpu.CompilerParams(vmem_limit_bytes=4 << 20),
    )(*[pltpu.with_memory_space_constraint(a, pltpu.HBM) for a in args])

    holder = 1
    swap = [(0, 1), (1, 0)]
    head_part = lax.ppermute(head_part, "tm", swap)
    plane = pl.pallas_call(
        functools.partial(join_kernel, trials, past),
        out_shape=tiled(spans * past),
        in_specs=[vmem] * 2,
        out_specs=vmem,
        compiler_params=small,
    )(head_part, body_part)
    for level in range(cross_levels):
        last = level == cross_levels - 1
        apart = 1 << level
        route = [(i * spans + c, (i ^ apart if c == holder else i) * spans + c) for i in range(subs) for c in range(spans)]
        there = lax.ppermute(plane, ("sub", "tm"), route)
        scale = 1.0 / math.sqrt(rows * subs) if last else None
        plane = pl.pallas_call(
            functools.partial(merge_kernel, level, trials, scale),
            out_shape=(tiled(past),) * spans if last else tiled(spans * past),
            in_specs=[vmem] * 3,
            out_specs=(vmem,) * spans if last else vmem,
            compiler_params=small,
        )(plane, there, steps)
    sent = lax.ppermute(plane[1 - holder], "tm", swap)
    return pl.pallas_call(
        functools.partial(last_kernel, trials, holder),
        out_shape=jax.ShapeDtypeStruct((trials, span), jnp.float32),
        in_specs=[vmem] * 2,
        out_specs=vmem,
        compiler_params=small,
    )(plane[holder], sent)


def solution(mesh):
    return jax.shard_map(
        shards,
        mesh=mesh,
        in_specs=(P(("beam", "sub"), "tm"), P(("beam", "sub")), P(None, "sub"), P(None, "sub")),
        out_specs=P(("beam", "sub"), "tm"),
        check_vma=False,
    )
```

```python
import functools
import math

import jax
import jax.numpy as jnp
from jax import lax
from jax.experimental import pallas as pl
from jax.experimental.pallas import tpu as pltpu
from jax.sharding import PartitionSpec as P

LANES = 128
SUBLANES = 8
WINDOW = 31
HALF = WINDOW // 2


def iota(shape, axis):
    return lax.broadcasted_iota(jnp.int32, shape, axis)


def turned(x, index, axis):
    return jnp.take_along_axis(x, index, axis=axis, mode="promise_in_bounds")


def blocks_of(columns):
    return -(-columns // LANES)


def later(tiles, shift, count, far=False):
    source = iota(shift.shape, 1) - shift
    index = source & (LANES - 1)
    zero = jnp.zeros(shift.shape, jnp.float32)
    spun = [zero, zero] + [turned(tile, index, 1) for tile in tiles]
    spun += [zero] * (count + 2 - len(spun))
    got = []
    for b in range(count):
        prior = jnp.where(source >= -LANES, spun[b + 1], spun[b]) if far else spun[b + 1]
        got.append(jnp.where(source >= 0, spun[b + 2], prior))
    return got


def folded(tiles):
    row = iota(tiles[0].shape, 0)
    reach = SUBLANES // 2
    while reach:
        first = row & reach == 0
        tiles = [
            jnp.where(
                first,
                a + pltpu.roll(a, SUBLANES - reach, 0),
                b + pltpu.roll(b, reach, 0),
            )
            for a, b in zip(tiles[:reach], tiles[reach:])
        ]
        reach //= 2
    return tiles[0]


def plane_kernel(shift_max, lead, *refs):
    sources, (plane_ref, edge_ref, steps_ref, level_ref), held, sems = refs[:4], refs[4:8], refs[8:12], refs[12]
    copies = [pltpu.make_async_copy(a, b, sems.at[i]) for i, (a, b) in enumerate(zip(sources, held))]
    for copy in copies:
        copy.start()
    fb_ref, bp_ref, ld_ref, cd_ref = held
    for copy in copies[1:]:
        copy.wait()
    rows, span = fb_ref.shape
    local_levels = ld_ref.shape[0]
    trials = cd_ref.shape[1]
    grow = trials.bit_length() - 1
    square = (rows, LANES)
    lane, row = iota(square, 1), iota(square, 0)
    inner, outer = row & (SUBLANES - 1), row >> 3

    pick = lane == inner * trials + outer
    parts = [jnp.where(pick, ld_ref[m : m + 1, :], 0).astype(jnp.bfloat16) for m in range(grow)]
    tail = jnp.zeros(square, jnp.int32)
    for m in range(grow, local_levels):
        bit = m - grow
        use = (lane == (inner >> (bit + 1)) * trials + outer) & (inner >> bit & 1 == 1)
        tail = tail + jnp.where(use, ld_ref[m : m + 1, :], 0)
    parts.append(tail.astype(jnp.float32).astype(jnp.bfloat16))
    rest = bp_ref[...]
    for _ in range(3):
        part = rest.astype(jnp.bfloat16)
        rest = rest - part.astype(jnp.float32)
        parts.append(jnp.where(pick, part.astype(jnp.float32), 0.0).astype(jnp.bfloat16))
    ones = jnp.ones((rows, LANES), jnp.bfloat16)
    spread = jnp.dot(jnp.concatenate(parts, axis=0), ones, preferred_element_type=jnp.float32)
    delays = spread[: (grow + 1) * rows].astype(jnp.int32)
    gain = spread[(grow + 1) * rows :]
    gain = (gain[:rows] + gain[rows : 2 * rows] + gain[2 * rows :]) * (1.0 / WINDOW)

    at = iota((2 * LANES, LANES), 0) - LANES
    to = iota((2 * LANES, LANES), 1) - HALF
    band = jnp.where(at == to, float(WINDOW), 0.0) - jnp.where(jnp.abs(at - to) <= HALF, 1.0, 0.0)
    band = band.astype(jnp.bfloat16)
    whole = span // LANES
    start_blocks = blocks_of(span + 2 * HALF)
    copies[0].wait()
    for block in range(start_blocks):
        low, high = max(block - 1, 0), min(block + 1, whole)
        part = band[(low - block + 1) * LANES : (high - block + 1) * LANES]
        level_ref[block * rows : (block + 1) * rows, :] = jnp.dot(
            fb_ref[:, low * LANES : high * LANES], part, preferred_element_type=jnp.float32
        )

    first_span = lax.axis_index("tm") == 0
    early = jnp.logical_and(iota((SUBLANES, LANES), 1) < HALF, first_span)
    bands = []
    for e in range(trials):
        scale = gain[e * SUBLANES : (e + 1) * SUBLANES]
        tiles = []
        for block in range(start_blocks):
            tile = level_ref[pl.ds(block * rows + e, SUBLANES, stride=trials), :] * scale
            tiles.append(jnp.where(early, 0.0, tile) if block == 0 else tile)
        bands.append(tiles)
    plane = [bands]
    for m in range(grow):
        count = blocks_of(span + 2 * HALF + (m + 1) * shift_max)
        old, plane = plane, []
        for c in range(2):
            for i, held in enumerate(old):
                j = c * len(old) + i
                new = []
                for e in range(len(held) // 2):
                    at_row = m * rows + (e * 2 * len(old) + j) * SUBLANES
                    moved = later(held[2 * e + 1], delays[at_row : at_row + SUBLANES], count)
                    base = held[2 * e]
                    new.append([base[b] + moved[b] if b < len(base) else moved[b] for b in range(count)])
                plane.append(new)
    count = blocks_of(span + HALF + local_levels * shift_max) + lead
    zero = jnp.zeros((SUBLANES, LANES), jnp.float32)
    for j in range(trials):
        at_row = grow * rows + j * SUBLANES
        shift = delays[at_row : at_row + SUBLANES] + (LANES - HALF)
        moved = later([zero] * (lead - 1) + plane[j][0], shift, count, far=True)
        level_ref[pl.ds(j, SUBLANES, stride=trials), :] = folded(moved + [zero] * (SUBLANES - count))
    eye = iota((trials, trials), 0) == iota((trials, trials), 1)
    for l in range(cd_ref.shape[0]):
        step = jnp.sum(jnp.where(eye, cd_ref[l : l + 1, :].astype(jnp.float32), 0.0), axis=1, keepdims=True)
        steps_ref[l * trials : (l + 1) * trials, :] = jnp.broadcast_to(step, (trials, LANES)).astype(jnp.int32)
    own = plane_ref.shape[0] // trials
    plane_ref[...] = level_ref[: own * trials, :]
    past = span // LANES
    width = edge_ref.shape[0] // trials
    edge_ref[...] = jnp.where(
        first_span,
        level_ref[past * trials : (past + width) * trials, :],
        level_ref[: width * trials, :],
    )


def join_kernel(past, lead, trials, plane_ref, edge_ref, out_ref):
    first_span = lax.axis_index("tm") == 0
    for block in range(plane_ref.shape[0] // trials):
        rows = slice(block * trials, (block + 1) * trials)
        here = plane_ref[rows, :]
        if rows.stop <= edge_ref.shape[0]:
            here = here + jnp.where(first_span, 0.0, edge_ref[rows, :])
        if block == past + lead - 1:
            there = edge_ref[(lead - 1) * trials : lead * trials, :]
            here = here + jnp.where(first_span, there, 0.0)
        out_ref[rows, :] = here


def put(out_ref, block, trials, lead, scale, new):
    if scale is None:
        out_ref[block * trials : (block + 1) * trials, :] = new
    elif block >= lead:
        out_ref[:, (block - lead) * LANES : (block - lead + 1) * LANES] = new * scale


def merge_kernel(level, trials, lead, scale, own_ref, there_ref, steps_ref, out_ref):
    is_upper = lax.axis_index("sub") >> level & 1 == 1
    blocks = own_ref.shape[0] // trials
    shift = steps_ref[level * trials : (level + 1) * trials, :]
    lower, upper = [], []
    for block in range(blocks):
        rows = slice(block * trials, (block + 1) * trials)
        own, there = own_ref[rows, :], there_ref[rows, :]
        lower.append(jnp.where(is_upper, there, own))
        upper.append(jnp.where(is_upper, own, there))
    moved = later(upper, shift, blocks)
    for block in range(blocks):
        put(out_ref, block, trials, lead, scale, lower[block] + moved[block])


def packed_kernel(level, trials, plane_ref, steps_ref, out_ref):
    rows = plane_ref.shape[0]
    note = steps_ref[level * trials : (level + 1) * trials, :].astype(jnp.float32)
    for slot in range(4):
        start = slot * (rows + trials)
        out_ref[start : start + rows, :] = plane_ref[...]
        out_ref[start + rows : start + rows + trials, :] = note


def merge_two_kernel(level, trials, lead, scale, in_ref, steps_ref, out_ref):
    is_odd = lax.axis_index("sub") >> level & 1 == 1
    stride = in_ref.shape[0] // 4
    blocks = stride // trials - 1
    outer = steps_ref[(level + 1) * trials : (level + 2) * trials, :]
    total = None
    for q in range(4):
        tiles = [in_ref[q * stride + b * trials : q * stride + (b + 1) * trials, :] for b in range(blocks)]
        if q:
            shift = outer if q >> 1 else jnp.zeros((trials, LANES), jnp.int32)
            if q & 1:
                notes = [
                    in_ref[(k + 1) * stride - trials : (k + 1) * stride, :] for k in (q - 1, q)
                ]
                shift = shift + jnp.where(is_odd, notes[1], notes[0]).astype(jnp.int32)
            tiles = later(tiles, shift, blocks)
        total = tiles if total is None else [a + b for a, b in zip(total, tiles)]
    for block in range(blocks):
        put(out_ref, block, trials, lead, scale, total[block])


def shards(filterbank, bandpass, local_delays, cross_delays):
    rows, span = filterbank.shape
    cross_levels, trials = cross_delays.shape
    subs = lax.axis_size("sub")
    local_levels = local_delays.shape[0]
    shift_max = span // 16
    lead = blocks_of(cross_levels * shift_max)
    past = span // LANES
    width = blocks_of(lead * LANES + HALF + local_levels * shift_max)
    assert rows == LANES == trials * SUBLANES and lax.axis_size("tm") == 2

    vmem = pl.BlockSpec(memory_space=pltpu.VMEM)
    tiled = lambda count: jax.ShapeDtypeStruct((count * trials, LANES), jnp.float32)
    small = pltpu.CompilerParams(vmem_limit_bytes=1 << 20)
    start_rows = rows * blocks_of(span + 2 * HALF)
    args = (filterbank, bandpass[None, :], local_delays, cross_delays)
    plane, edge, steps = pl.pallas_call(
        functools.partial(plane_kernel, shift_max, lead),
        out_shape=(
            tiled(lead + past),
            tiled(width),
            jax.ShapeDtypeStruct((cross_levels * trials, LANES), jnp.int32),
        ),
        in_specs=[pl.BlockSpec(memory_space=pltpu.HBM)] * len(args),
        out_specs=(vmem,) * 3,
        scratch_shapes=[pltpu.VMEM((start_rows, LANES), jnp.float32)]
        + [pltpu.VMEM(a.shape, a.dtype) for a in args]
        + [pltpu.SemaphoreType.DMA((len(args),))],
        compiler_params=pltpu.CompilerParams(vmem_limit_bytes=4 << 20),
    )(*[pltpu.with_memory_space_constraint(a, pltpu.HBM) for a in args])
    edge = lax.ppermute(edge, "tm", [(0, 1), (1, 0)])
    plane = pl.pallas_call(
        functools.partial(join_kernel, past, lead, trials),
        out_shape=tiled(lead + past),
        in_specs=[vmem] * 2,
        out_specs=vmem,
        compiler_params=small,
    )(plane, edge)
    level = 0
    while level < cross_levels:
        pair = level + 1 < cross_levels
        last = level + 1 + pair == cross_levels
        scale = 1.0 / math.sqrt(rows * subs) if last else None
        shape = jax.ShapeDtypeStruct((trials, span), jnp.float32) if last else tiled(lead + past)
        call = functools.partial(pl.pallas_call, out_specs=vmem, compiler_params=small)
        if pair:
            packed = call(
                functools.partial(packed_kernel, level, trials),
                out_shape=tiled(4 * (lead + past + 1)),
                in_specs=[vmem] * 2,
            )(plane, steps)
            groups = [
                [i | k << level for k in range(4)] for i in range(subs) if i >> level & 3 == 0
            ]
            inbox = lax.all_to_all(
                packed.reshape(4, -1, LANES), "sub", 0, 0, axis_index_groups=groups, tiled=True
            )
            plane = call(
                functools.partial(merge_two_kernel, level, trials, lead, scale),
                out_shape=shape,
                in_specs=[vmem] * 2,
            )(inbox.reshape(-1, LANES), steps)
        else:
            there = lax.ppermute(plane, "sub", [(i, i ^ 1 << level) for i in range(subs)])
            plane = call(
                functools.partial(merge_kernel, level, trials, lead, scale),
                out_shape=shape,
                in_specs=[vmem] * 3,
            )(plane, there, steps)
        level += 1 + pair
    return plane


def solution(mesh):
    return jax.shard_map(
        shards,
        mesh=mesh,
        in_specs=(P(("beam", "sub"), "tm"), P(("beam", "sub")), P(None, "sub"), P(None, "sub")),
        out_specs=P(("beam", "sub"), "tm"),
        check_vma=False,
    )
```

```python
import functools
import math

import jax
import jax.numpy as jnp
from jax import lax
from jax.experimental import pallas as pl
from jax.experimental.pallas import tpu as pltpu
from jax.sharding import PartitionSpec as P

LANES = 128
SUBLANES = 8
WINDOW = 31
HALF = WINDOW // 2


def iota(shape, axis):
    return lax.broadcasted_iota(jnp.int32, shape, axis)


def turned(x, index, axis):
    return jnp.take_along_axis(x, index, axis=axis, mode="promise_in_bounds")


def blocks_of(columns):
    return -(-columns // LANES)


def later(tiles, shift, count, far=False):
    source = iota(shift.shape, 1) - shift
    index = source & (LANES - 1)
    zero = jnp.zeros(shift.shape, jnp.float32)
    spun = [zero, zero] + [turned(tile, index, 1) for tile in tiles]
    spun += [zero] * (count + 2 - len(spun))
    got = []
    for b in range(count):
        prior = jnp.where(source >= -LANES, spun[b + 1], spun[b]) if far else spun[b + 1]
        got.append(jnp.where(source >= 0, spun[b + 2], prior))
    return got


def folded(tiles):
    row = iota(tiles[0].shape, 0)
    reach = SUBLANES // 2
    while reach:
        first = row & reach == 0
        tiles = [
            jnp.where(
                first,
                a + pltpu.roll(a, SUBLANES - reach, 0),
                b + pltpu.roll(b, reach, 0),
            )
            for a, b in zip(tiles[:reach], tiles[reach:])
        ]
        reach //= 2
    return tiles[0]


def plane_kernel(shift_max, *refs):
    sources, (keep_ref, send_ref, steps_ref, level_ref), held, sems = refs[:4], refs[4:8], refs[8:12], refs[12]
    copies = [pltpu.make_async_copy(a, b, sems.at[i]) for i, (a, b) in enumerate(zip(sources, held))]
    for copy in copies:
        copy.start()
    fb_ref, bp_ref, ld_ref, cd_ref = held
    for copy in copies[1:]:
        copy.wait()
    rows, span = fb_ref.shape
    local_levels = ld_ref.shape[0]
    trials = cd_ref.shape[1]
    grow = trials.bit_length() - 1
    square = (rows, LANES)
    lane, row = iota(square, 1), iota(square, 0)
    inner, outer = row & (SUBLANES - 1), row >> 3

    pick = lane == inner * trials + outer
    parts = [jnp.where(pick, ld_ref[m : m + 1, :], 0).astype(jnp.bfloat16) for m in range(grow)]
    tail = jnp.zeros(square, jnp.int32)
    for m in range(grow, local_levels):
        bit = m - grow
        use = (lane == (inner >> (bit + 1)) * trials + outer) & (inner >> bit & 1 == 1)
        tail = tail + jnp.where(use, ld_ref[m : m + 1, :], 0)
    parts.append(tail.astype(jnp.float32).astype(jnp.bfloat16))
    rest = bp_ref[...]
    for _ in range(3):
        part = rest.astype(jnp.bfloat16)
        rest = rest - part.astype(jnp.float32)
        parts.append(jnp.where(pick, part.astype(jnp.float32), 0.0).astype(jnp.bfloat16))
    ones = jnp.ones((rows, LANES), jnp.bfloat16)
    spread = jnp.dot(jnp.concatenate(parts, axis=0), ones, preferred_element_type=jnp.float32)
    delays = spread[: (grow + 1) * rows].astype(jnp.int32)
    gain = spread[(grow + 1) * rows :]
    gain = (gain[:rows] + gain[rows : 2 * rows] + gain[2 * rows :]) * (1.0 / WINDOW)

    at = iota((2 * LANES, LANES), 0) - LANES
    to = iota((2 * LANES, LANES), 1) - HALF
    band = jnp.where(at == to, float(WINDOW), 0.0) - jnp.where(jnp.abs(at - to) <= HALF, 1.0, 0.0)
    band = band.astype(jnp.bfloat16)
    whole = span // LANES
    start_blocks = blocks_of(span + 2 * HALF)
    copies[0].wait()
    for block in range(start_blocks):
        low, high = max(block - 1, 0), min(block + 1, whole)
        part = band[(low - block + 1) * LANES : (high - block + 1) * LANES]
        level_ref[block * rows : (block + 1) * rows, :] = jnp.dot(
            fb_ref[:, low * LANES : high * LANES], part, preferred_element_type=jnp.float32
        )

    first_span = lax.axis_index("tm") == 0
    early = jnp.logical_and(iota((SUBLANES, LANES), 1) < HALF, first_span)
    bands = []
    for e in range(trials):
        scale = gain[e * SUBLANES : (e + 1) * SUBLANES]
        tiles = []
        for block in range(start_blocks):
            tile = level_ref[pl.ds(block * rows + e, SUBLANES, stride=trials), :] * scale
            tiles.append(jnp.where(early, 0.0, tile) if block == 0 else tile)
        bands.append(tiles)
    plane = [bands]
    for m in range(grow):
        count = blocks_of(span + 2 * HALF + (m + 1) * shift_max)
        old, plane = plane, []
        for c in range(2):
            for i, held in enumerate(old):
                j = c * len(old) + i
                new = []
                for e in range(len(held) // 2):
                    at_row = m * rows + (e * 2 * len(old) + j) * SUBLANES
                    moved = later(held[2 * e + 1], delays[at_row : at_row + SUBLANES], count)
                    base = held[2 * e]
                    new.append([base[b] + moved[b] if b < len(base) else moved[b] for b in range(count)])
                plane.append(new)
    count = blocks_of(span + HALF + local_levels * shift_max) + 1
    zero = jnp.zeros((SUBLANES, LANES), jnp.float32)
    for j in range(trials):
        at_row = grow * rows + j * SUBLANES
        shift = delays[at_row : at_row + SUBLANES] + (LANES - HALF)
        moved = later(plane[j][0], shift, count, far=True)
        level_ref[pl.ds(j, SUBLANES, stride=trials), :] = folded(moved + [zero] * (SUBLANES - count))
    lower_rows = row_half(cd_ref.shape[0]) == 0
    for block in range(count):
        rows0 = level_ref[block * trials : block * trials + SUBLANES, :]
        rows1 = level_ref[block * trials + SUBLANES : (block + 1) * trials, :]
        keep_ref[block * SUBLANES : (block + 1) * SUBLANES, :] = jnp.where(lower_rows, rows0, rows1)
        send_ref[block * SUBLANES : (block + 1) * SUBLANES, :] = jnp.where(lower_rows, rows1, rows0)
    eye = iota((trials, trials), 0) == iota((trials, trials), 1)
    for l in range(cd_ref.shape[0]):
        step = jnp.sum(jnp.where(eye, cd_ref[l : l + 1, :].astype(jnp.float32), 0.0), axis=1, keepdims=True)
        step = jnp.where(lower_rows, step[:SUBLANES], step[SUBLANES:])
        step = jnp.broadcast_to(step, (SUBLANES, LANES)).astype(jnp.int32)
        steps_ref[l * SUBLANES : (l + 1) * SUBLANES, :] = step


def row_half(cross_levels):
    half = lax.axis_index("tm")
    for level in range(cross_levels):
        half = half ^ (lax.axis_index("sub") >> level & 1)
    return half


def tile_of(ref, block):
    return ref[block * SUBLANES : (block + 1) * SUBLANES, :]


def join_kernel(past, keep_ref, there_ref, out_ref):
    first_span = lax.axis_index("tm") == 0
    held = keep_ref.shape[0] // SUBLANES
    for block in range(out_ref.shape[0] // SUBLANES):
        new = None
        if block + 1 < held:
            new = jnp.where(first_span, tile_of(keep_ref, block + 1), tile_of(there_ref, block + 1))
        if block >= past - 1:
            at = block - past + 1
            other = jnp.where(first_span, tile_of(there_ref, at), tile_of(keep_ref, at))
            new = other if new is None else new + other
        out_ref[block * SUBLANES : (block + 1) * SUBLANES, :] = new


def merge_kernel(level, scale, own_ref, there_ref, steps_ref, out_ref, send_ref=None):
    is_upper = lax.axis_index("sub") >> level & 1 == 1
    blocks = own_ref.shape[0] // SUBLANES
    lower, upper = [], []
    for block in range(blocks):
        own, there = tile_of(own_ref, block), tile_of(there_ref, block)
        lower.append(jnp.where(is_upper, there, own))
        upper.append(jnp.where(is_upper, own, there))
    moved = later(upper, tile_of(steps_ref, level), blocks)
    new = [a + b for a, b in zip(lower, moved)]
    if scale is None:
        for block in range(blocks):
            out_ref[block * SUBLANES : (block + 1) * SUBLANES, :] = new[block]
        return
    first_span = lax.axis_index("tm") == 0
    past = blocks // 2
    for block in range(past):
        early, late = new[block] * scale, new[block + past] * scale
        out_ref[block * SUBLANES : (block + 1) * SUBLANES, :] = jnp.where(first_span, early, late)
        send_ref[block * SUBLANES : (block + 1) * SUBLANES, :] = jnp.where(first_span, late, early)


def last_kernel(cross_levels, keep_ref, there_ref, out_ref):
    lower_rows = row_half(cross_levels) == 0
    for block in range(keep_ref.shape[0] // SUBLANES):
        keep, there = tile_of(keep_ref, block), tile_of(there_ref, block)
        cols = slice(block * LANES, (block + 1) * LANES)
        out_ref[:SUBLANES, cols] = jnp.where(lower_rows, keep, there)
        out_ref[SUBLANES:, cols] = jnp.where(lower_rows, there, keep)


def shards(filterbank, bandpass, local_delays, cross_delays):
    rows, span = filterbank.shape
    cross_levels, trials = cross_delays.shape
    subs, spans = lax.axis_size("sub"), lax.axis_size("tm")
    local_levels = local_delays.shape[0]
    shift_max = span // 16
    past = span // LANES
    held = blocks_of(span + HALF + local_levels * shift_max) + 1
    assert rows == LANES == trials * SUBLANES and trials == 2 * SUBLANES
    assert spans == 2 and held <= SUBLANES

    vmem = pl.BlockSpec(memory_space=pltpu.VMEM)
    tiled = lambda count, kind=jnp.float32: jax.ShapeDtypeStruct((count * SUBLANES, LANES), kind)
    small = pltpu.CompilerParams(vmem_limit_bytes=1 << 20)
    call = functools.partial(pl.pallas_call, compiler_params=small)
    args = (filterbank, bandpass[None, :], local_delays, cross_delays)
    start_rows = rows * blocks_of(span + 2 * HALF)
    keep, send, steps = pl.pallas_call(
        functools.partial(plane_kernel, shift_max),
        out_shape=(tiled(held), tiled(held), tiled(cross_levels, jnp.int32)),
        in_specs=[pl.BlockSpec(memory_space=pltpu.HBM)] * len(args),
        out_specs=(vmem,) * 3,
        scratch_shapes=[pltpu.VMEM((start_rows, LANES), jnp.float32)]
        + [pltpu.VMEM(a.shape, a.dtype) for a in args]
        + [pltpu.SemaphoreType.DMA((len(args),))],
        compiler_params=pltpu.CompilerParams(vmem_limit_bytes=4 << 20),
    )(*[pltpu.with_memory_space_constraint(a, pltpu.HBM) for a in args])
    swap = [(0, 1), (1, 0)]
    there = lax.ppermute(send, "tm", swap)
    plane = call(
        functools.partial(join_kernel, past),
        out_shape=tiled(spans * past),
        in_specs=[vmem] * 2,
        out_specs=vmem,
    )(keep, there)
    for level in range(cross_levels):
        last = level == cross_levels - 1
        mask = spans << level | 1
        there = lax.ppermute(plane, ("sub", "tm"), [(i, i ^ mask) for i in range(subs * spans)])
        scale = 1.0 / math.sqrt(rows * subs) if last else None
        plane = call(
            functools.partial(merge_kernel, level, scale),
            out_shape=(tiled(past),) * 2 if last else tiled(spans * past),
            in_specs=[vmem] * 3,
            out_specs=(vmem,) * 2 if last else vmem,
        )(plane, there, steps)
    keep, send = plane
    return call(
        functools.partial(last_kernel, cross_levels),
        out_shape=jax.ShapeDtypeStruct((trials, span), jnp.float32),
        in_specs=[vmem] * 2,
        out_specs=vmem,
    )(keep, lax.ppermute(send, "tm", swap))


def solution(mesh):
    return jax.shard_map(
        shards,
        mesh=mesh,
        in_specs=(P(("beam", "sub"), "tm"), P(("beam", "sub")), P(None, "sub"), P(None, "sub")),
        out_specs=P(("beam", "sub"), "tm"),
        check_vma=False,
    )
```

```python
import functools
import math

import jax
import jax.numpy as jnp
from jax import lax
from jax.experimental import pallas as pl
from jax.experimental.pallas import tpu as pltpu
from jax.sharding import PartitionSpec as P

LANES = 128
SUBLANES = 8
WINDOW = 31
HALF = WINDOW // 2


def iota(shape, axis):
    return lax.broadcasted_iota(jnp.int32, shape, axis)


def turned(x, index, axis):
    return jnp.take_along_axis(x, index, axis=axis, mode="promise_in_bounds")


def blocks_of(columns):
    return -(-columns // LANES)


def later(tiles, shift, count, far=False):
    source = iota(shift.shape, 1) - shift
    index = source & (LANES - 1)
    zero = jnp.zeros(shift.shape, jnp.float32)
    spun = [zero, zero] + [turned(tile, index, 1) for tile in tiles]
    spun += [zero] * (count + 2 - len(spun))
    got = []
    for b in range(count):
        prior = jnp.where(source >= -LANES, spun[b + 1], spun[b]) if far else spun[b + 1]
        got.append(jnp.where(source >= 0, spun[b + 2], prior))
    return got


def folded(tiles):
    row = iota(tiles[0].shape, 0)
    reach = SUBLANES // 2
    while reach:
        first = row & reach == 0
        tiles = [
            jnp.where(
                first,
                a + pltpu.roll(a, SUBLANES - reach, 0),
                b + pltpu.roll(b, reach, 0),
            )
            for a, b in zip(tiles[:reach], tiles[reach:])
        ]
        reach //= 2
    return tiles[0]


def plane_kernel(shift_max, *refs):
    sources, (keep_ref, send_ref, steps_ref, level_ref), held, sems = refs[:4], refs[4:8], refs[8:12], refs[12]
    copies = [pltpu.make_async_copy(a, b, sems.at[i]) for i, (a, b) in enumerate(zip(sources, held))]
    for copy in copies:
        copy.start()
    fb_ref, bp_ref, ld_ref, cd_ref = held
    rows, span = fb_ref.shape
    local_levels = ld_ref.shape[0]
    trials = cd_ref.shape[1]
    grow = trials.bit_length() - 1
    square = (rows, LANES)
    lane, row = iota(square, 1), iota(square, 0)
    inner, outer = row & (SUBLANES - 1), row >> 3

    at = iota((2 * LANES, LANES), 0) - LANES
    to = iota((2 * LANES, LANES), 1) - HALF
    band = jnp.where(at == to, float(WINDOW), 0.0) - jnp.where(jnp.abs(at - to) <= HALF, 1.0, 0.0)
    band = band.astype(jnp.bfloat16)
    pick = lane == inner * trials + outer
    uses = []
    for bit in range(local_levels - grow):
        uses.append((lane == (inner >> (bit + 1)) * trials + outer) & (inner >> bit & 1 == 1))
    on, off = jnp.ones(square, jnp.bfloat16), jnp.zeros(square, jnp.bfloat16)
    ones = jnp.concatenate(
        [jnp.concatenate([on, off], axis=1), jnp.concatenate([off, on], axis=1)], axis=0
    )

    for copy in copies[1:]:
        copy.wait()
    tail = jnp.zeros(square, jnp.int32)
    for bit, use in enumerate(uses):
        tail = tail + jnp.where(use, ld_ref[grow + bit : grow + bit + 1, :], 0)
    parts = [tail] + [jnp.where(pick, ld_ref[m : m + 1, :], 0) for m in range(grow)]
    parts = [part.astype(jnp.float32).astype(jnp.bfloat16) for part in parts]
    rest = bp_ref[...]
    for _ in range(3):
        part = rest.astype(jnp.bfloat16).astype(jnp.float32)
        rest = rest - part
        parts.append(jnp.where(pick, part, 0.0).astype(jnp.bfloat16))
    parts += [off] * (len(parts) % 2)
    pairs = [jnp.concatenate(parts[i : i + 2], axis=1) for i in range(0, len(parts), 2)]
    spread = jnp.dot(jnp.concatenate(pairs, axis=0), ones, preferred_element_type=jnp.float32)
    spread = [
        spread[i // 2 * rows : (i // 2 + 1) * rows, i % 2 * LANES : (i % 2 + 1) * LANES]
        for i in range(len(parts))
    ]
    tail_delays = spread[0].astype(jnp.int32)
    delays = [spread[m + 1].astype(jnp.int32) for m in range(grow)]
    gain = (spread[grow + 1] + spread[grow + 2] + spread[grow + 3]) * (1.0 / WINDOW)

    whole = span // LANES
    start_blocks = blocks_of(span + 2 * HALF)
    copies[0].wait()
    for block in range(start_blocks):
        low, high = max(block - 1, 0), min(block + 1, whole)
        part = band[(low - block + 1) * LANES : (high - block + 1) * LANES]
        level_ref[block * rows : (block + 1) * rows, :] = jnp.dot(
            fb_ref[:, low * LANES : high * LANES], part, preferred_element_type=jnp.float32
        )

    first_span = lax.axis_index("tm") == 0
    early = jnp.logical_and(iota((SUBLANES, LANES), 1) < HALF, first_span)
    bands = []
    for e in range(trials):
        scale = gain[e * SUBLANES : (e + 1) * SUBLANES]
        tiles = []
        for block in range(start_blocks):
            tile = level_ref[pl.ds(block * rows + e, SUBLANES, stride=trials), :] * scale
            tiles.append(jnp.where(early, 0.0, tile) if block == 0 else tile)
        bands.append(tiles)
    plane = [bands]
    for m in range(grow):
        count = blocks_of(span + 2 * HALF + (m + 1) * shift_max)
        old, plane = plane, []
        for c in range(2):
            for i, held in enumerate(old):
                j = c * len(old) + i
                new = []
                for e in range(len(held) // 2):
                    at_row = (e * 2 * len(old) + j) * SUBLANES
                    moved = later(held[2 * e + 1], delays[m][at_row : at_row + SUBLANES], count)
                    base = held[2 * e]
                    new.append([base[b] + moved[b] if b < len(base) else moved[b] for b in range(count)])
                plane.append(new)
    count = blocks_of(span + HALF + local_levels * shift_max) + 1
    zero = jnp.zeros((SUBLANES, LANES), jnp.float32)
    for j in range(trials):
        shift = tail_delays[j * SUBLANES : (j + 1) * SUBLANES] + (LANES - HALF)
        moved = later(plane[j][0], shift, count, far=True)
        level_ref[pl.ds(j, SUBLANES, stride=trials), :] = folded(moved + [zero] * (SUBLANES - count))
    lower_rows = row_half(cd_ref.shape[0]) == 0
    for block in range(count):
        rows0 = level_ref[block * trials : block * trials + SUBLANES, :]
        rows1 = level_ref[block * trials + SUBLANES : (block + 1) * trials, :]
        keep_ref[block * SUBLANES : (block + 1) * SUBLANES, :] = jnp.where(lower_rows, rows0, rows1)
        send_ref[block * SUBLANES : (block + 1) * SUBLANES, :] = jnp.where(lower_rows, rows1, rows0)
    eye = iota((trials, trials), 0) == iota((trials, trials), 1)
    for l in range(cd_ref.shape[0]):
        step = jnp.sum(jnp.where(eye, cd_ref[l : l + 1, :].astype(jnp.float32), 0.0), axis=1, keepdims=True)
        step = jnp.where(lower_rows, step[:SUBLANES], step[SUBLANES:])
        step = jnp.broadcast_to(step, (SUBLANES, LANES)).astype(jnp.int32)
        steps_ref[l * SUBLANES : (l + 1) * SUBLANES, :] = step


def row_half(cross_levels):
    half = lax.axis_index("tm")
    for level in range(cross_levels):
        half = half ^ (lax.axis_index("sub") >> level & 1)
    return half


def tile_of(ref, block):
    return ref[block * SUBLANES : (block + 1) * SUBLANES, :]


def join_kernel(past, keep_ref, there_ref, out_ref):
    first_span = lax.axis_index("tm") == 0
    held = keep_ref.shape[0] // SUBLANES
    for block in range(out_ref.shape[0] // SUBLANES):
        new = None
        if block + 1 < held:
            new = jnp.where(first_span, tile_of(keep_ref, block + 1), tile_of(there_ref, block + 1))
        if block >= past - 1:
            at = block - past + 1
            other = jnp.where(first_span, tile_of(there_ref, at), tile_of(keep_ref, at))
            new = other if new is None else new + other
        out_ref[block * SUBLANES : (block + 1) * SUBLANES, :] = new


def merge_kernel(level, scale, own_ref, there_ref, steps_ref, out_ref, send_ref=None):
    is_upper = lax.axis_index("sub") >> level & 1 == 1
    blocks = own_ref.shape[0] // SUBLANES
    lower, upper = [], []
    for block in range(blocks):
        own, there = tile_of(own_ref, block), tile_of(there_ref, block)
        lower.append(jnp.where(is_upper, there, own))
        upper.append(jnp.where(is_upper, own, there))
    moved = later(upper, tile_of(steps_ref, level), blocks)
    new = [a + b for a, b in zip(lower, moved)]
    if scale is None:
        for block in range(blocks):
            out_ref[block * SUBLANES : (block + 1) * SUBLANES, :] = new[block]
        return
    first_span = lax.axis_index("tm") == 0
    past = blocks // 2
    for block in range(past):
        early, late = new[block] * scale, new[block + past] * scale
        out_ref[block * SUBLANES : (block + 1) * SUBLANES, :] = jnp.where(first_span, early, late)
        send_ref[block * SUBLANES : (block + 1) * SUBLANES, :] = jnp.where(first_span, late, early)


def last_kernel(cross_levels, keep_ref, there_ref, out_ref):
    lower_rows = row_half(cross_levels) == 0
    for block in range(keep_ref.shape[0] // SUBLANES):
        keep, there = tile_of(keep_ref, block), tile_of(there_ref, block)
        cols = slice(block * LANES, (block + 1) * LANES)
        out_ref[:SUBLANES, cols] = jnp.where(lower_rows, keep, there)
        out_ref[SUBLANES:, cols] = jnp.where(lower_rows, there, keep)


def shards(filterbank, bandpass, local_delays, cross_delays):
    rows, span = filterbank.shape
    cross_levels, trials = cross_delays.shape
    subs, spans = lax.axis_size("sub"), lax.axis_size("tm")
    local_levels = local_delays.shape[0]
    shift_max = span // 16
    past = span // LANES
    held = blocks_of(span + HALF + local_levels * shift_max) + 1
    assert rows == LANES == trials * SUBLANES and trials == 2 * SUBLANES
    assert spans == 2 and held <= SUBLANES

    vmem = pl.BlockSpec(memory_space=pltpu.VMEM)
    tiled = lambda count, kind=jnp.float32: jax.ShapeDtypeStruct((count * SUBLANES, LANES), kind)
    small = pltpu.CompilerParams(vmem_limit_bytes=1 << 20)
    call = functools.partial(pl.pallas_call, compiler_params=small)
    args = (filterbank, bandpass[None, :], local_delays, cross_delays)
    start_rows = rows * blocks_of(span + 2 * HALF)
    keep, send, steps = pl.pallas_call(
        functools.partial(plane_kernel, shift_max),
        out_shape=(tiled(held), tiled(held), tiled(cross_levels, jnp.int32)),
        in_specs=[pl.BlockSpec(memory_space=pltpu.HBM)] * len(args),
        out_specs=(vmem,) * 3,
        scratch_shapes=[pltpu.VMEM((start_rows, LANES), jnp.float32)]
        + [pltpu.VMEM(a.shape, a.dtype) for a in args]
        + [pltpu.SemaphoreType.DMA((len(args),))],
        compiler_params=pltpu.CompilerParams(vmem_limit_bytes=4 << 20),
    )(*[pltpu.with_memory_space_constraint(a, pltpu.HBM) for a in args])
    swap = [(0, 1), (1, 0)]
    there = lax.ppermute(send, "tm", swap)
    plane = call(
        functools.partial(join_kernel, past),
        out_shape=tiled(spans * past),
        in_specs=[vmem] * 2,
        out_specs=vmem,
    )(keep, there)
    for level in range(cross_levels):
        last = level == cross_levels - 1
        mask = spans << level | 1
        there = lax.ppermute(plane, ("sub", "tm"), [(i, i ^ mask) for i in range(subs * spans)])
        scale = 1.0 / math.sqrt(rows * subs) if last else None
        plane = call(
            functools.partial(merge_kernel, level, scale),
            out_shape=(tiled(past),) * 2 if last else tiled(spans * past),
            in_specs=[vmem] * 3,
            out_specs=(vmem,) * 2 if last else vmem,
        )(plane, there, steps)
    keep, send = plane
    return call(
        functools.partial(last_kernel, cross_levels),
        out_shape=jax.ShapeDtypeStruct((trials, span), jnp.float32),
        in_specs=[vmem] * 2,
        out_specs=vmem,
    )(keep, lax.ppermute(send, "tm", swap))


def solution(mesh):
    return jax.shard_map(
        shards,
        mesh=mesh,
        in_specs=(P(("beam", "sub"), "tm"), P(("beam", "sub")), P(None, "sub"), P(None, "sub")),
        out_specs=P(("beam", "sub"), "tm"),
        check_vma=False,
    )
```

```python
import functools
import math

import jax
import jax.numpy as jnp
from jax import lax
from jax.experimental import pallas as pl
from jax.experimental.pallas import tpu as pltpu
from jax.sharding import PartitionSpec as P

LANES = 128
SUBLANES = 8
WINDOW = 31
HALF = WINDOW // 2


def iota(shape, axis):
    return lax.broadcasted_iota(jnp.int32, shape, axis)


def turned(x, index, axis):
    return jnp.take_along_axis(x, index, axis=axis, mode="promise_in_bounds")


def blocks_of(columns):
    return -(-columns // LANES)


def later(tiles, shift, count):
    source = iota(shift.shape, 1) - shift
    index = source & (LANES - 1)
    zero = jnp.zeros(shift.shape, jnp.float32)
    spun = [zero] + [turned(tile, index, 1) for tile in tiles]
    return [jnp.where(source >= 0, spun[b + 1], spun[b]) for b in range(count)]


def folded(tiles):
    row = iota(tiles[0].shape, 0)
    reach = SUBLANES // 2
    while reach:
        first = row & reach == 0
        tiles = [
            jnp.where(
                first,
                a + pltpu.roll(a, SUBLANES - reach, 0),
                b + pltpu.roll(b, reach, 0),
            )
            for a, b in zip(tiles[:reach], tiles[reach:])
        ]
        reach //= 2
    return tiles[0]


def table_kernel(*refs):
    fb_ref, *sources = refs[:4]
    own_ref, shifts_ref, gain_ref, steps_ref, band_ref = refs[4:9]
    held, sems = refs[9:12], refs[12]
    copies = [
        pltpu.make_async_copy(a, b, sems.at[i])
        for i, (a, b) in enumerate(zip([*sources, fb_ref], [*held, own_ref]))
    ]
    for copy in copies:
        copy.start()
    bp_ref, ld_ref, cd_ref = held
    rows = own_ref.shape[0]
    local_levels = ld_ref.shape[0]
    cross_levels, trials = cd_ref.shape
    grow = trials.bit_length() - 1
    square = (rows, LANES)
    lane, row = iota(square, 1), iota(square, 0)
    inner, outer = row & (SUBLANES - 1), row >> 3

    at, to = iota(band_ref.shape, 0) - LANES, iota(band_ref.shape, 1)
    band = jnp.where(at == to, float(WINDOW), 0.0) - jnp.where(jnp.abs(at - to) <= HALF, 1.0, 0.0)
    band_ref[...] = band.astype(jnp.bfloat16)
    pick = lane == inner * trials + outer
    uses = []
    for bit in range(local_levels - grow):
        uses.append((lane == (inner >> (bit + 1)) * trials + outer) & (inner >> bit & 1 == 1))
    on, off = jnp.ones(square, jnp.bfloat16), jnp.zeros(square, jnp.bfloat16)
    ones = jnp.concatenate(
        [jnp.concatenate([on, off], axis=1), jnp.concatenate([off, on], axis=1)], axis=0
    )

    for copy in copies[:-1]:
        copy.wait()
    tail = jnp.zeros(square, jnp.int32)
    for bit, use in enumerate(uses):
        tail = tail + jnp.where(use, ld_ref[grow + bit : grow + bit + 1, :], 0)
    parts = [jnp.where(pick, ld_ref[m : m + 1, :], 0) for m in range(grow)] + [tail]
    parts = [part.astype(jnp.float32).astype(jnp.bfloat16) for part in parts]
    rest = bp_ref[...]
    for _ in range(3):
        part = rest.astype(jnp.bfloat16).astype(jnp.float32)
        rest = rest - part
        parts.append(jnp.where(pick, part, 0.0).astype(jnp.bfloat16))
    parts += [off] * (len(parts) % 2)
    pairs = [jnp.concatenate(parts[i : i + 2], axis=1) for i in range(0, len(parts), 2)]
    spread = jnp.dot(jnp.concatenate(pairs, axis=0), ones, preferred_element_type=jnp.float32)
    spread = [
        spread[i // 2 * rows : (i // 2 + 1) * rows, i % 2 * LANES : (i % 2 + 1) * LANES]
        for i in range(len(parts))
    ]
    lower_rows = row_half(cross_levels) == 0
    half = rows // 2
    for m in range(grow - 1):
        shifts_ref[m * rows : (m + 1) * rows, :] = spread[m].astype(jnp.int32)
    for i, part in enumerate(spread[grow - 1 : grow + 1]):
        kept = jnp.where(lower_rows, part[:half], part[half:])
        start = (grow - 1) * rows + i * half
        shifts_ref[start : start + half, :] = kept.astype(jnp.int32)
    gain_ref[...] = (spread[grow + 1] + spread[grow + 2] + spread[grow + 3]) * (1.0 / WINDOW)
    eye = iota((trials, trials), 0) == iota((trials, trials), 1)
    for l in range(cross_levels):
        step = jnp.sum(jnp.where(eye, cd_ref[l : l + 1, :].astype(jnp.float32), 0.0), axis=1, keepdims=True)
        step = jnp.where(lower_rows, step[:SUBLANES], step[SUBLANES:])
        step = jnp.broadcast_to(step, (SUBLANES, LANES)).astype(jnp.int32)
        steps_ref[l * SUBLANES : (l + 1) * SUBLANES, :] = step
    copies[-1].wait()


def plane_kernel(trials, own_ref, other_ref, shifts_ref, gain_ref, band_ref, out_ref, whole_ref, level_ref):
    rows, span = own_ref.shape
    grow = trials.bit_length() - 1
    columns = whole_ref.shape[1]
    blocks = columns // LANES
    first_span = lax.axis_index("tm") == 0

    @pl.when(first_span)
    def _():
        whole_ref[:, :span] = own_ref[...]
        whole_ref[:, span:] = other_ref[...]

    @pl.when(jnp.logical_not(first_span))
    def _():
        whole_ref[:, :span] = other_ref[...]
        whole_ref[:, span:] = own_ref[...]

    for block in range(0, blocks, 2):
        low, high = max(block - 1, 0), min(block + 3, blocks)
        part = band_ref[(low - block + 1) * LANES : (high - block + 1) * LANES, :]
        got = jnp.dot(
            whole_ref[:, low * LANES : high * LANES], part, preferred_element_type=jnp.float32
        )
        level_ref[block * rows : (block + 1) * rows, :] = got[:, :LANES]
        level_ref[(block + 1) * rows : (block + 2) * rows, :] = got[:, LANES:]

    bands = []
    for e in range(trials):
        scale = gain_ref[e * SUBLANES : (e + 1) * SUBLANES, :]
        bands.append(
            [level_ref[pl.ds(block * rows + e, SUBLANES, stride=trials), :] * scale for block in range(blocks)]
        )
    plane = [bands]

    def merged(low, high, at_row):
        moved = later(high, shifts_ref[at_row : at_row + SUBLANES, :], blocks)
        return [a + b for a, b in zip(low, moved)]

    for m in range(grow - 1):
        old, plane = plane, []
        for c in range(2):
            for i, held in enumerate(old):
                j = c * len(old) + i
                starts = [m * rows + (e * 2 * len(old) + j) * SUBLANES for e in range(len(held) // 2)]
                plane.append([merged(held[2 * e], held[2 * e + 1], start) for e, start in enumerate(starts)])
    for j, held in enumerate(plane):
        at_row = (grow - 1) * rows + j * SUBLANES
        new = merged(held[0], held[1], at_row)
        at_row += rows // 2
        moved = later(new, shifts_ref[at_row : at_row + SUBLANES, :], blocks)
        out_ref[pl.ds(j, SUBLANES, stride=SUBLANES), :] = folded(moved)


def row_half(cross_levels):
    half = lax.axis_index("tm")
    for level in range(cross_levels):
        half = half ^ (lax.axis_index("sub") >> level & 1)
    return half


def tile_of(ref, block):
    return ref[block * SUBLANES : (block + 1) * SUBLANES, :]


def merge_kernel(level, scale, own_ref, there_ref, steps_ref, out_ref, send_ref=None):
    is_upper = lax.axis_index("sub") >> level & 1 == 1
    blocks = own_ref.shape[0] // SUBLANES
    lower, upper = [], []
    for block in range(blocks):
        own, there = tile_of(own_ref, block), tile_of(there_ref, block)
        lower.append(jnp.where(is_upper, there, own))
        upper.append(jnp.where(is_upper, own, there))
    moved = later(upper, tile_of(steps_ref, level), blocks)
    new = [a + b for a, b in zip(lower, moved)]
    if scale is None:
        for block in range(blocks):
            out_ref[block * SUBLANES : (block + 1) * SUBLANES, :] = new[block]
        return
    first_span = lax.axis_index("tm") == 0
    past = blocks // 2
    for block in range(past):
        early, late = new[block] * scale, new[block + past] * scale
        out_ref[block * SUBLANES : (block + 1) * SUBLANES, :] = jnp.where(first_span, early, late)
        send_ref[block * SUBLANES : (block + 1) * SUBLANES, :] = jnp.where(first_span, late, early)


def last_kernel(cross_levels, keep_ref, there_ref, out_ref):
    lower_rows = row_half(cross_levels) == 0
    for block in range(keep_ref.shape[0] // SUBLANES):
        keep, there = tile_of(keep_ref, block), tile_of(there_ref, block)
        cols = slice(block * LANES, (block + 1) * LANES)
        out_ref[:SUBLANES, cols] = jnp.where(lower_rows, keep, there)
        out_ref[SUBLANES:, cols] = jnp.where(lower_rows, there, keep)


def shards(filterbank, bandpass, local_delays, cross_delays):
    rows, span = filterbank.shape
    cross_levels, trials = cross_delays.shape
    subs, spans = lax.axis_size("sub"), lax.axis_size("tm")
    local_levels = local_delays.shape[0]
    shift_max = span // 16
    grow = trials.bit_length() - 1
    past = span // LANES
    assert rows == LANES == trials * SUBLANES and trials == 2 * SUBLANES
    assert spans * past == SUBLANES and (local_levels - grow) * shift_max < LANES

    vmem = pl.BlockSpec(memory_space=pltpu.VMEM)
    tiled = lambda count, kind=jnp.float32: jax.ShapeDtypeStruct((count * SUBLANES, LANES), kind)
    room = lambda size: pltpu.CompilerParams(vmem_limit_bytes=size << 20)
    call = functools.partial(pl.pallas_call, compiler_params=room(1))
    swap = [(0, 1), (1, 0)]
    other = lax.ppermute(filterbank, "tm", swap)
    args = (filterbank, bandpass[None, :], local_delays, cross_delays)
    own, shifts, gain, steps, band = pl.pallas_call(
        table_kernel,
        out_shape=(
            jax.ShapeDtypeStruct(filterbank.shape, filterbank.dtype),
            tiled(grow * trials, jnp.int32),
            tiled(trials),
            tiled(cross_levels, jnp.int32),
            jax.ShapeDtypeStruct((4 * LANES, 2 * LANES), jnp.bfloat16),
        ),
        in_specs=[pl.BlockSpec(memory_space=pltpu.HBM)] * len(args),
        out_specs=(vmem,) * 5,
        scratch_shapes=[pltpu.VMEM(a.shape, a.dtype) for a in args[1:]]
        + [pltpu.SemaphoreType.DMA((len(args),))],
        compiler_params=room(4),
    )(*[pltpu.with_memory_space_constraint(a, pltpu.HBM) for a in args])
    plane = pl.pallas_call(
        functools.partial(plane_kernel, trials),
        out_shape=tiled(spans * past),
        in_specs=[vmem] * 5,
        out_specs=vmem,
        scratch_shapes=[
            pltpu.VMEM((rows, spans * span), filterbank.dtype),
            pltpu.VMEM((rows * spans * past, LANES), jnp.float32),
        ],
        compiler_params=room(6),
    )(own, other, shifts, gain, band)
    for level in range(cross_levels):
        last = level == cross_levels - 1
        mask = spans << level | 1
        there = lax.ppermute(plane, ("sub", "tm"), [(i, i ^ mask) for i in range(subs * spans)])
        scale = 1.0 / math.sqrt(rows * subs) if last else None
        plane = call(
            functools.partial(merge_kernel, level, scale),
            out_shape=(tiled(past),) * 2 if last else tiled(spans * past),
            in_specs=[vmem] * 3,
            out_specs=(vmem,) * 2 if last else vmem,
        )(plane, there, steps)
    keep, send = plane
    return call(
        functools.partial(last_kernel, cross_levels),
        out_shape=jax.ShapeDtypeStruct((trials, span), jnp.float32),
        in_specs=[vmem] * 2,
        out_specs=vmem,
    )(keep, lax.ppermute(send, "tm", swap))


def solution(mesh):
    return jax.shard_map(
        shards,
        mesh=mesh,
        in_specs=(P(("beam", "sub"), "tm"), P(("beam", "sub")), P(None, "sub"), P(None, "sub")),
        out_specs=P(("beam", "sub"), "tm"),
        check_vma=False,
    )
```

```python
import functools
import math

import jax
import jax.numpy as jnp
from jax import lax
from jax.experimental import pallas as pl
from jax.experimental.pallas import tpu as pltpu
from jax.sharding import PartitionSpec as P

LANES = 128
SUBLANES = 8
WINDOW = 31
HALF = WINDOW // 2


def iota(shape, axis):
    return lax.broadcasted_iota(jnp.int32, shape, axis)


def turned(x, index, axis):
    return jnp.take_along_axis(x, index, axis=axis, mode="promise_in_bounds")


def blocks_of(columns):
    return -(-columns // LANES)


def later(tiles, shift, count):
    source = iota(shift.shape, 1) - shift
    index = source & (LANES - 1)
    zero = jnp.zeros(shift.shape, jnp.float32)
    spun = [zero] + [turned(tile, index, 1) for tile in tiles]
    return [jnp.where(source >= 0, spun[b + 1], spun[b]) for b in range(count)]


def folded(tiles):
    row = iota(tiles[0].shape, 0)
    reach = SUBLANES // 2
    while reach:
        first = row & reach == 0
        tiles = [
            jnp.where(
                first,
                a + pltpu.roll(a, SUBLANES - reach, 0),
                b + pltpu.roll(b, reach, 0),
            )
            for a, b in zip(tiles[:reach], tiles[reach:])
        ]
        reach //= 2
    return tiles[0]


def table_kernel(*refs):
    fb_ref, *sources = refs[:4]
    own_ref, shifts_ref, gain_ref, steps_ref, band_ref = refs[4:9]
    held, sems = refs[9:12], refs[12]
    copies = [
        pltpu.make_async_copy(a, b, sems.at[i])
        for i, (a, b) in enumerate(zip([*sources, fb_ref], [*held, own_ref]))
    ]
    for copy in copies:
        copy.start()
    bp_ref, ld_ref, cd_ref = held
    rows = own_ref.shape[0]
    local_levels = ld_ref.shape[0]
    cross_levels, trials = cd_ref.shape
    grow = trials.bit_length() - 1
    square = (rows, LANES)
    lane, row = iota(square, 1), iota(square, 0)
    inner, outer = row & (SUBLANES - 1), row >> 3

    at, to = iota(band_ref.shape, 0) - LANES, iota(band_ref.shape, 1)
    band = jnp.where(at == to, float(WINDOW), 0.0) - jnp.where(jnp.abs(at - to) <= HALF, 1.0, 0.0)
    band_ref[...] = band.astype(jnp.bfloat16)
    pick = lane == inner * trials + outer
    uses = []
    for bit in range(local_levels - grow):
        uses.append((lane == (inner >> (bit + 1)) * trials + outer) & (inner >> bit & 1 == 1))
    on, off = jnp.ones(square, jnp.bfloat16), jnp.zeros(square, jnp.bfloat16)
    ones = jnp.concatenate(
        [jnp.concatenate([on, off], axis=1), jnp.concatenate([off, on], axis=1)], axis=0
    )

    for copy in copies[:-1]:
        copy.wait()
    tail = jnp.zeros(square, jnp.int32)
    for bit, use in enumerate(uses):
        tail = tail + jnp.where(use, ld_ref[grow + bit : grow + bit + 1, :], 0)
    parts = [jnp.where(pick, ld_ref[m : m + 1, :], 0) for m in range(grow)] + [tail]
    parts = [part.astype(jnp.float32).astype(jnp.bfloat16) for part in parts]
    rest = bp_ref[...]
    for _ in range(3):
        part = rest.astype(jnp.bfloat16).astype(jnp.float32)
        rest = rest - part
        parts.append(jnp.where(pick, part, 0.0).astype(jnp.bfloat16))
    parts += [off] * (len(parts) % 2)
    pairs = [jnp.concatenate(parts[i : i + 2], axis=1) for i in range(0, len(parts), 2)]
    spread = jnp.dot(jnp.concatenate(pairs, axis=0), ones, preferred_element_type=jnp.float32)
    spread = [
        spread[i // 2 * rows : (i // 2 + 1) * rows, i % 2 * LANES : (i % 2 + 1) * LANES]
        for i in range(len(parts))
    ]
    lower_rows = row_half(cross_levels) == 0
    half = rows // 2
    for m in range(grow - 1):
        shifts_ref[m * rows : (m + 1) * rows, :] = spread[m].astype(jnp.int32)
    for i, part in enumerate(spread[grow - 1 : grow + 1]):
        kept = jnp.where(lower_rows, part[:half], part[half:])
        start = (grow - 1) * rows + i * half
        shifts_ref[start : start + half, :] = kept.astype(jnp.int32)
    gain_ref[...] = (spread[grow + 1] + spread[grow + 2] + spread[grow + 3]) * (1.0 / WINDOW)
    eye = iota((trials, trials), 0) == iota((trials, trials), 1)
    for l in range(cross_levels):
        step = jnp.sum(jnp.where(eye, cd_ref[l : l + 1, :].astype(jnp.float32), 0.0), axis=1, keepdims=True)
        step = jnp.where(lower_rows, step[:SUBLANES], step[SUBLANES:])
        step = jnp.broadcast_to(step, (SUBLANES, LANES)).astype(jnp.int32)
        steps_ref[l * SUBLANES : (l + 1) * SUBLANES, :] = step
    copies[-1].wait()


def plane_kernel(trials, own_ref, other_ref, shifts_ref, gain_ref, band_ref, out_ref, whole_ref, level_ref):
    rows, span = own_ref.shape
    grow = trials.bit_length() - 1
    blocks = whole_ref.shape[1] // LANES - 2
    first_span = lax.axis_index("tm") == 0
    early = slice(LANES, LANES + span)
    late = slice(LANES + span, LANES + 2 * span)
    none = jnp.zeros((rows, LANES), own_ref.dtype)
    whole_ref[:, :LANES] = none
    whole_ref[:, LANES + 2 * span :] = none

    @pl.when(first_span)
    def _():
        whole_ref[:, early] = own_ref[...]
        whole_ref[:, late] = other_ref[...]

    @pl.when(jnp.logical_not(first_span))
    def _():
        whole_ref[:, early] = other_ref[...]
        whole_ref[:, late] = own_ref[...]

    about = [whole_ref[:, block * LANES : (block + 4) * LANES] for block in range(0, blocks, 2)]
    got = jnp.dot(jnp.concatenate(about, axis=0), band_ref[...], preferred_element_type=jnp.float32)
    for block in range(0, blocks, 2):
        part = got[block // 2 * rows : (block // 2 + 1) * rows]
        level_ref[block * rows : (block + 1) * rows, :] = part[:, :LANES]
        level_ref[(block + 1) * rows : (block + 2) * rows, :] = part[:, LANES:]

    bands = []
    for e in range(trials):
        scale = gain_ref[e * SUBLANES : (e + 1) * SUBLANES, :]
        bands.append(
            [level_ref[pl.ds(block * rows + e, SUBLANES, stride=trials), :] * scale for block in range(blocks)]
        )
    plane = [bands]

    def merged(low, high, at_row):
        moved = later(high, shifts_ref[at_row : at_row + SUBLANES, :], blocks)
        return [a + b for a, b in zip(low, moved)]

    for m in range(grow - 1):
        old, plane = plane, []
        for c in range(2):
            for i, held in enumerate(old):
                j = c * len(old) + i
                starts = [m * rows + (e * 2 * len(old) + j) * SUBLANES for e in range(len(held) // 2)]
                plane.append([merged(held[2 * e], held[2 * e + 1], start) for e, start in enumerate(starts)])
    for j, held in enumerate(plane):
        at_row = (grow - 1) * rows + j * SUBLANES
        new = merged(held[0], held[1], at_row)
        at_row += rows // 2
        moved = later(new, shifts_ref[at_row : at_row + SUBLANES, :], blocks)
        out_ref[pl.ds(j, SUBLANES, stride=SUBLANES), :] = folded(moved)


def row_half(cross_levels):
    half = lax.axis_index("tm")
    for level in range(cross_levels):
        half = half ^ (lax.axis_index("sub") >> level & 1)
    return half


def tile_of(ref, block):
    return ref[block * SUBLANES : (block + 1) * SUBLANES, :]


def merge_kernel(level, scale, own_ref, there_ref, steps_ref, out_ref, send_ref=None):
    is_upper = lax.axis_index("sub") >> level & 1 == 1
    blocks = own_ref.shape[0] // SUBLANES
    lower, upper = [], []
    for block in range(blocks):
        own, there = tile_of(own_ref, block), tile_of(there_ref, block)
        lower.append(jnp.where(is_upper, there, own))
        upper.append(jnp.where(is_upper, own, there))
    moved = later(upper, tile_of(steps_ref, level), blocks)
    new = [a + b for a, b in zip(lower, moved)]
    if scale is None:
        for block in range(blocks):
            out_ref[block * SUBLANES : (block + 1) * SUBLANES, :] = new[block]
        return
    first_span = lax.axis_index("tm") == 0
    past = blocks // 2
    for block in range(past):
        early, late = new[block] * scale, new[block + past] * scale
        out_ref[block * SUBLANES : (block + 1) * SUBLANES, :] = jnp.where(first_span, early, late)
        send_ref[block * SUBLANES : (block + 1) * SUBLANES, :] = jnp.where(first_span, late, early)


def last_kernel(cross_levels, keep_ref, there_ref, out_ref):
    lower_rows = row_half(cross_levels) == 0
    for block in range(keep_ref.shape[0] // SUBLANES):
        keep, there = tile_of(keep_ref, block), tile_of(there_ref, block)
        cols = slice(block * LANES, (block + 1) * LANES)
        out_ref[:SUBLANES, cols] = jnp.where(lower_rows, keep, there)
        out_ref[SUBLANES:, cols] = jnp.where(lower_rows, there, keep)


def shards(filterbank, bandpass, local_delays, cross_delays):
    rows, span = filterbank.shape
    cross_levels, trials = cross_delays.shape
    subs, spans = lax.axis_size("sub"), lax.axis_size("tm")
    local_levels = local_delays.shape[0]
    shift_max = span // 16
    grow = trials.bit_length() - 1
    past = span // LANES
    assert rows == LANES == trials * SUBLANES and trials == 2 * SUBLANES
    assert spans * past == SUBLANES and (local_levels - grow) * shift_max < LANES

    vmem = pl.BlockSpec(memory_space=pltpu.VMEM)
    tiled = lambda count, kind=jnp.float32: jax.ShapeDtypeStruct((count * SUBLANES, LANES), kind)
    room = lambda size: pltpu.CompilerParams(vmem_limit_bytes=size << 20)
    call = functools.partial(pl.pallas_call, compiler_params=room(1))
    swap = [(0, 1), (1, 0)]
    other = lax.ppermute(filterbank, "tm", swap)
    args = (filterbank, bandpass[None, :], local_delays, cross_delays)
    own, shifts, gain, steps, band = pl.pallas_call(
        table_kernel,
        out_shape=(
            jax.ShapeDtypeStruct(filterbank.shape, filterbank.dtype),
            tiled(grow * trials, jnp.int32),
            tiled(trials),
            tiled(cross_levels, jnp.int32),
            jax.ShapeDtypeStruct((4 * LANES, 2 * LANES), jnp.bfloat16),
        ),
        in_specs=[pl.BlockSpec(memory_space=pltpu.HBM)] * len(args),
        out_specs=(vmem,) * 5,
        scratch_shapes=[pltpu.VMEM(a.shape, a.dtype) for a in args[1:]]
        + [pltpu.SemaphoreType.DMA((len(args),))],
        compiler_params=room(4),
    )(*[pltpu.with_memory_space_constraint(a, pltpu.HBM) for a in args])
    plane = pl.pallas_call(
        functools.partial(plane_kernel, trials),
        out_shape=tiled(spans * past),
        in_specs=[vmem] * 5,
        out_specs=vmem,
        scratch_shapes=[
            pltpu.VMEM((rows, spans * span + 2 * LANES), filterbank.dtype),
            pltpu.VMEM((rows * spans * past, LANES), jnp.float32),
        ],
        compiler_params=room(6),
    )(own, other, shifts, gain, band)
    for level in range(cross_levels):
        last = level == cross_levels - 1
        mask = spans << level | 1
        there = lax.ppermute(plane, ("sub", "tm"), [(i, i ^ mask) for i in range(subs * spans)])
        scale = 1.0 / math.sqrt(rows * subs) if last else None
        plane = call(
            functools.partial(merge_kernel, level, scale),
            out_shape=(tiled(past),) * 2 if last else tiled(spans * past),
            in_specs=[vmem] * 3,
            out_specs=(vmem,) * 2 if last else vmem,
        )(plane, there, steps)
    keep, send = plane
    return call(
        functools.partial(last_kernel, cross_levels),
        out_shape=jax.ShapeDtypeStruct((trials, span), jnp.float32),
        in_specs=[vmem] * 2,
        out_specs=vmem,
    )(keep, lax.ppermute(send, "tm", swap))


def solution(mesh):
    return jax.shard_map(
        shards,
        mesh=mesh,
        in_specs=(P(("beam", "sub"), "tm"), P(("beam", "sub")), P(None, "sub"), P(None, "sub")),
        out_specs=P(("beam", "sub"), "tm"),
        check_vma=False,
    )
```

```python
import functools
import math

import jax
import jax.numpy as jnp
from jax import lax
from jax.experimental import pallas as pl
from jax.experimental.pallas import tpu as pltpu
from jax.sharding import PartitionSpec as P

LANES = 128
SUBLANES = 8
WINDOW = 31
HALF = WINDOW // 2


def iota(shape, axis):
    return lax.broadcasted_iota(jnp.int32, shape, axis)


def turned(x, index, axis):
    return jnp.take_along_axis(x, index, axis=axis, mode="promise_in_bounds")


def blocks_of(columns):
    return -(-columns // LANES)


def later(tiles, shift, count):
    source = iota(shift.shape, 1) - shift
    index = source & (LANES - 1)
    zero = jnp.zeros(shift.shape, jnp.float32)
    spun = [zero] + [turned(tile, index, 1) for tile in tiles]
    return [jnp.where(source >= 0, spun[b + 1], spun[b]) for b in range(count)]


def folded(tiles):
    row = iota(tiles[0].shape, 0)
    reach = SUBLANES // 2
    while reach:
        first = row & reach == 0
        tiles = [
            jnp.where(
                first,
                a + pltpu.roll(a, SUBLANES - reach, 0),
                b + pltpu.roll(b, reach, 0),
            )
            for a, b in zip(tiles[:reach], tiles[reach:])
        ]
        reach //= 2
    return tiles[0]


def table_kernel(*refs):
    fb_ref, *sources = refs[:4]
    own_ref, shifts_ref, gain_ref, steps_ref, band_ref = refs[4:9]
    held, sems = refs[9:12], refs[12]
    copies = [
        pltpu.make_async_copy(a, b, sems.at[i])
        for i, (a, b) in enumerate(zip([*sources, fb_ref], [*held, own_ref]))
    ]
    for copy in copies:
        copy.start()
    bp_ref, ld_ref, cd_ref = held
    rows = own_ref.shape[0]
    local_levels = ld_ref.shape[0]
    cross_levels, trials = cd_ref.shape
    grow = trials.bit_length() - 1
    parity = row_half(cross_levels)
    square = (rows, LANES)
    lane, row = iota(square, 1), iota(square, 0)
    inner, outer = row & (SUBLANES - 1), row >> 3
    half = (rows // 2, LANES)
    lane_h, row_h = iota(half, 1), iota(half, 0)
    inner_h, outer_h = row_h & (SUBLANES - 1), (row_h >> 3) * 2 + parity

    at, to = iota(band_ref.shape, 0) - LANES, iota(band_ref.shape, 1)
    band = jnp.where(at == to, float(WINDOW), 0.0) - jnp.where(jnp.abs(at - to) <= HALF, 1.0, 0.0)
    band_ref[...] = band.astype(jnp.bfloat16)
    pick = lane == inner * trials + outer
    pick_h = lane_h == inner_h * trials + outer_h
    uses = []
    for bit in range(local_levels - grow):
        uses.append((lane_h == (inner_h >> (bit + 1)) * trials + outer_h) & (inner_h >> bit & 1 == 1))
    on, off = jnp.ones((LANES, LANES), jnp.bfloat16), jnp.zeros((LANES, LANES), jnp.bfloat16)
    ones = jnp.concatenate(
        [jnp.concatenate([on, off], axis=1), jnp.concatenate([off, on], axis=1)], axis=0
    )

    for copy in copies[:-1]:
        copy.wait()
    tail = jnp.zeros(half, jnp.int32)
    for bit, use in enumerate(uses):
        tail = tail + jnp.where(use, ld_ref[grow + bit : grow + bit + 1, :], 0)
    parts = [jnp.where(pick_h, ld_ref[m : m + 1, :], 0) for m in range(grow)]
    parts += [tail] + [jnp.zeros(half, jnp.int32)] * ((grow + 1) % 2)
    parts = [part.astype(jnp.float32).astype(jnp.bfloat16) for part in parts]
    pieces = [jnp.concatenate(parts[i : i + 2], axis=0) for i in range(0, len(parts), 2)]
    rest = bp_ref[...]
    for _ in range(3):
        part = rest.astype(jnp.bfloat16).astype(jnp.float32)
        rest = rest - part
        pieces.append(jnp.where(pick, part, 0.0).astype(jnp.bfloat16))
    pieces += [off] * (len(pieces) % 2)
    pairs = [jnp.concatenate(pieces[i : i + 2], axis=1) for i in range(0, len(pieces), 2)]
    spread = jnp.dot(jnp.concatenate(pairs, axis=0), ones, preferred_element_type=jnp.float32)
    spread = [
        spread[i // 2 * rows : (i // 2 + 1) * rows, i % 2 * LANES : (i % 2 + 1) * LANES]
        for i in range(len(pieces))
    ]
    count = len(parts) // 2
    for i in range(count):
        shifts_ref[i * rows : (i + 1) * rows, :] = spread[i].astype(jnp.int32)
    gain_ref[...] = (spread[count] + spread[count + 1] + spread[count + 2]) * (1.0 / WINDOW)
    kept = (SUBLANES, trials)
    kept = iota(kept, 1) == iota(kept, 0) * 2 + parity
    for l in range(cross_levels):
        step = jnp.sum(jnp.where(kept, cd_ref[l : l + 1, :].astype(jnp.float32), 0.0), axis=1, keepdims=True)
        step = jnp.broadcast_to(step, (SUBLANES, LANES)).astype(jnp.int32)
        steps_ref[l * SUBLANES : (l + 1) * SUBLANES, :] = step
    copies[-1].wait()


def plane_kernel(trials, own_ref, other_ref, shifts_ref, gain_ref, band_ref, out_ref, whole_ref, level_ref):
    rows, span = own_ref.shape
    grow = trials.bit_length() - 1
    columns = whole_ref.shape[1]
    blocks = columns // LANES
    first_span = lax.axis_index("tm") == 0

    @pl.when(first_span)
    def _():
        whole_ref[:, :span] = own_ref[...]
        whole_ref[:, span:] = other_ref[...]

    @pl.when(jnp.logical_not(first_span))
    def _():
        whole_ref[:, :span] = other_ref[...]
        whole_ref[:, span:] = own_ref[...]

    for block in range(0, blocks, 2):
        low, high = max(block - 1, 0), min(block + 3, blocks)
        part = band_ref[(low - block + 1) * LANES : (high - block + 1) * LANES, :]
        got = jnp.dot(
            whole_ref[:, low * LANES : high * LANES], part, preferred_element_type=jnp.float32
        )
        level_ref[block * rows : (block + 1) * rows, :] = got[:, :LANES]
        level_ref[(block + 1) * rows : (block + 2) * rows, :] = got[:, LANES:]

    bands = []
    for e in range(trials):
        scale = gain_ref[e * SUBLANES : (e + 1) * SUBLANES, :]
        bands.append(
            [level_ref[pl.ds(block * rows + e, SUBLANES, stride=trials), :] * scale for block in range(blocks)]
        )
    plane = [bands]

    def merged(low, high, at_row):
        moved = later(high, shifts_ref[at_row : at_row + SUBLANES, :], blocks)
        return [a + b for a, b in zip(low, moved)]

    for m in range(grow):
        old, plane = plane, []
        for c in range(2 if m else 1):
            for i, held in enumerate(old):
                j = c * len(old) + i
                starts = [m * rows // 2 + ((e << m) + j) * SUBLANES for e in range(len(held) // 2)]
                plane.append([merged(held[2 * e], held[2 * e + 1], start) for e, start in enumerate(starts)])
    for j, held in enumerate(plane):
        at_row = grow * rows // 2 + j * SUBLANES
        moved = later(held[0], shifts_ref[at_row : at_row + SUBLANES, :], blocks)
        out_ref[pl.ds(j, SUBLANES, stride=SUBLANES), :] = folded(moved)


def row_half(cross_levels):
    half = lax.axis_index("tm")
    for level in range(cross_levels):
        half = half ^ (lax.axis_index("sub") >> level & 1)
    return half


def tile_of(ref, block):
    return ref[block * SUBLANES : (block + 1) * SUBLANES, :]


def merge_kernel(level, scale, own_ref, there_ref, steps_ref, out_ref, send_ref=None):
    is_upper = lax.axis_index("sub") >> level & 1 == 1
    blocks = own_ref.shape[0] // SUBLANES
    lower, upper = [], []
    for block in range(blocks):
        own, there = tile_of(own_ref, block), tile_of(there_ref, block)
        lower.append(jnp.where(is_upper, there, own))
        upper.append(jnp.where(is_upper, own, there))
    moved = later(upper, tile_of(steps_ref, level), blocks)
    new = [a + b for a, b in zip(lower, moved)]
    if scale is None:
        for block in range(blocks):
            out_ref[block * SUBLANES : (block + 1) * SUBLANES, :] = new[block]
        return
    first_span = lax.axis_index("tm") == 0
    past = blocks // 2
    for block in range(past):
        early, late = new[block] * scale, new[block + past] * scale
        out_ref[block * SUBLANES : (block + 1) * SUBLANES, :] = jnp.where(first_span, early, late)
        send_ref[block * SUBLANES : (block + 1) * SUBLANES, :] = jnp.where(first_span, late, early)


def last_kernel(cross_levels, keep_ref, there_ref, out_ref):
    is_even = row_half(cross_levels) == 0
    row = iota((SUBLANES, LANES), 0)
    for block in range(keep_ref.shape[0] // SUBLANES):
        keep, there = tile_of(keep_ref, block), tile_of(there_ref, block)
        even, odd = jnp.where(is_even, keep, there), jnp.where(is_even, there, keep)
        for part in range(2):
            source = (row >> 1) + part * (SUBLANES // 2)
            new = jnp.where(row & 1 == 0, turned(even, source, 0), turned(odd, source, 0))
            out_ref[part * SUBLANES : (part + 1) * SUBLANES, block * LANES : (block + 1) * LANES] = new


def shards(filterbank, bandpass, local_delays, cross_delays):
    rows, span = filterbank.shape
    cross_levels, trials = cross_delays.shape
    subs, spans = lax.axis_size("sub"), lax.axis_size("tm")
    local_levels = local_delays.shape[0]
    shift_max = span // 16
    grow = trials.bit_length() - 1
    past = span // LANES
    assert rows == LANES == trials * SUBLANES and trials == 2 * SUBLANES
    assert spans * past == SUBLANES and (local_levels - grow) * shift_max < LANES

    vmem = pl.BlockSpec(memory_space=pltpu.VMEM)
    tiled = lambda count, kind=jnp.float32: jax.ShapeDtypeStruct((count * SUBLANES, LANES), kind)
    room = lambda size: pltpu.CompilerParams(vmem_limit_bytes=size << 20)
    call = functools.partial(pl.pallas_call, compiler_params=room(1))
    swap = [(0, 1), (1, 0)]
    other = lax.ppermute(filterbank, "tm", swap)
    args = (filterbank, bandpass[None, :], local_delays, cross_delays)
    own, shifts, gain, steps, band = pl.pallas_call(
        table_kernel,
        out_shape=(
            jax.ShapeDtypeStruct(filterbank.shape, filterbank.dtype),
            tiled((grow + 2) // 2 * trials, jnp.int32),
            tiled(trials),
            tiled(cross_levels, jnp.int32),
            jax.ShapeDtypeStruct((4 * LANES, 2 * LANES), jnp.bfloat16),
        ),
        in_specs=[pl.BlockSpec(memory_space=pltpu.HBM)] * len(args),
        out_specs=(vmem,) * 5,
        scratch_shapes=[pltpu.VMEM(a.shape, a.dtype) for a in args[1:]]
        + [pltpu.SemaphoreType.DMA((len(args),))],
        compiler_params=room(4),
    )(*[pltpu.with_memory_space_constraint(a, pltpu.HBM) for a in args])
    plane = pl.pallas_call(
        functools.partial(plane_kernel, trials),
        out_shape=tiled(spans * past),
        in_specs=[vmem] * 5,
        out_specs=vmem,
        scratch_shapes=[
            pltpu.VMEM((rows, spans * span), filterbank.dtype),
            pltpu.VMEM((rows * spans * past, LANES), jnp.float32),
        ],
        compiler_params=room(6),
    )(own, other, shifts, gain, band)
    for level in range(cross_levels):
        last = level == cross_levels - 1
        mask = spans << level | 1
        there = lax.ppermute(plane, ("sub", "tm"), [(i, i ^ mask) for i in range(subs * spans)])
        scale = 1.0 / math.sqrt(rows * subs) if last else None
        plane = call(
            functools.partial(merge_kernel, level, scale),
            out_shape=(tiled(past),) * 2 if last else tiled(spans * past),
            in_specs=[vmem] * 3,
            out_specs=(vmem,) * 2 if last else vmem,
        )(plane, there, steps)
    keep, send = plane
    return call(
        functools.partial(last_kernel, cross_levels),
        out_shape=jax.ShapeDtypeStruct((trials, span), jnp.float32),
        in_specs=[vmem] * 2,
        out_specs=vmem,
    )(keep, lax.ppermute(send, "tm", swap))


def solution(mesh):
    return jax.shard_map(
        shards,
        mesh=mesh,
        in_specs=(P(("beam", "sub"), "tm"), P(("beam", "sub")), P(None, "sub"), P(None, "sub")),
        out_specs=P(("beam", "sub"), "tm"),
        check_vma=False,
    )
```

```python
import functools
import math

import jax
import jax.numpy as jnp
from jax import lax
from jax.experimental import pallas as pl
from jax.experimental.pallas import tpu as pltpu
from jax.sharding import PartitionSpec as P

LANES = 128
SUBLANES = 8
WINDOW = 31
HALF = WINDOW // 2
CODE_TOP = 32000.0


def iota(shape, axis):
    return lax.broadcasted_iota(jnp.int32, shape, axis)


def turned(x, index, axis):
    return jnp.take_along_axis(x, index, axis=axis, mode="promise_in_bounds")


def blocks_of(columns):
    return -(-columns // LANES)


def later(tiles, shift, count):
    source = iota(shift.shape, 1) - shift
    index = source & (LANES - 1)
    zero = jnp.zeros(shift.shape, jnp.float32)
    spun = [zero] + [turned(tile, index, 1) for tile in tiles]
    return [jnp.where(source >= 0, spun[b + 1], spun[b]) for b in range(count)]


def folded(tiles):
    row = iota(tiles[0].shape, 0)
    reach = SUBLANES // 2
    while reach:
        first = row & reach == 0
        tiles = [
            jnp.where(
                first,
                a + pltpu.roll(a, SUBLANES - reach, 0),
                b + pltpu.roll(b, reach, 0),
            )
            for a, b in zip(tiles[:reach], tiles[reach:])
        ]
        reach //= 2
    return tiles[0]


def table_kernel(*refs):
    fb_ref, *sources = refs[:4]
    own_ref, shifts_ref, gain_ref, steps_ref, band_ref = refs[4:9]
    held, sems = refs[9:12], refs[12]
    copies = [
        pltpu.make_async_copy(a, b, sems.at[i])
        for i, (a, b) in enumerate(zip([*sources, fb_ref], [*held, own_ref]))
    ]
    for copy in copies:
        copy.start()
    bp_ref, ld_ref, cd_ref = held
    rows = own_ref.shape[0]
    local_levels = ld_ref.shape[0]
    cross_levels, trials = cd_ref.shape
    grow = trials.bit_length() - 1
    parity = row_half(cross_levels)
    square = (rows, LANES)
    lane, row = iota(square, 1), iota(square, 0)
    inner, outer = row & (SUBLANES - 1), row >> 3
    half = (rows // 2, LANES)
    lane_h, row_h = iota(half, 1), iota(half, 0)
    inner_h, outer_h = row_h & (SUBLANES - 1), (row_h >> 3) * 2 + parity

    at, to = iota(band_ref.shape, 0) - LANES, iota(band_ref.shape, 1)
    band = jnp.where(at == to, float(WINDOW), 0.0) - jnp.where(jnp.abs(at - to) <= HALF, 1.0, 0.0)
    band_ref[...] = band.astype(jnp.bfloat16)
    pick = lane == inner * trials + outer
    pick_h = lane_h == inner_h * trials + outer_h
    uses = []
    for bit in range(local_levels - grow):
        uses.append((lane_h == (inner_h >> (bit + 1)) * trials + outer_h) & (inner_h >> bit & 1 == 1))
    on, off = jnp.ones((LANES, LANES), jnp.bfloat16), jnp.zeros((LANES, LANES), jnp.bfloat16)
    ones = jnp.concatenate(
        [jnp.concatenate([on, off], axis=1), jnp.concatenate([off, on], axis=1)], axis=0
    )

    for copy in copies[:-1]:
        copy.wait()
    tail = jnp.zeros(half, jnp.int32)
    for bit, use in enumerate(uses):
        tail = tail + jnp.where(use, ld_ref[grow + bit : grow + bit + 1, :], 0)
    parts = [jnp.where(pick_h, ld_ref[m : m + 1, :], 0) for m in range(grow)]
    parts += [tail] + [jnp.zeros(half, jnp.int32)] * ((grow + 1) % 2)
    parts = [part.astype(jnp.float32).astype(jnp.bfloat16) for part in parts]
    pieces = [jnp.concatenate(parts[i : i + 2], axis=0) for i in range(0, len(parts), 2)]
    rest = bp_ref[...]
    for _ in range(3):
        part = rest.astype(jnp.bfloat16).astype(jnp.float32)
        rest = rest - part
        pieces.append(jnp.where(pick, part, 0.0).astype(jnp.bfloat16))
    pieces += [off] * (len(pieces) % 2)
    pairs = [jnp.concatenate(pieces[i : i + 2], axis=1) for i in range(0, len(pieces), 2)]
    spread = jnp.dot(jnp.concatenate(pairs, axis=0), ones, preferred_element_type=jnp.float32)
    spread = [
        spread[i // 2 * rows : (i // 2 + 1) * rows, i % 2 * LANES : (i % 2 + 1) * LANES]
        for i in range(len(pieces))
    ]
    count = len(parts) // 2
    for i in range(count):
        shifts_ref[i * rows : (i + 1) * rows, :] = spread[i].astype(jnp.int32)
    gain_ref[...] = (spread[count] + spread[count + 1] + spread[count + 2]) * (1.0 / WINDOW)
    kept = (SUBLANES, trials)
    kept = iota(kept, 1) == iota(kept, 0) * 2 + parity
    for l in range(cross_levels):
        step = jnp.sum(jnp.where(kept, cd_ref[l : l + 1, :].astype(jnp.float32), 0.0), axis=1, keepdims=True)
        step = jnp.broadcast_to(step, (SUBLANES, LANES)).astype(jnp.int32)
        steps_ref[l * SUBLANES : (l + 1) * SUBLANES, :] = step
    copies[-1].wait()


def plane_kernel(trials, own_ref, other_ref, shifts_ref, gain_ref, band_ref, out_ref, whole_ref, level_ref):
    rows, span = own_ref.shape
    grow = trials.bit_length() - 1
    columns = whole_ref.shape[1]
    blocks = columns // LANES
    first_span = lax.axis_index("tm") == 0

    @pl.when(first_span)
    def _():
        whole_ref[:, :span] = own_ref[...]
        whole_ref[:, span:] = other_ref[...]

    @pl.when(jnp.logical_not(first_span))
    def _():
        whole_ref[:, :span] = other_ref[...]
        whole_ref[:, span:] = own_ref[...]

    for block in range(0, blocks, 2):
        low, high = max(block - 1, 0), min(block + 3, blocks)
        part = band_ref[(low - block + 1) * LANES : (high - block + 1) * LANES, :]
        got = jnp.dot(
            whole_ref[:, low * LANES : high * LANES], part, preferred_element_type=jnp.float32
        )
        level_ref[block * rows : (block + 1) * rows, :] = got[:, :LANES]
        level_ref[(block + 1) * rows : (block + 2) * rows, :] = got[:, LANES:]

    bands = []
    for e in range(trials):
        scale = gain_ref[e * SUBLANES : (e + 1) * SUBLANES, :]
        bands.append(
            [level_ref[pl.ds(block * rows + e, SUBLANES, stride=trials), :] * scale for block in range(blocks)]
        )
    plane = [bands]

    def merged(low, high, at_row):
        moved = later(high, shifts_ref[at_row : at_row + SUBLANES, :], blocks)
        return [a + b for a, b in zip(low, moved)]

    for m in range(grow):
        old, plane = plane, []
        for c in range(2 if m else 1):
            for i, held in enumerate(old):
                j = c * len(old) + i
                starts = [m * rows // 2 + ((e << m) + j) * SUBLANES for e in range(len(held) // 2)]
                plane.append([merged(held[2 * e], held[2 * e + 1], start) for e, start in enumerate(starts)])
    for j, held in enumerate(plane):
        at_row = grow * rows // 2 + j * SUBLANES
        moved = later(held[0], shifts_ref[at_row : at_row + SUBLANES, :], blocks)
        out_ref[pl.ds(j, SUBLANES, stride=SUBLANES), :] = folded(moved)


def row_half(cross_levels):
    half = lax.axis_index("tm")
    for level in range(cross_levels):
        half = half ^ (lax.axis_index("sub") >> level & 1)
    return half


def tile_of(ref, block):
    return ref[block * SUBLANES : (block + 1) * SUBLANES, :]


def coded(tile):
    top = jnp.max(jnp.abs(tile), axis=1, keepdims=True)
    exponent = jnp.ceil(jnp.log(jnp.maximum(top, 2.0**-100)) * (1.0 / math.log(2.0)))
    return jnp.round(tile * (jnp.exp2(-exponent) * CODE_TOP)).astype(jnp.int32), exponent.astype(jnp.int32)


def merge_kernel(level, scale, own_ref, there_ref, steps_ref, out_ref, send_ref=None):
    is_upper = lax.axis_index("sub") >> level & 1 == 1
    blocks = own_ref.shape[0] // SUBLANES
    pair = 2 * SUBLANES
    if there_ref.dtype == jnp.int16:
        exponents = there_ref[blocks * SUBLANES :, :].astype(jnp.int32)[:SUBLANES]
    lower, upper = [], []
    for block in range(blocks):
        own = tile_of(own_ref, block)
        if there_ref.dtype == jnp.int16:
            at_row = block // 2 * pair
            there = there_ref[at_row : at_row + pair, :].astype(jnp.int32)
            there = there[block % 2 * SUBLANES : (block % 2 + 1) * SUBLANES].astype(jnp.float32)
            exponent = turned(exponents, jnp.full(exponents.shape, block, jnp.int32), 1)
            there = there * (jnp.exp2(exponent.astype(jnp.float32)) * (1.0 / CODE_TOP))
        else:
            there = tile_of(there_ref, block)
        lower.append(jnp.where(is_upper, there, own))
        upper.append(jnp.where(is_upper, own, there))
    moved = later(upper, tile_of(steps_ref, level), blocks)
    new = [a + b for a, b in zip(lower, moved)]
    if scale is None:
        for block in range(blocks):
            out_ref[block * SUBLANES : (block + 1) * SUBLANES, :] = new[block]
        if send_ref is not None:
            lane = iota((SUBLANES, LANES), 1)
            notes = jnp.zeros((SUBLANES, LANES), jnp.int32)
            codes = []
            for block in range(blocks):
                code, exponent = coded(new[block])
                codes.append(code)
                notes = jnp.where(lane == block, exponent, notes)
            codes += [notes, notes]
            for i in range(0, len(codes), 2):
                both = jnp.concatenate(codes[i : i + 2], axis=0).astype(jnp.int16)
                send_ref[i * SUBLANES : (i + 2) * SUBLANES, :] = both
        return
    first_span = lax.axis_index("tm") == 0
    past = blocks // 2
    for block in range(past):
        early, late = new[block] * scale, new[block + past] * scale
        out_ref[block * SUBLANES : (block + 1) * SUBLANES, :] = jnp.where(first_span, early, late)
        send_ref[block * SUBLANES : (block + 1) * SUBLANES, :] = jnp.where(first_span, late, early)


def last_kernel(cross_levels, keep_ref, there_ref, out_ref):
    is_even = row_half(cross_levels) == 0
    row = iota((SUBLANES, LANES), 0)
    for block in range(keep_ref.shape[0] // SUBLANES):
        keep, there = tile_of(keep_ref, block), tile_of(there_ref, block)
        even, odd = jnp.where(is_even, keep, there), jnp.where(is_even, there, keep)
        for part in range(2):
            source = (row >> 1) + part * (SUBLANES // 2)
            new = jnp.where(row & 1 == 0, turned(even, source, 0), turned(odd, source, 0))
            out_ref[part * SUBLANES : (part + 1) * SUBLANES, block * LANES : (block + 1) * LANES] = new


def shards(filterbank, bandpass, local_delays, cross_delays):
    rows, span = filterbank.shape
    cross_levels, trials = cross_delays.shape
    subs, spans = lax.axis_size("sub"), lax.axis_size("tm")
    local_levels = local_delays.shape[0]
    shift_max = span // 16
    grow = trials.bit_length() - 1
    past = span // LANES
    assert rows == LANES == trials * SUBLANES and trials == 2 * SUBLANES
    assert spans * past == SUBLANES and (local_levels - grow) * shift_max < LANES

    vmem = pl.BlockSpec(memory_space=pltpu.VMEM)
    tiled = lambda count, kind=jnp.float32: jax.ShapeDtypeStruct((count * SUBLANES, LANES), kind)
    room = lambda size: pltpu.CompilerParams(vmem_limit_bytes=size << 20)
    call = functools.partial(pl.pallas_call, compiler_params=room(1))
    swap = [(0, 1), (1, 0)]
    other = lax.ppermute(filterbank, "tm", swap)
    args = (filterbank, bandpass[None, :], local_delays, cross_delays)
    own, shifts, gain, steps, band = pl.pallas_call(
        table_kernel,
        out_shape=(
            jax.ShapeDtypeStruct(filterbank.shape, filterbank.dtype),
            tiled((grow + 2) // 2 * trials, jnp.int32),
            tiled(trials),
            tiled(cross_levels, jnp.int32),
            jax.ShapeDtypeStruct((4 * LANES, 2 * LANES), jnp.bfloat16),
        ),
        in_specs=[pl.BlockSpec(memory_space=pltpu.HBM)] * len(args),
        out_specs=(vmem,) * 5,
        scratch_shapes=[pltpu.VMEM(a.shape, a.dtype) for a in args[1:]]
        + [pltpu.SemaphoreType.DMA((len(args),))],
        compiler_params=room(4),
    )(*[pltpu.with_memory_space_constraint(a, pltpu.HBM) for a in args])
    plane = pl.pallas_call(
        functools.partial(plane_kernel, trials),
        out_shape=tiled(spans * past),
        in_specs=[vmem] * 5,
        out_specs=vmem,
        scratch_shapes=[
            pltpu.VMEM((rows, spans * span), filterbank.dtype),
            pltpu.VMEM((rows * spans * past, LANES), jnp.float32),
        ],
        compiler_params=room(6),
    )(own, other, shifts, gain, band)
    sent = plane
    for level in range(cross_levels):
        mask = spans << level | 1
        there = lax.ppermute(sent, ("sub", "tm"), [(i, i ^ mask) for i in range(subs * spans)])
        scale, shapes = None, (tiled(spans * past),)
        if level == cross_levels - 2:
            shapes += (tiled(spans * past + 2, jnp.int16),)
        elif level == cross_levels - 1:
            scale, shapes = 1.0 / math.sqrt(rows * subs), (tiled(past),) * 2
        plane, *more = call(
            functools.partial(merge_kernel, level, scale),
            out_shape=shapes,
            in_specs=[vmem] * 3,
            out_specs=(vmem,) * len(shapes),
        )(plane, there, steps)
        sent = more[0] if more else plane
    keep, send = plane, sent
    return call(
        functools.partial(last_kernel, cross_levels),
        out_shape=jax.ShapeDtypeStruct((trials, span), jnp.float32),
        in_specs=[vmem] * 2,
        out_specs=vmem,
    )(keep, lax.ppermute(send, "tm", swap))


def solution(mesh):
    return jax.shard_map(
        shards,
        mesh=mesh,
        in_specs=(P(("beam", "sub"), "tm"), P(("beam", "sub")), P(None, "sub"), P(None, "sub")),
        out_specs=P(("beam", "sub"), "tm"),
        check_vma=False,
    )
```

```python
import functools
import math

import jax
import jax.numpy as jnp
from jax import lax
from jax.experimental import pallas as pl
from jax.experimental.pallas import tpu as pltpu
from jax.sharding import PartitionSpec as P

LANES = 128
SUBLANES = 8
WINDOW = 31
HALF = WINDOW // 2


def iota(shape, axis):
    return lax.broadcasted_iota(jnp.int32, shape, axis)


def turned(x, index, axis):
    return jnp.take_along_axis(x, index, axis=axis, mode="promise_in_bounds")


def blocks_of(columns):
    return -(-columns // LANES)


def later(tiles, shift, count):
    source = iota(shift.shape, 1) - shift
    index = source & (LANES - 1)
    zero = jnp.zeros(shift.shape, jnp.float32)
    spun = [zero] + [turned(tile, index, 1) for tile in tiles]
    return [jnp.where(source >= 0, spun[b + 1], spun[b]) for b in range(count)]


def folded(tiles):
    row = iota(tiles[0].shape, 0)
    reach = SUBLANES // 2
    while reach:
        first = row & reach == 0
        tiles = [
            jnp.where(
                first,
                a + pltpu.roll(a, SUBLANES - reach, 0),
                b + pltpu.roll(b, reach, 0),
            )
            for a, b in zip(tiles[:reach], tiles[reach:])
        ]
        reach //= 2
    return tiles[0]


def table_kernel(*refs):
    fb_ref, *sources = refs[:4]
    own_ref, own_level_ref, shifts_ref, gain_ref, steps_ref, band_ref = refs[4:10]
    held, sems = refs[10:13], refs[13]
    copies = [
        pltpu.make_async_copy(a, b, sems.at[i])
        for i, (a, b) in enumerate(zip([*sources, fb_ref], [*held, own_ref]))
    ]
    for copy in copies:
        copy.start()
    bp_ref, ld_ref, cd_ref = held
    rows = own_ref.shape[0]
    local_levels = ld_ref.shape[0]
    cross_levels, trials = cd_ref.shape
    grow = trials.bit_length() - 1
    parity = row_half(cross_levels)
    square = (rows, LANES)
    lane, row = iota(square, 1), iota(square, 0)
    inner, outer = row & (SUBLANES - 1), row >> 3
    half = (rows // 2, LANES)
    lane_h, row_h = iota(half, 1), iota(half, 0)
    inner_h, outer_h = row_h & (SUBLANES - 1), (row_h >> 3) * 2 + parity

    at, to = iota(band_ref.shape, 0) - LANES, iota(band_ref.shape, 1)
    band = jnp.where(at == to, float(WINDOW), 0.0) - jnp.where(jnp.abs(at - to) <= HALF, 1.0, 0.0)
    band_ref[...] = band.astype(jnp.bfloat16)
    pick = lane == inner * trials + outer
    pick_h = lane_h == inner_h * trials + outer_h
    uses = []
    for bit in range(local_levels - grow):
        uses.append((lane_h == (inner_h >> (bit + 1)) * trials + outer_h) & (inner_h >> bit & 1 == 1))
    on, off = jnp.ones((LANES, LANES), jnp.bfloat16), jnp.zeros((LANES, LANES), jnp.bfloat16)
    ones = jnp.concatenate(
        [jnp.concatenate([on, off], axis=1), jnp.concatenate([off, on], axis=1)], axis=0
    )

    for copy in copies[:-1]:
        copy.wait()
    tail = jnp.zeros(half, jnp.int32)
    for bit, use in enumerate(uses):
        tail = tail + jnp.where(use, ld_ref[grow + bit : grow + bit + 1, :], 0)
    parts = [jnp.where(pick_h, ld_ref[m : m + 1, :], 0) for m in range(grow)]
    parts += [tail] + [jnp.zeros(half, jnp.int32)] * ((grow + 1) % 2)
    parts = [part.astype(jnp.float32).astype(jnp.bfloat16) for part in parts]
    pieces = [jnp.concatenate(parts[i : i + 2], axis=0) for i in range(0, len(parts), 2)]
    rest = bp_ref[...]
    for _ in range(3):
        part = rest.astype(jnp.bfloat16).astype(jnp.float32)
        rest = rest - part
        pieces.append(jnp.where(pick, part, 0.0).astype(jnp.bfloat16))
    pieces += [off] * (len(pieces) % 2)
    pairs = [jnp.concatenate(pieces[i : i + 2], axis=1) for i in range(0, len(pieces), 2)]
    spread = jnp.dot(jnp.concatenate(pairs, axis=0), ones, preferred_element_type=jnp.float32)
    spread = [
        spread[i // 2 * rows : (i // 2 + 1) * rows, i % 2 * LANES : (i % 2 + 1) * LANES]
        for i in range(len(pieces))
    ]
    count = len(parts) // 2
    for i in range(count):
        shifts_ref[i * rows : (i + 1) * rows, :] = spread[i].astype(jnp.int32)
    gain_ref[...] = (spread[count] + spread[count + 1] + spread[count + 2]) * (1.0 / WINDOW)
    kept = (SUBLANES, trials)
    kept = iota(kept, 1) == iota(kept, 0) * 2 + parity
    for l in range(cross_levels):
        step = jnp.sum(jnp.where(kept, cd_ref[l : l + 1, :].astype(jnp.float32), 0.0), axis=1, keepdims=True)
        step = jnp.broadcast_to(step, (SUBLANES, LANES)).astype(jnp.int32)
        steps_ref[l * SUBLANES : (l + 1) * SUBLANES, :] = step
    copies[-1].wait()
    window_sums(own_ref, band_ref, own_level_ref)


def window_sums(samples_ref, band_ref, level_ref):
    rows = samples_ref.shape[0]
    blocks = samples_ref.shape[1] // LANES
    for block in range(0, blocks, 2):
        low, high = max(block - 1, 0), min(block + 3, blocks)
        part = band_ref[(low - block + 1) * LANES : (high - block + 1) * LANES, :]
        got = jnp.dot(
            samples_ref[:, low * LANES : high * LANES], part, preferred_element_type=jnp.float32
        )
        level_ref[block * rows : (block + 1) * rows, :] = got[:, :LANES]
        level_ref[(block + 1) * rows : (block + 2) * rows, :] = got[:, LANES:]


def plane_kernel(trials, *refs):
    own_ref, other_ref, own_level_ref, shifts_ref, gain_ref, band_ref = refs[:6]
    out_ref, other_level_ref, seam_ref = refs[6:]
    rows, span = own_ref.shape
    grow = trials.bit_length() - 1
    per_span = span // LANES
    blocks = 2 * per_span
    first_span = lax.axis_index("tm") == 0
    window_sums(other_ref, band_ref, other_level_ref)

    own_early, own_late = own_ref[:, span - LANES :], own_ref[:, :LANES]
    other_early, other_late = other_ref[:, span - LANES :], other_ref[:, :LANES]
    early = jnp.where(first_span, own_early, other_early)
    late = jnp.where(first_span, other_late, own_late)
    after, before = band_ref[3 * LANES :, LANES:], band_ref[:LANES, :LANES]
    seam_ref[:rows, :] = jnp.dot(late, after, preferred_element_type=jnp.float32)
    seam_ref[rows:, :] = jnp.dot(early, before, preferred_element_type=jnp.float32)

    bands = []
    for e in range(trials):
        scale = gain_ref[e * SUBLANES : (e + 1) * SUBLANES, :]
        rows_of = lambda ref, block: ref[pl.ds(block * rows + e, SUBLANES, stride=trials), :]
        own = [rows_of(own_level_ref, block) for block in range(per_span)]
        other = [rows_of(other_level_ref, block) for block in range(per_span)]
        tiles = [jnp.where(first_span, a, b) for a, b in zip(own, other)]
        tiles += [jnp.where(first_span, b, a) for a, b in zip(own, other)]
        tiles[per_span - 1] += rows_of(seam_ref, 0)
        tiles[per_span] += rows_of(seam_ref, 1)
        bands.append([tile * scale for tile in tiles])
    plane = [bands]

    def merged(low, high, at_row):
        moved = later(high, shifts_ref[at_row : at_row + SUBLANES, :], blocks)
        return [a + b for a, b in zip(low, moved)]

    for m in range(grow):
        old, plane = plane, []
        for c in range(2 if m else 1):
            for i, held in enumerate(old):
                j = c * len(old) + i
                starts = [m * rows // 2 + ((e << m) + j) * SUBLANES for e in range(len(held) // 2)]
                plane.append([merged(held[2 * e], held[2 * e + 1], start) for e, start in enumerate(starts)])
    for j, held in enumerate(plane):
        at_row = grow * rows // 2 + j * SUBLANES
        moved = later(held[0], shifts_ref[at_row : at_row + SUBLANES, :], blocks)
        out_ref[pl.ds(j, SUBLANES, stride=SUBLANES), :] = folded(moved)


def row_half(cross_levels):
    half = lax.axis_index("tm")
    for level in range(cross_levels):
        half = half ^ (lax.axis_index("sub") >> level & 1)
    return half


def tile_of(ref, block):
    return ref[block * SUBLANES : (block + 1) * SUBLANES, :]


def merge_kernel(level, scale, own_ref, there_ref, steps_ref, out_ref, send_ref=None):
    is_upper = lax.axis_index("sub") >> level & 1 == 1
    blocks = own_ref.shape[0] // SUBLANES
    lower, upper = [], []
    for block in range(blocks):
        own, there = tile_of(own_ref, block), tile_of(there_ref, block)
        lower.append(jnp.where(is_upper, there, own))
        upper.append(jnp.where(is_upper, own, there))
    moved = later(upper, tile_of(steps_ref, level), blocks)
    new = [a + b for a, b in zip(lower, moved)]
    if scale is None:
        for block in range(blocks):
            out_ref[block * SUBLANES : (block + 1) * SUBLANES, :] = new[block]
        return
    first_span = lax.axis_index("tm") == 0
    past = blocks // 2
    for block in range(past):
        early, late = new[block] * scale, new[block + past] * scale
        out_ref[block * SUBLANES : (block + 1) * SUBLANES, :] = jnp.where(first_span, early, late)
        send_ref[block * SUBLANES : (block + 1) * SUBLANES, :] = jnp.where(first_span, late, early)


def last_kernel(cross_levels, keep_ref, there_ref, out_ref):
    is_even = row_half(cross_levels) == 0
    row = iota((SUBLANES, LANES), 0)
    for block in range(keep_ref.shape[0] // SUBLANES):
        keep, there = tile_of(keep_ref, block), tile_of(there_ref, block)
        even, odd = jnp.where(is_even, keep, there), jnp.where(is_even, there, keep)
        for part in range(2):
            source = (row >> 1) + part * (SUBLANES // 2)
            new = jnp.where(row & 1 == 0, turned(even, source, 0), turned(odd, source, 0))
            out_ref[part * SUBLANES : (part + 1) * SUBLANES, block * LANES : (block + 1) * LANES] = new


def shards(filterbank, bandpass, local_delays, cross_delays):
    rows, span = filterbank.shape
    cross_levels, trials = cross_delays.shape
    subs, spans = lax.axis_size("sub"), lax.axis_size("tm")
    local_levels = local_delays.shape[0]
    shift_max = span // 16
    grow = trials.bit_length() - 1
    past = span // LANES
    assert rows == LANES == trials * SUBLANES and trials == 2 * SUBLANES
    assert spans * past == SUBLANES and (local_levels - grow) * shift_max < LANES

    vmem = pl.BlockSpec(memory_space=pltpu.VMEM)
    tiled = lambda count, kind=jnp.float32: jax.ShapeDtypeStruct((count * SUBLANES, LANES), kind)
    room = lambda size: pltpu.CompilerParams(vmem_limit_bytes=size << 20)
    call = functools.partial(pl.pallas_call, compiler_params=room(1))
    swap = [(0, 1), (1, 0)]
    other = lax.ppermute(filterbank, "tm", swap)
    args = (filterbank, bandpass[None, :], local_delays, cross_delays)
    own, own_level, shifts, gain, steps, band = pl.pallas_call(
        table_kernel,
        out_shape=(
            jax.ShapeDtypeStruct(filterbank.shape, filterbank.dtype),
            tiled(past * trials),
            tiled((grow + 2) // 2 * trials, jnp.int32),
            tiled(trials),
            tiled(cross_levels, jnp.int32),
            jax.ShapeDtypeStruct((4 * LANES, 2 * LANES), jnp.bfloat16),
        ),
        in_specs=[pl.BlockSpec(memory_space=pltpu.HBM)] * len(args),
        out_specs=(vmem,) * 6,
        scratch_shapes=[pltpu.VMEM(a.shape, a.dtype) for a in args[1:]]
        + [pltpu.SemaphoreType.DMA((len(args),))],
        compiler_params=room(4),
    )(*[pltpu.with_memory_space_constraint(a, pltpu.HBM) for a in args])
    plane = pl.pallas_call(
        functools.partial(plane_kernel, trials),
        out_shape=tiled(spans * past),
        in_specs=[vmem] * 6,
        out_specs=vmem,
        scratch_shapes=[
            pltpu.VMEM((rows * past, LANES), jnp.float32),
            pltpu.VMEM((rows * 2, LANES), jnp.float32),
        ],
        compiler_params=room(6),
    )(own, other, own_level, shifts, gain, band)
    for level in range(cross_levels):
        last = level == cross_levels - 1
        mask = spans << level | 1
        there = lax.ppermute(plane, ("sub", "tm"), [(i, i ^ mask) for i in range(subs * spans)])
        scale = 1.0 / math.sqrt(rows * subs) if last else None
        plane = call(
            functools.partial(merge_kernel, level, scale),
            out_shape=(tiled(past),) * 2 if last else tiled(spans * past),
            in_specs=[vmem] * 3,
            out_specs=(vmem,) * 2 if last else vmem,
        )(plane, there, steps)
    keep, send = plane
    return call(
        functools.partial(last_kernel, cross_levels),
        out_shape=jax.ShapeDtypeStruct((trials, span), jnp.float32),
        in_specs=[vmem] * 2,
        out_specs=vmem,
    )(keep, lax.ppermute(send, "tm", swap))


def solution(mesh):
    return jax.shard_map(
        shards,
        mesh=mesh,
        in_specs=(P(("beam", "sub"), "tm"), P(("beam", "sub")), P(None, "sub"), P(None, "sub")),
        out_specs=P(("beam", "sub"), "tm"),
        check_vma=False,
    )
```

```python
import functools
import math

import jax
import jax.numpy as jnp
from jax import lax
from jax.experimental import pallas as pl
from jax.experimental.pallas import tpu as pltpu
from jax.sharding import PartitionSpec as P

LANES = 128
SUBLANES = 8
WINDOW = 31
HALF = WINDOW // 2


def iota(shape, axis):
    return lax.broadcasted_iota(jnp.int32, shape, axis)


def turned(x, index, axis):
    return jnp.take_along_axis(x, index, axis=axis, mode="promise_in_bounds")


def blocks_of(columns):
    return -(-columns // LANES)


def later(tiles, shift, count):
    source = iota(shift.shape, 1) - shift
    index = source & (LANES - 1)
    zero = jnp.zeros(shift.shape, jnp.float32)
    spun = [zero] + [turned(tile, index, 1) for tile in tiles]
    return [jnp.where(source >= 0, spun[b + 1], spun[b]) for b in range(count)]


def folded(tiles):
    row = iota(tiles[0].shape, 0)
    reach = SUBLANES // 2
    while reach:
        first = row & reach == 0
        tiles = [
            jnp.where(
                first,
                a + pltpu.roll(a, SUBLANES - reach, 0),
                b + pltpu.roll(b, reach, 0),
            )
            for a, b in zip(tiles[:reach], tiles[reach:])
        ]
        reach //= 2
    return tiles[0]


def table_kernel(*refs):
    fb_ref, *sources = refs[:4]
    own_ref, shifts_ref, gain_ref, steps_ref, band_ref = refs[4:9]
    held, sems = refs[9:12], refs[12]
    copies = [
        pltpu.make_async_copy(a, b, sems.at[i])
        for i, (a, b) in enumerate(zip([*sources, fb_ref], [*held, own_ref]))
    ]
    for copy in copies:
        copy.start()
    bp_ref, ld_ref, cd_ref = held
    rows = own_ref.shape[0]
    local_levels = ld_ref.shape[0]
    cross_levels, trials = cd_ref.shape
    grow = trials.bit_length() - 1
    parity = row_half(cross_levels)
    square = (rows, LANES)
    lane, row = iota(square, 1), iota(square, 0)
    inner, outer = row & (SUBLANES - 1), row >> 3
    half = (rows // 2, LANES)
    lane_h, row_h = iota(half, 1), iota(half, 0)
    inner_h, outer_h = row_h & (SUBLANES - 1), (row_h >> 3) * 2 + parity

    at, to = iota(band_ref.shape, 0) - LANES, iota(band_ref.shape, 1)
    band = jnp.where(at == to, float(WINDOW), 0.0) - jnp.where(jnp.abs(at - to) <= HALF, 1.0, 0.0)
    band_ref[...] = band.astype(jnp.bfloat16)
    pick = lane == inner * trials + outer
    pick_h = lane_h == inner_h * trials + outer_h
    uses = []
    for bit in range(local_levels - grow):
        uses.append((lane_h == (inner_h >> (bit + 1)) * trials + outer_h) & (inner_h >> bit & 1 == 1))
    on, off = jnp.ones((LANES, LANES), jnp.bfloat16), jnp.zeros((LANES, LANES), jnp.bfloat16)
    ones = jnp.concatenate(
        [jnp.concatenate([on, off], axis=1), jnp.concatenate([off, on], axis=1)], axis=0
    )

    for copy in copies[:-1]:
        copy.wait()
    tail = jnp.zeros(half, jnp.int32)
    for bit, use in enumerate(uses):
        tail = tail + jnp.where(use, ld_ref[grow + bit : grow + bit + 1, :], 0)
    parts = [jnp.where(pick_h, ld_ref[m : m + 1, :], 0) for m in range(grow)]
    parts += [tail] + [jnp.zeros(half, jnp.int32)] * ((grow + 1) % 2)
    parts = [part.astype(jnp.float32).astype(jnp.bfloat16) for part in parts]
    pieces = [jnp.concatenate(parts[i : i + 2], axis=0) for i in range(0, len(parts), 2)]
    rest = bp_ref[...]
    for _ in range(3):
        part = rest.astype(jnp.bfloat16).astype(jnp.float32)
        rest = rest - part
        pieces.append(jnp.where(pick, part, 0.0).astype(jnp.bfloat16))
    pieces += [off] * (len(pieces) % 2)
    pairs = [jnp.concatenate(pieces[i : i + 2], axis=1) for i in range(0, len(pieces), 2)]
    spread = jnp.dot(jnp.concatenate(pairs, axis=0), ones, preferred_element_type=jnp.float32)
    spread = [
        spread[i // 2 * rows : (i // 2 + 1) * rows, i % 2 * LANES : (i % 2 + 1) * LANES]
        for i in range(len(pieces))
    ]
    count = len(parts) // 2
    for i in range(count):
        shifts_ref[i * rows : (i + 1) * rows, :] = spread[i].astype(jnp.int32)
    gain_ref[...] = (spread[count] + spread[count + 1] + spread[count + 2]) * (1.0 / WINDOW)
    kept = (SUBLANES, trials)
    kept = iota(kept, 1) == iota(kept, 0) * 2 + parity
    for l in range(cross_levels):
        step = jnp.sum(jnp.where(kept, cd_ref[l : l + 1, :].astype(jnp.float32), 0.0), axis=1, keepdims=True)
        step = jnp.broadcast_to(step, (SUBLANES, LANES)).astype(jnp.int32)
        steps_ref[l * SUBLANES : (l + 1) * SUBLANES, :] = step
    copies[-1].wait()


def plane_kernel(trials, own_ref, other_ref, shifts_ref, gain_ref, band_ref, out_ref, whole_ref, level_ref):
    rows, span = own_ref.shape
    grow = trials.bit_length() - 1
    columns = whole_ref.shape[1]
    blocks = columns // LANES
    first_span = lax.axis_index("tm") == 0

    @pl.when(first_span)
    def _():
        whole_ref[:, :span] = own_ref[...]
        whole_ref[:, span:] = other_ref[...]

    @pl.when(jnp.logical_not(first_span))
    def _():
        whole_ref[:, :span] = other_ref[...]
        whole_ref[:, span:] = own_ref[...]

    carried = {}

    def moved(tiles, at_row):
        source = iota((SUBLANES, LANES), 1) - shifts_ref[at_row : at_row + SUBLANES, :]
        index = source & (LANES - 1)
        got = []
        for tile in tiles:
            spun = turned(tile, index, 1)
            prior = carried.get(at_row, jnp.zeros((SUBLANES, LANES), jnp.float32))
            got.append(jnp.where(source >= 0, spun, prior))
            carried[at_row] = spun
        return got

    ends = []
    for block in range(0, blocks, 2):
        low, high = max(block - 1, 0), min(block + 3, blocks)
        part = band_ref[(low - block + 1) * LANES : (high - block + 1) * LANES, :]
        got = jnp.dot(
            whole_ref[:, low * LANES : high * LANES], part, preferred_element_type=jnp.float32
        )
        level_ref[block * rows : (block + 1) * rows, :] = got[:, :LANES]
        level_ref[(block + 1) * rows : (block + 2) * rows, :] = got[:, LANES:]
        bands = []
        for e in range(trials):
            scale = gain_ref[e * SUBLANES : (e + 1) * SUBLANES, :]
            starts = [(block + k) * rows + e for k in range(2)]
            bands.append([level_ref[pl.ds(start, SUBLANES, stride=trials), :] * scale for start in starts])
        plane = [bands]
        for m in range(grow):
            old, plane = plane, []
            for c in range(2 if m else 1):
                for i, held in enumerate(old):
                    j = c * len(old) + i
                    new = []
                    for e in range(len(held) // 2):
                        high_tiles = moved(held[2 * e + 1], m * rows // 2 + ((e << m) + j) * SUBLANES)
                        new.append([x + y for x, y in zip(held[2 * e], high_tiles)])
                    plane.append(new)
        ends.append([moved(held[0], grow * rows // 2 + j * SUBLANES) for j, held in enumerate(plane)])
    for j in range(SUBLANES):
        out_ref[pl.ds(j, SUBLANES, stride=SUBLANES), :] = folded([tile for end in ends for tile in end[j]])


def row_half(cross_levels):
    half = lax.axis_index("tm")
    for level in range(cross_levels):
        half = half ^ (lax.axis_index("sub") >> level & 1)
    return half


def tile_of(ref, block):
    return ref[block * SUBLANES : (block + 1) * SUBLANES, :]


def merge_kernel(level, scale, own_ref, there_ref, steps_ref, out_ref, send_ref=None):
    is_upper = lax.axis_index("sub") >> level & 1 == 1
    blocks = own_ref.shape[0] // SUBLANES
    lower, upper = [], []
    for block in range(blocks):
        own, there = tile_of(own_ref, block), tile_of(there_ref, block)
        lower.append(jnp.where(is_upper, there, own))
        upper.append(jnp.where(is_upper, own, there))
    moved = later(upper, tile_of(steps_ref, level), blocks)
    new = [a + b for a, b in zip(lower, moved)]
    if scale is None:
        for block in range(blocks):
            out_ref[block * SUBLANES : (block + 1) * SUBLANES, :] = new[block]
        return
    first_span = lax.axis_index("tm") == 0
    past = blocks // 2
    for block in range(past):
        early, late = new[block] * scale, new[block + past] * scale
        out_ref[block * SUBLANES : (block + 1) * SUBLANES, :] = jnp.where(first_span, early, late)
        send_ref[block * SUBLANES : (block + 1) * SUBLANES, :] = jnp.where(first_span, late, early)


def last_kernel(cross_levels, keep_ref, there_ref, out_ref):
    is_even = row_half(cross_levels) == 0
    row = iota((SUBLANES, LANES), 0)
    for block in range(keep_ref.shape[0] // SUBLANES):
        keep, there = tile_of(keep_ref, block), tile_of(there_ref, block)
        even, odd = jnp.where(is_even, keep, there), jnp.where(is_even, there, keep)
        for part in range(2):
            source = (row >> 1) + part * (SUBLANES // 2)
            new = jnp.where(row & 1 == 0, turned(even, source, 0), turned(odd, source, 0))
            out_ref[part * SUBLANES : (part + 1) * SUBLANES, block * LANES : (block + 1) * LANES] = new


def shards(filterbank, bandpass, local_delays, cross_delays):
    rows, span = filterbank.shape
    cross_levels, trials = cross_delays.shape
    subs, spans = lax.axis_size("sub"), lax.axis_size("tm")
    local_levels = local_delays.shape[0]
    shift_max = span // 16
    grow = trials.bit_length() - 1
    past = span // LANES
    assert rows == LANES == trials * SUBLANES and trials == 2 * SUBLANES
    assert spans * past == SUBLANES and (local_levels - grow) * shift_max < LANES

    vmem = pl.BlockSpec(memory_space=pltpu.VMEM)
    tiled = lambda count, kind=jnp.float32: jax.ShapeDtypeStruct((count * SUBLANES, LANES), kind)
    room = lambda size: pltpu.CompilerParams(vmem_limit_bytes=size << 20)
    call = functools.partial(pl.pallas_call, compiler_params=room(1))
    swap = [(0, 1), (1, 0)]
    other = lax.ppermute(filterbank, "tm", swap)
    args = (filterbank, bandpass[None, :], local_delays, cross_delays)
    own, shifts, gain, steps, band = pl.pallas_call(
        table_kernel,
        out_shape=(
            jax.ShapeDtypeStruct(filterbank.shape, filterbank.dtype),
            tiled((grow + 2) // 2 * trials, jnp.int32),
            tiled(trials),
            tiled(cross_levels, jnp.int32),
            jax.ShapeDtypeStruct((4 * LANES, 2 * LANES), jnp.bfloat16),
        ),
        in_specs=[pl.BlockSpec(memory_space=pltpu.HBM)] * len(args),
        out_specs=(vmem,) * 5,
        scratch_shapes=[pltpu.VMEM(a.shape, a.dtype) for a in args[1:]]
        + [pltpu.SemaphoreType.DMA((len(args),))],
        compiler_params=room(4),
    )(*[pltpu.with_memory_space_constraint(a, pltpu.HBM) for a in args])
    plane = pl.pallas_call(
        functools.partial(plane_kernel, trials),
        out_shape=tiled(spans * past),
        in_specs=[vmem] * 5,
        out_specs=vmem,
        scratch_shapes=[
            pltpu.VMEM((rows, spans * span), filterbank.dtype),
            pltpu.VMEM((rows * spans * past, LANES), jnp.float32),
        ],
        compiler_params=room(6),
    )(own, other, shifts, gain, band)
    for level in range(cross_levels):
        last = level == cross_levels - 1
        mask = spans << level | 1
        there = lax.ppermute(plane, ("sub", "tm"), [(i, i ^ mask) for i in range(subs * spans)])
        scale = 1.0 / math.sqrt(rows * subs) if last else None
        plane = call(
            functools.partial(merge_kernel, level, scale),
            out_shape=(tiled(past),) * 2 if last else tiled(spans * past),
            in_specs=[vmem] * 3,
            out_specs=(vmem,) * 2 if last else vmem,
        )(plane, there, steps)
    keep, send = plane
    return call(
        functools.partial(last_kernel, cross_levels),
        out_shape=jax.ShapeDtypeStruct((trials, span), jnp.float32),
        in_specs=[vmem] * 2,
        out_specs=vmem,
    )(keep, lax.ppermute(send, "tm", swap))


def solution(mesh):
    return jax.shard_map(
        shards,
        mesh=mesh,
        in_specs=(P(("beam", "sub"), "tm"), P(("beam", "sub")), P(None, "sub"), P(None, "sub")),
        out_specs=P(("beam", "sub"), "tm"),
        check_vma=False,
    )
```

```python
import functools
import math

import jax
import jax.numpy as jnp
from jax import lax
from jax.experimental import pallas as pl
from jax.experimental.pallas import tpu as pltpu
from jax.sharding import PartitionSpec as P

LANES = 128
SUBLANES = 8
WINDOW = 31
HALF = WINDOW // 2


def iota(shape, axis):
    return lax.broadcasted_iota(jnp.int32, shape, axis)


def turned(x, index, axis):
    return jnp.take_along_axis(x, index, axis=axis, mode="promise_in_bounds")


def blocks_of(columns):
    return -(-columns // LANES)


def later(tiles, shift, count):
    source = iota(shift.shape, 1) - shift
    index = source & (LANES - 1)
    zero = jnp.zeros(shift.shape, jnp.float32)
    spun = [zero] + [turned(tile, index, 1) for tile in tiles]
    return [jnp.where(source >= 0, spun[b + 1], spun[b]) for b in range(count)]


def folded(tiles):
    row = iota(tiles[0].shape, 0)
    reach = SUBLANES // 2
    while reach:
        first = row & reach == 0
        tiles = [
            jnp.where(
                first,
                a + pltpu.roll(a, SUBLANES - reach, 0),
                b + pltpu.roll(b, reach, 0),
            )
            for a, b in zip(tiles[:reach], tiles[reach:])
        ]
        reach //= 2
    return tiles[0]


def table_kernel(*refs):
    fb_ref, *sources = refs[:4]
    own_ref, shifts_ref, gain_ref, steps_ref, band_ref = refs[4:9]
    held, sems = refs[9:12], refs[12]
    copies = [
        pltpu.make_async_copy(a, b, sems.at[i])
        for i, (a, b) in enumerate(zip([*sources, fb_ref], [*held, own_ref]))
    ]
    for copy in copies:
        copy.start()
    bp_ref, ld_ref, cd_ref = held
    rows = own_ref.shape[0]
    local_levels = ld_ref.shape[0]
    cross_levels, trials = cd_ref.shape
    grow = trials.bit_length() - 1
    parity = row_half(cross_levels)
    square = (rows, LANES)
    lane, row = iota(square, 1), iota(square, 0)
    inner, outer = row & (SUBLANES - 1), row >> 3
    half = (rows // 2, LANES)
    lane_h, row_h = iota(half, 1), iota(half, 0)
    inner_h, outer_h = row_h & (SUBLANES - 1), (row_h >> 3) * 2 + parity

    at, to = iota(band_ref.shape, 0) - LANES, iota(band_ref.shape, 1)
    band = jnp.where(at == to, float(WINDOW), 0.0) - jnp.where(jnp.abs(at - to) <= HALF, 1.0, 0.0)
    band_ref[...] = band.astype(jnp.bfloat16)
    pick = lane == inner * trials + outer
    pick_h = lane_h == inner_h * trials + outer_h
    uses = []
    for bit in range(local_levels - grow):
        uses.append((lane_h == (inner_h >> (bit + 1)) * trials + outer_h) & (inner_h >> bit & 1 == 1))
    on, off = jnp.ones((LANES, LANES), jnp.bfloat16), jnp.zeros((LANES, LANES), jnp.bfloat16)
    ones = jnp.concatenate(
        [jnp.concatenate([on, off], axis=1), jnp.concatenate([off, on], axis=1)], axis=0
    )

    for copy in copies[:-1]:
        copy.wait()
    tail = jnp.zeros(half, jnp.int32)
    for bit, use in enumerate(uses):
        tail = tail + jnp.where(use, ld_ref[grow + bit : grow + bit + 1, :], 0)
    parts = [jnp.where(pick_h, ld_ref[m : m + 1, :], 0) for m in range(grow)]
    parts += [tail] + [jnp.zeros(half, jnp.int32)] * ((grow + 1) % 2)
    parts = [part.astype(jnp.float32).astype(jnp.bfloat16) for part in parts]
    pieces = [jnp.concatenate(parts[i : i + 2], axis=0) for i in range(0, len(parts), 2)]
    rest = bp_ref[...]
    for _ in range(3):
        part = rest.astype(jnp.bfloat16).astype(jnp.float32)
        rest = rest - part
        pieces.append(jnp.where(pick, part, 0.0).astype(jnp.bfloat16))
    pieces += [off] * (len(pieces) % 2)
    pairs = [jnp.concatenate(pieces[i : i + 2], axis=1) for i in range(0, len(pieces), 2)]
    spread = jnp.dot(jnp.concatenate(pairs, axis=0), ones, preferred_element_type=jnp.float32)
    spread = [
        spread[i // 2 * rows : (i // 2 + 1) * rows, i % 2 * LANES : (i % 2 + 1) * LANES]
        for i in range(len(pieces))
    ]
    count = len(parts) // 2
    for i in range(count):
        shifts_ref[i * rows : (i + 1) * rows, :] = spread[i].astype(jnp.int32)
    gain_ref[...] = (spread[count] + spread[count + 1] + spread[count + 2]) * (1.0 / WINDOW)
    kept = (SUBLANES, trials)
    kept = iota(kept, 1) == iota(kept, 0) * 2 + parity
    for l in range(cross_levels):
        step = jnp.sum(jnp.where(kept, cd_ref[l : l + 1, :].astype(jnp.float32), 0.0), axis=1, keepdims=True)
        step = jnp.broadcast_to(step, (SUBLANES, LANES)).astype(jnp.int32)
        steps_ref[l * SUBLANES : (l + 1) * SUBLANES, :] = step
    copies[-1].wait()


def plane_kernel(trials, own_ref, other_ref, shifts_ref, gain_ref, band_ref, out_ref, whole_ref, level_ref):
    rows, span = own_ref.shape
    grow = trials.bit_length() - 1
    columns = whole_ref.shape[1]
    blocks = columns // LANES
    first_span = lax.axis_index("tm") == 0

    @pl.when(first_span)
    def _():
        whole_ref[:, :span] = own_ref[...]
        whole_ref[:, span:] = other_ref[...]

    @pl.when(jnp.logical_not(first_span))
    def _():
        whole_ref[:, :span] = other_ref[...]
        whole_ref[:, span:] = own_ref[...]

    for block in range(0, blocks, 2):
        low, high = max(block - 1, 0), min(block + 3, blocks)
        part = band_ref[(low - block + 1) * LANES : (high - block + 1) * LANES, :]
        got = jnp.dot(
            whole_ref[:, low * LANES : high * LANES], part, preferred_element_type=jnp.float32
        )
        level_ref[block * rows : (block + 1) * rows, :] = got[:, :LANES]
        level_ref[(block + 1) * rows : (block + 2) * rows, :] = got[:, LANES:]

    carried = {}

    def moved(tiles, at_row):
        source = iota((SUBLANES, LANES), 1) - shifts_ref[at_row : at_row + SUBLANES, :]
        index = source & (LANES - 1)
        got = []
        for tile in tiles:
            spun = turned(tile, index, 1)
            prior = carried.get(at_row, jnp.zeros((SUBLANES, LANES), jnp.float32))
            got.append(jnp.where(source >= 0, spun, prior))
            carried[at_row] = spun
        return got

    ends = []
    for block in range(0, blocks, 2):
        bands = []
        for e in range(trials):
            scale = gain_ref[e * SUBLANES : (e + 1) * SUBLANES, :]
            starts = [(block + k) * rows + e for k in range(2)]
            bands.append([level_ref[pl.ds(start, SUBLANES, stride=trials), :] * scale for start in starts])
        plane = [bands]
        for m in range(grow):
            old, plane = plane, []
            for c in range(2 if m else 1):
                for i, held in enumerate(old):
                    j = c * len(old) + i
                    new = []
                    for e in range(len(held) // 2):
                        high_tiles = moved(held[2 * e + 1], m * rows // 2 + ((e << m) + j) * SUBLANES)
                        new.append([x + y for x, y in zip(held[2 * e], high_tiles)])
                    plane.append(new)
        ends.append([moved(held[0], grow * rows // 2 + j * SUBLANES) for j, held in enumerate(plane)])
    for j in range(SUBLANES):
        out_ref[pl.ds(j, SUBLANES, stride=SUBLANES), :] = folded([tile for end in ends for tile in end[j]])


def row_half(cross_levels):
    half = lax.axis_index("tm")
    for level in range(cross_levels):
        half = half ^ (lax.axis_index("sub") >> level & 1)
    return half


def tile_of(ref, block):
    return ref[block * SUBLANES : (block + 1) * SUBLANES, :]


def merge_kernel(level, scale, own_ref, there_ref, steps_ref, out_ref, send_ref=None):
    is_upper = lax.axis_index("sub") >> level & 1 == 1
    blocks = own_ref.shape[0] // SUBLANES
    lower, upper = [], []
    for block in range(blocks):
        own, there = tile_of(own_ref, block), tile_of(there_ref, block)
        lower.append(jnp.where(is_upper, there, own))
        upper.append(jnp.where(is_upper, own, there))
    moved = later(upper, tile_of(steps_ref, level), blocks)
    new = [a + b for a, b in zip(lower, moved)]
    if scale is None:
        for block in range(blocks):
            out_ref[block * SUBLANES : (block + 1) * SUBLANES, :] = new[block]
        return
    first_span = lax.axis_index("tm") == 0
    past = blocks // 2
    for block in range(past):
        early, late = new[block] * scale, new[block + past] * scale
        out_ref[block * SUBLANES : (block + 1) * SUBLANES, :] = jnp.where(first_span, early, late)
        send_ref[block * SUBLANES : (block + 1) * SUBLANES, :] = jnp.where(first_span, late, early)


def last_kernel(cross_levels, keep_ref, there_ref, out_ref):
    is_even = row_half(cross_levels) == 0
    row = iota((SUBLANES, LANES), 0)
    for block in range(keep_ref.shape[0] // SUBLANES):
        keep, there = tile_of(keep_ref, block), tile_of(there_ref, block)
        even, odd = jnp.where(is_even, keep, there), jnp.where(is_even, there, keep)
        for part in range(2):
            source = (row >> 1) + part * (SUBLANES // 2)
            new = jnp.where(row & 1 == 0, turned(even, source, 0), turned(odd, source, 0))
            out_ref[part * SUBLANES : (part + 1) * SUBLANES, block * LANES : (block + 1) * LANES] = new


def shards(filterbank, bandpass, local_delays, cross_delays):
    rows, span = filterbank.shape
    cross_levels, trials = cross_delays.shape
    subs, spans = lax.axis_size("sub"), lax.axis_size("tm")
    local_levels = local_delays.shape[0]
    shift_max = span // 16
    grow = trials.bit_length() - 1
    past = span // LANES
    assert rows == LANES == trials * SUBLANES and trials == 2 * SUBLANES
    assert spans * past == SUBLANES and (local_levels - grow) * shift_max < LANES

    vmem = pl.BlockSpec(memory_space=pltpu.VMEM)
    tiled = lambda count, kind=jnp.float32: jax.ShapeDtypeStruct((count * SUBLANES, LANES), kind)
    room = lambda size: pltpu.CompilerParams(vmem_limit_bytes=size << 20)
    call = functools.partial(pl.pallas_call, compiler_params=room(1))
    swap = [(0, 1), (1, 0)]
    other = lax.ppermute(filterbank, "tm", swap)
    args = (filterbank, bandpass[None, :], local_delays, cross_delays)
    own, shifts, gain, steps, band = pl.pallas_call(
        table_kernel,
        out_shape=(
            jax.ShapeDtypeStruct(filterbank.shape, filterbank.dtype),
            tiled((grow + 2) // 2 * trials, jnp.int32),
            tiled(trials),
            tiled(cross_levels, jnp.int32),
            jax.ShapeDtypeStruct((4 * LANES, 2 * LANES), jnp.bfloat16),
        ),
        in_specs=[pl.BlockSpec(memory_space=pltpu.HBM)] * len(args),
        out_specs=(vmem,) * 5,
        scratch_shapes=[pltpu.VMEM(a.shape, a.dtype) for a in args[1:]]
        + [pltpu.SemaphoreType.DMA((len(args),))],
        compiler_params=room(4),
    )(*[pltpu.with_memory_space_constraint(a, pltpu.HBM) for a in args])
    plane = pl.pallas_call(
        functools.partial(plane_kernel, trials),
        out_shape=tiled(spans * past),
        in_specs=[vmem] * 5,
        out_specs=vmem,
        scratch_shapes=[
            pltpu.VMEM((rows, spans * span), filterbank.dtype),
            pltpu.VMEM((rows * spans * past, LANES), jnp.float32),
        ],
        compiler_params=room(6),
    )(own, other, shifts, gain, band)
    for level in range(cross_levels):
        last = level == cross_levels - 1
        mask = spans << level | 1
        there = lax.ppermute(plane, ("sub", "tm"), [(i, i ^ mask) for i in range(subs * spans)])
        scale = 1.0 / math.sqrt(rows * subs) if last else None
        plane = call(
            functools.partial(merge_kernel, level, scale),
            out_shape=(tiled(past),) * 2 if last else tiled(spans * past),
            in_specs=[vmem] * 3,
            out_specs=(vmem,) * 2 if last else vmem,
        )(plane, there, steps)
    keep, send = plane
    return call(
        functools.partial(last_kernel, cross_levels),
        out_shape=jax.ShapeDtypeStruct((trials, span), jnp.float32),
        in_specs=[vmem] * 2,
        out_specs=vmem,
    )(keep, lax.ppermute(send, "tm", swap))


def solution(mesh):
    return jax.shard_map(
        shards,
        mesh=mesh,
        in_specs=(P(("beam", "sub"), "tm"), P(("beam", "sub")), P(None, "sub"), P(None, "sub")),
        out_specs=P(("beam", "sub"), "tm"),
        check_vma=False,
    )
```

```python
import functools
import math

import jax
import jax.numpy as jnp
from jax import lax
from jax.experimental import pallas as pl
from jax.experimental.pallas import tpu as pltpu
from jax.sharding import PartitionSpec as P

LANES = 128
SUBLANES = 8
WINDOW = 31
HALF = WINDOW // 2


def iota(shape, axis):
    return lax.broadcasted_iota(jnp.int32, shape, axis)


def turned(x, index, axis):
    return jnp.take_along_axis(x, index, axis=axis, mode="promise_in_bounds")


def blocks_of(columns):
    return -(-columns // LANES)


def later(tiles, shift, count):
    source = iota(shift.shape, 1) - shift
    index = source & (LANES - 1)
    zero = jnp.zeros(shift.shape, jnp.float32)
    spun = [zero] + [turned(tile, index, 1) for tile in tiles]
    return [jnp.where(source >= 0, spun[b + 1], spun[b]) for b in range(count)]


def folded(tiles):
    row = iota(tiles[0].shape, 0)
    reach = SUBLANES // 2
    while reach:
        first = row & reach == 0
        tiles = [
            jnp.where(
                first,
                a + pltpu.roll(a, SUBLANES - reach, 0),
                b + pltpu.roll(b, reach, 0),
            )
            for a, b in zip(tiles[:reach], tiles[reach:])
        ]
        reach //= 2
    return tiles[0]


def table_kernel(*refs):
    fb_ref, *sources = refs[:4]
    own_ref, shifts_ref, gain_ref, steps_ref, band_ref, order_ref = refs[4:10]
    held, sems = refs[10:13], refs[13]
    copies = [
        pltpu.make_async_copy(a, b, sems.at[i])
        for i, (a, b) in enumerate(zip([*sources, fb_ref], [*held, own_ref]))
    ]
    for copy in copies:
        copy.start()
    bp_ref, ld_ref, cd_ref = held
    rows = own_ref.shape[0]
    local_levels = ld_ref.shape[0]
    cross_levels, trials = cd_ref.shape
    grow = trials.bit_length() - 1
    parity = row_half(cross_levels)
    square = (rows, LANES)
    lane, row = iota(square, 1), iota(square, 0)
    inner, outer = row & (SUBLANES - 1), row >> 3
    half = (rows // 2, LANES)
    lane_h, row_h = iota(half, 1), iota(half, 0)
    inner_h, outer_h = row_h & (SUBLANES - 1), (row_h >> 3) * 2 + parity

    at, to = iota(band_ref.shape, 0) - LANES, iota(band_ref.shape, 1)
    band = jnp.where(at == to, float(WINDOW), 0.0) - jnp.where(jnp.abs(at - to) <= HALF, 1.0, 0.0)
    band_ref[...] = band.astype(jnp.bfloat16)
    pick = lane == inner * trials + outer
    order_ref[...] = jnp.where(pick, 1.0, 0.0).astype(jnp.bfloat16)
    pick_h = lane_h == inner_h * trials + outer_h
    uses = []
    for bit in range(local_levels - grow):
        uses.append((lane_h == (inner_h >> (bit + 1)) * trials + outer_h) & (inner_h >> bit & 1 == 1))
    on, off = jnp.ones((LANES, LANES), jnp.bfloat16), jnp.zeros((LANES, LANES), jnp.bfloat16)
    ones = jnp.concatenate(
        [jnp.concatenate([on, off], axis=1), jnp.concatenate([off, on], axis=1)], axis=0
    )

    for copy in copies[:-1]:
        copy.wait()
    tail = jnp.zeros(half, jnp.int32)
    for bit, use in enumerate(uses):
        tail = tail + jnp.where(use, ld_ref[grow + bit : grow + bit + 1, :], 0)
    parts = [jnp.where(pick_h, ld_ref[m : m + 1, :], 0) for m in range(grow)]
    parts += [tail] + [jnp.zeros(half, jnp.int32)] * ((grow + 1) % 2)
    parts = [part.astype(jnp.float32).astype(jnp.bfloat16) for part in parts]
    pieces = [jnp.concatenate(parts[i : i + 2], axis=0) for i in range(0, len(parts), 2)]
    rest = bp_ref[...]
    for _ in range(3):
        part = rest.astype(jnp.bfloat16).astype(jnp.float32)
        rest = rest - part
        pieces.append(jnp.where(pick, part, 0.0).astype(jnp.bfloat16))
    pieces += [off] * (len(pieces) % 2)
    pairs = [jnp.concatenate(pieces[i : i + 2], axis=1) for i in range(0, len(pieces), 2)]
    spread = jnp.dot(jnp.concatenate(pairs, axis=0), ones, preferred_element_type=jnp.float32)
    spread = [
        spread[i // 2 * rows : (i // 2 + 1) * rows, i % 2 * LANES : (i % 2 + 1) * LANES]
        for i in range(len(pieces))
    ]
    count = len(parts) // 2
    for i in range(count):
        shifts_ref[i * rows : (i + 1) * rows, :] = spread[i].astype(jnp.int32)
    gain_ref[...] = (spread[count] + spread[count + 1] + spread[count + 2]) * (1.0 / WINDOW)
    kept = (SUBLANES, trials)
    kept = iota(kept, 1) == iota(kept, 0) * 2 + parity
    for l in range(cross_levels):
        step = jnp.sum(jnp.where(kept, cd_ref[l : l + 1, :].astype(jnp.float32), 0.0), axis=1, keepdims=True)
        step = jnp.broadcast_to(step, (SUBLANES, LANES)).astype(jnp.int32)
        steps_ref[l * SUBLANES : (l + 1) * SUBLANES, :] = step
    copies[-1].wait()


def plane_kernel(trials, own_ref, other_ref, shifts_ref, gain_ref, band_ref, order_ref, out_ref, whole_ref, level_ref):
    rows, span = own_ref.shape
    grow = trials.bit_length() - 1
    columns = whole_ref.shape[1]
    blocks = columns // LANES
    first_span = lax.axis_index("tm") == 0

    for part in range(0, span, 2 * LANES):
        cols = slice(part, part + 2 * LANES)
        own, other = (
            jnp.dot(order_ref[...], ref[:, cols], preferred_element_type=jnp.float32) for ref in (own_ref, other_ref)
        )
        whole_ref[:, cols] = jnp.where(first_span, own, other).astype(jnp.bfloat16)
        cols = slice(span + part, span + part + 2 * LANES)
        whole_ref[:, cols] = jnp.where(first_span, other, own).astype(jnp.bfloat16)

    for block in range(0, blocks, 2):
        low, high = max(block - 1, 0), min(block + 3, blocks)
        part = band_ref[(low - block + 1) * LANES : (high - block + 1) * LANES, :]
        got = jnp.dot(
            whole_ref[:, low * LANES : high * LANES], part, preferred_element_type=jnp.float32
        )
        level_ref[block * rows : (block + 1) * rows, :] = got[:, :LANES]
        level_ref[(block + 1) * rows : (block + 2) * rows, :] = got[:, LANES:]

    bands = []
    for e in range(trials):
        scale = gain_ref[e * SUBLANES : (e + 1) * SUBLANES, :]
        bands.append(
            [
                level_ref[block * rows + e * SUBLANES : block * rows + (e + 1) * SUBLANES, :] * scale
                for block in range(blocks)
            ]
        )
    plane = [bands]

    def merged(low, high, at_row):
        moved = later(high, shifts_ref[at_row : at_row + SUBLANES, :], blocks)
        return [a + b for a, b in zip(low, moved)]

    for m in range(grow):
        old, plane = plane, []
        for c in range(2 if m else 1):
            for i, held in enumerate(old):
                j = c * len(old) + i
                starts = [m * rows // 2 + ((e << m) + j) * SUBLANES for e in range(len(held) // 2)]
                plane.append([merged(held[2 * e], held[2 * e + 1], start) for e, start in enumerate(starts)])
    for j, held in enumerate(plane):
        at_row = grow * rows // 2 + j * SUBLANES
        moved = later(held[0], shifts_ref[at_row : at_row + SUBLANES, :], blocks)
        out_ref[pl.ds(j, SUBLANES, stride=SUBLANES), :] = folded(moved)


def row_half(cross_levels):
    half = lax.axis_index("tm")
    for level in range(cross_levels):
        half = half ^ (lax.axis_index("sub") >> level & 1)
    return half


def tile_of(ref, block):
    return ref[block * SUBLANES : (block + 1) * SUBLANES, :]


def merge_kernel(level, scale, own_ref, there_ref, steps_ref, out_ref, send_ref=None):
    is_upper = lax.axis_index("sub") >> level & 1 == 1
    blocks = own_ref.shape[0] // SUBLANES
    lower, upper = [], []
    for block in range(blocks):
        own, there = tile_of(own_ref, block), tile_of(there_ref, block)
        lower.append(jnp.where(is_upper, there, own))
        upper.append(jnp.where(is_upper, own, there))
    moved = later(upper, tile_of(steps_ref, level), blocks)
    new = [a + b for a, b in zip(lower, moved)]
    if scale is None:
        for block in range(blocks):
            out_ref[block * SUBLANES : (block + 1) * SUBLANES, :] = new[block]
        return
    first_span = lax.axis_index("tm") == 0
    past = blocks // 2
    for block in range(past):
        early, late = new[block] * scale, new[block + past] * scale
        out_ref[block * SUBLANES : (block + 1) * SUBLANES, :] = jnp.where(first_span, early, late)
        send_ref[block * SUBLANES : (block + 1) * SUBLANES, :] = jnp.where(first_span, late, early)


def last_kernel(cross_levels, keep_ref, there_ref, out_ref):
    is_even = row_half(cross_levels) == 0
    row = iota((SUBLANES, LANES), 0)
    for block in range(keep_ref.shape[0] // SUBLANES):
        keep, there = tile_of(keep_ref, block), tile_of(there_ref, block)
        even, odd = jnp.where(is_even, keep, there), jnp.where(is_even, there, keep)
        for part in range(2):
            source = (row >> 1) + part * (SUBLANES // 2)
            new = jnp.where(row & 1 == 0, turned(even, source, 0), turned(odd, source, 0))
            out_ref[part * SUBLANES : (part + 1) * SUBLANES, block * LANES : (block + 1) * LANES] = new


def shards(filterbank, bandpass, local_delays, cross_delays):
    rows, span = filterbank.shape
    cross_levels, trials = cross_delays.shape
    subs, spans = lax.axis_size("sub"), lax.axis_size("tm")
    local_levels = local_delays.shape[0]
    shift_max = span // 16
    grow = trials.bit_length() - 1
    past = span // LANES
    assert rows == LANES == trials * SUBLANES and trials == 2 * SUBLANES
    assert spans * past == SUBLANES and (local_levels - grow) * shift_max < LANES

    vmem = pl.BlockSpec(memory_space=pltpu.VMEM)
    tiled = lambda count, kind=jnp.float32: jax.ShapeDtypeStruct((count * SUBLANES, LANES), kind)
    room = lambda size: pltpu.CompilerParams(vmem_limit_bytes=size << 20)
    call = functools.partial(pl.pallas_call, compiler_params=room(1))
    swap = [(0, 1), (1, 0)]
    other = lax.ppermute(filterbank, "tm", swap)
    args = (filterbank, bandpass[None, :], local_delays, cross_delays)
    own, shifts, gain, steps, band, order = pl.pallas_call(
        table_kernel,
        out_shape=(
            jax.ShapeDtypeStruct(filterbank.shape, filterbank.dtype),
            tiled((grow + 2) // 2 * trials, jnp.int32),
            tiled(trials),
            tiled(cross_levels, jnp.int32),
            jax.ShapeDtypeStruct((4 * LANES, 2 * LANES), jnp.bfloat16),
            jax.ShapeDtypeStruct((rows, rows), jnp.bfloat16),
        ),
        in_specs=[pl.BlockSpec(memory_space=pltpu.HBM)] * len(args),
        out_specs=(vmem,) * 6,
        scratch_shapes=[pltpu.VMEM(a.shape, a.dtype) for a in args[1:]]
        + [pltpu.SemaphoreType.DMA((len(args),))],
        compiler_params=room(4),
    )(*[pltpu.with_memory_space_constraint(a, pltpu.HBM) for a in args])
    plane = pl.pallas_call(
        functools.partial(plane_kernel, trials),
        out_shape=tiled(spans * past),
        in_specs=[vmem] * 6,
        out_specs=vmem,
        scratch_shapes=[
            pltpu.VMEM((rows, spans * span), filterbank.dtype),
            pltpu.VMEM((rows * spans * past, LANES), jnp.float32),
        ],
        compiler_params=room(6),
    )(own, other, shifts, gain, band, order)
    for level in range(cross_levels):
        last = level == cross_levels - 1
        mask = spans << level | 1
        there = lax.ppermute(plane, ("sub", "tm"), [(i, i ^ mask) for i in range(subs * spans)])
        scale = 1.0 / math.sqrt(rows * subs) if last else None
        plane = call(
            functools.partial(merge_kernel, level, scale),
            out_shape=(tiled(past),) * 2 if last else tiled(spans * past),
            in_specs=[vmem] * 3,
            out_specs=(vmem,) * 2 if last else vmem,
        )(plane, there, steps)
    keep, send = plane
    return call(
        functools.partial(last_kernel, cross_levels),
        out_shape=jax.ShapeDtypeStruct((trials, span), jnp.float32),
        in_specs=[vmem] * 2,
        out_specs=vmem,
    )(keep, lax.ppermute(send, "tm", swap))


def solution(mesh):
    return jax.shard_map(
        shards,
        mesh=mesh,
        in_specs=(P(("beam", "sub"), "tm"), P(("beam", "sub")), P(None, "sub"), P(None, "sub")),
        out_specs=P(("beam", "sub"), "tm"),
        check_vma=False,
    )
```

```python
import functools
import math

import jax
import jax.numpy as jnp
from jax import lax
from jax.experimental import pallas as pl
from jax.experimental.pallas import tpu as pltpu
from jax.sharding import PartitionSpec as P

LANES = 128
SUBLANES = 8
WINDOW = 31
HALF = WINDOW // 2


def iota(shape, axis):
    return lax.broadcasted_iota(jnp.int32, shape, axis)


def turned(x, index, axis):
    return jnp.take_along_axis(x, index, axis=axis, mode="promise_in_bounds")


def blocks_of(columns):
    return -(-columns // LANES)


def later(tiles, shift, count):
    source = iota(shift.shape, 1) - shift
    index = source & (LANES - 1)
    zero = jnp.zeros(shift.shape, jnp.float32)
    spun = [zero] + [turned(tile, index, 1) for tile in tiles]
    return [jnp.where(source >= 0, spun[b + 1], spun[b]) for b in range(count)]


def folded(tiles):
    row = iota(tiles[0].shape, 0)
    reach = SUBLANES // 2
    while reach:
        first = row & reach == 0
        tiles = [
            jnp.where(
                first,
                a + pltpu.roll(a, SUBLANES - reach, 0),
                b + pltpu.roll(b, reach, 0),
            )
            for a, b in zip(tiles[:reach], tiles[reach:])
        ]
        reach //= 2
    return tiles[0]


def table_kernel(*refs):
    fb_ref, *sources = refs[:4]
    own_ref, shifts_ref, gain_ref, steps_ref, band_ref = refs[4:9]
    held, sems = refs[9:12], refs[12]
    copies = [
        pltpu.make_async_copy(a, b, sems.at[i])
        for i, (a, b) in enumerate(zip([*sources, fb_ref], [*held, own_ref]))
    ]
    for copy in copies:
        copy.start()
    bp_ref, ld_ref, cd_ref = held
    rows = own_ref.shape[0]
    local_levels = ld_ref.shape[0]
    cross_levels, trials = cd_ref.shape
    grow = trials.bit_length() - 1
    parity = row_half(cross_levels)
    square = (rows, LANES)
    lane, row = iota(square, 1), iota(square, 0)
    inner, outer = row & (SUBLANES - 1), row >> 3
    half = (rows // 2, LANES)
    lane_h, row_h = iota(half, 1), iota(half, 0)
    inner_h, outer_h = row_h & (SUBLANES - 1), (row_h >> 3) * 2 + parity

    at, to = iota(band_ref.shape, 0) - LANES, iota(band_ref.shape, 1)
    band = jnp.where(at == to, float(WINDOW), 0.0) - jnp.where(jnp.abs(at - to) <= HALF, 1.0, 0.0)
    band_ref[...] = band.astype(jnp.bfloat16)
    pick = lane == inner * trials + outer
    pick_h = lane_h == inner_h * trials + outer_h
    uses = []
    for bit in range(local_levels - grow):
        uses.append((lane_h == (inner_h >> (bit + 1)) * trials + outer_h) & (inner_h >> bit & 1 == 1))
    on, off = jnp.ones((LANES, LANES), jnp.bfloat16), jnp.zeros((LANES, LANES), jnp.bfloat16)
    ones = jnp.concatenate(
        [jnp.concatenate([on, off], axis=1), jnp.concatenate([off, on], axis=1)], axis=0
    )

    for copy in copies[:-1]:
        copy.wait()
    tail = jnp.zeros(half, jnp.int32)
    for bit, use in enumerate(uses):
        tail = tail + jnp.where(use, ld_ref[grow + bit : grow + bit + 1, :], 0)
    parts = [jnp.where(pick_h, ld_ref[m : m + 1, :], 0) for m in range(grow)]
    parts += [tail] + [jnp.zeros(half, jnp.int32)] * ((grow + 1) % 2)
    parts = [part.astype(jnp.float32).astype(jnp.bfloat16) for part in parts]
    pieces = [jnp.concatenate(parts[i : i + 2], axis=0) for i in range(0, len(parts), 2)]
    rest = bp_ref[...]
    for _ in range(3):
        part = rest.astype(jnp.bfloat16).astype(jnp.float32)
        rest = rest - part
        pieces.append(jnp.where(pick, part, 0.0).astype(jnp.bfloat16))
    pieces += [off] * (len(pieces) % 2)
    pairs = [jnp.concatenate(pieces[i : i + 2], axis=1) for i in range(0, len(pieces), 2)]
    spread = jnp.dot(jnp.concatenate(pairs, axis=0), ones, preferred_element_type=jnp.float32)
    spread = [
        spread[i // 2 * rows : (i // 2 + 1) * rows, i % 2 * LANES : (i % 2 + 1) * LANES]
        for i in range(len(pieces))
    ]
    count = len(parts) // 2
    for i in range(count):
        shifts_ref[i * rows : (i + 1) * rows, :] = spread[i].astype(jnp.int32)
    gain_ref[...] = (spread[count] + spread[count + 1] + spread[count + 2]) * (1.0 / WINDOW)
    kept = (SUBLANES, trials)
    kept = iota(kept, 1) == iota(kept, 0) * 2 + parity
    for l in range(cross_levels):
        step = jnp.sum(jnp.where(kept, cd_ref[l : l + 1, :].astype(jnp.float32), 0.0), axis=1, keepdims=True)
        step = jnp.broadcast_to(step, (SUBLANES, LANES)).astype(jnp.int32)
        steps_ref[l * SUBLANES : (l + 1) * SUBLANES, :] = step
    copies[-1].wait()


def plane_kernel(trials, own_ref, other_ref, shifts_ref, gain_ref, band_ref, out_ref, level_ref):
    rows, span = own_ref.shape
    grow = trials.bit_length() - 1
    first_span = lax.axis_index("tm") == 0
    own, other = (
        [ref[:, start : start + LANES] for start in range(0, span, LANES)] for ref in (own_ref, other_ref)
    )
    whole = [jnp.where(first_span, a, b) for a, b in zip(own, other)]
    whole += [jnp.where(first_span, b, a) for a, b in zip(own, other)]
    blocks = len(whole)

    for block in range(0, blocks, 2):
        low, high = max(block - 1, 0), min(block + 3, blocks)
        part = band_ref[(low - block + 1) * LANES : (high - block + 1) * LANES, :]
        got = jnp.dot(
            jnp.concatenate(whole[low:high], axis=1), part, preferred_element_type=jnp.float32
        )
        level_ref[block * rows : (block + 1) * rows, :] = got[:, :LANES]
        level_ref[(block + 1) * rows : (block + 2) * rows, :] = got[:, LANES:]

    bands = []
    for e in range(trials):
        scale = gain_ref[e * SUBLANES : (e + 1) * SUBLANES, :]
        bands.append(
            [level_ref[pl.ds(block * rows + e, SUBLANES, stride=trials), :] * scale for block in range(blocks)]
        )
    plane = [bands]

    def merged(low, high, at_row):
        moved = later(high, shifts_ref[at_row : at_row + SUBLANES, :], blocks)
        return [a + b for a, b in zip(low, moved)]

    for m in range(grow):
        old, plane = plane, []
        for c in range(2 if m else 1):
            for i, held in enumerate(old):
                j = c * len(old) + i
                starts = [m * rows // 2 + ((e << m) + j) * SUBLANES for e in range(len(held) // 2)]
                plane.append([merged(held[2 * e], held[2 * e + 1], start) for e, start in enumerate(starts)])
    for j, held in enumerate(plane):
        at_row = grow * rows // 2 + j * SUBLANES
        moved = later(held[0], shifts_ref[at_row : at_row + SUBLANES, :], blocks)
        out_ref[pl.ds(j, SUBLANES, stride=SUBLANES), :] = folded(moved)


def row_half(cross_levels):
    half = lax.axis_index("tm")
    for level in range(cross_levels):
        half = half ^ (lax.axis_index("sub") >> level & 1)
    return half


def tile_of(ref, block):
    return ref[block * SUBLANES : (block + 1) * SUBLANES, :]


def merge_kernel(level, scale, own_ref, there_ref, steps_ref, out_ref, send_ref=None):
    is_upper = lax.axis_index("sub") >> level & 1 == 1
    blocks = own_ref.shape[0] // SUBLANES
    lower, upper = [], []
    for block in range(blocks):
        own, there = tile_of(own_ref, block), tile_of(there_ref, block)
        lower.append(jnp.where(is_upper, there, own))
        upper.append(jnp.where(is_upper, own, there))
    moved = later(upper, tile_of(steps_ref, level), blocks)
    new = [a + b for a, b in zip(lower, moved)]
    if scale is None:
        for block in range(blocks):
            out_ref[block * SUBLANES : (block + 1) * SUBLANES, :] = new[block]
        return
    first_span = lax.axis_index("tm") == 0
    past = blocks // 2
    for block in range(past):
        early, late = new[block] * scale, new[block + past] * scale
        out_ref[block * SUBLANES : (block + 1) * SUBLANES, :] = jnp.where(first_span, early, late)
        send_ref[block * SUBLANES : (block + 1) * SUBLANES, :] = jnp.where(first_span, late, early)


def last_kernel(cross_levels, keep_ref, there_ref, out_ref):
    is_even = row_half(cross_levels) == 0
    row = iota((SUBLANES, LANES), 0)
    for block in range(keep_ref.shape[0] // SUBLANES):
        keep, there = tile_of(keep_ref, block), tile_of(there_ref, block)
        even, odd = jnp.where(is_even, keep, there), jnp.where(is_even, there, keep)
        for part in range(2):
            source = (row >> 1) + part * (SUBLANES // 2)
            new = jnp.where(row & 1 == 0, turned(even, source, 0), turned(odd, source, 0))
            out_ref[part * SUBLANES : (part + 1) * SUBLANES, block * LANES : (block + 1) * LANES] = new


def shards(filterbank, bandpass, local_delays, cross_delays):
    rows, span = filterbank.shape
    cross_levels, trials = cross_delays.shape
    subs, spans = lax.axis_size("sub"), lax.axis_size("tm")
    local_levels = local_delays.shape[0]
    shift_max = span // 16
    grow = trials.bit_length() - 1
    past = span // LANES
    assert rows == LANES == trials * SUBLANES and trials == 2 * SUBLANES
    assert spans * past == SUBLANES and (local_levels - grow) * shift_max < LANES

    vmem = pl.BlockSpec(memory_space=pltpu.VMEM)
    tiled = lambda count, kind=jnp.float32: jax.ShapeDtypeStruct((count * SUBLANES, LANES), kind)
    room = lambda size: pltpu.CompilerParams(vmem_limit_bytes=size << 20)
    call = functools.partial(pl.pallas_call, compiler_params=room(1))
    swap = [(0, 1), (1, 0)]
    other = lax.ppermute(filterbank, "tm", swap)
    args = (filterbank, bandpass[None, :], local_delays, cross_delays)
    own, shifts, gain, steps, band = pl.pallas_call(
        table_kernel,
        out_shape=(
            jax.ShapeDtypeStruct(filterbank.shape, filterbank.dtype),
            tiled((grow + 2) // 2 * trials, jnp.int32),
            tiled(trials),
            tiled(cross_levels, jnp.int32),
            jax.ShapeDtypeStruct((4 * LANES, 2 * LANES), jnp.bfloat16),
        ),
        in_specs=[pl.BlockSpec(memory_space=pltpu.HBM)] * len(args),
        out_specs=(vmem,) * 5,
        scratch_shapes=[pltpu.VMEM(a.shape, a.dtype) for a in args[1:]]
        + [pltpu.SemaphoreType.DMA((len(args),))],
        compiler_params=room(4),
    )(*[pltpu.with_memory_space_constraint(a, pltpu.HBM) for a in args])
    plane = pl.pallas_call(
        functools.partial(plane_kernel, trials),
        out_shape=tiled(spans * past),
        in_specs=[vmem] * 5,
        out_specs=vmem,
        scratch_shapes=[pltpu.VMEM((rows * spans * past, LANES), jnp.float32)],
        compiler_params=room(6),
    )(own, other, shifts, gain, band)
    for level in range(cross_levels):
        last = level == cross_levels - 1
        mask = spans << level | 1
        there = lax.ppermute(plane, ("sub", "tm"), [(i, i ^ mask) for i in range(subs * spans)])
        scale = 1.0 / math.sqrt(rows * subs) if last else None
        plane = call(
            functools.partial(merge_kernel, level, scale),
            out_shape=(tiled(past),) * 2 if last else tiled(spans * past),
            in_specs=[vmem] * 3,
            out_specs=(vmem,) * 2 if last else vmem,
        )(plane, there, steps)
    keep, send = plane
    return call(
        functools.partial(last_kernel, cross_levels),
        out_shape=jax.ShapeDtypeStruct((trials, span), jnp.float32),
        in_specs=[vmem] * 2,
        out_specs=vmem,
    )(keep, lax.ppermute(send, "tm", swap))


def solution(mesh):
    return jax.shard_map(
        shards,
        mesh=mesh,
        in_specs=(P(("beam", "sub"), "tm"), P(("beam", "sub")), P(None, "sub"), P(None, "sub")),
        out_specs=P(("beam", "sub"), "tm"),
        check_vma=False,
    )
```

```python
import functools
import math

import jax
import jax.numpy as jnp
from jax import lax
from jax.experimental import pallas as pl
from jax.experimental.pallas import tpu as pltpu
from jax.sharding import PartitionSpec as P

LANES = 128
SUBLANES = 8
WINDOW = 31
HALF = WINDOW // 2


def iota(shape, axis):
    return lax.broadcasted_iota(jnp.int32, shape, axis)


def turned(x, index, axis):
    return jnp.take_along_axis(x, index, axis=axis, mode="promise_in_bounds")


def blocks_of(columns):
    return -(-columns // LANES)


def later(tiles, shift, count):
    source = iota(shift.shape, 1) - shift
    index = source & (LANES - 1)
    zero = jnp.zeros(shift.shape, jnp.float32)
    spun = [zero] + [turned(tile, index, 1) for tile in tiles]
    return [jnp.where(source >= 0, spun[b + 1], spun[b]) for b in range(count)]


def folded(tiles):
    row = iota(tiles[0].shape, 0)
    reach = SUBLANES // 2
    while reach:
        first = row & reach == 0
        tiles = [
            jnp.where(
                first,
                a + pltpu.roll(a, SUBLANES - reach, 0),
                b + pltpu.roll(b, reach, 0),
            )
            for a, b in zip(tiles[:reach], tiles[reach:])
        ]
        reach //= 2
    return tiles[0]


def table_kernel(*refs):
    fb_ref, *sources = refs[:4]
    own_ref, own_level_ref, shifts_ref, gain_ref, steps_ref, band_ref = refs[4:10]
    held, sems = refs[10:13], refs[13]
    copies = [
        pltpu.make_async_copy(a, b, sems.at[i])
        for i, (a, b) in enumerate(zip([*sources, fb_ref], [*held, own_ref]))
    ]
    for copy in copies:
        copy.start()
    bp_ref, ld_ref, cd_ref = held
    rows = own_ref.shape[0]
    local_levels = ld_ref.shape[0]
    cross_levels, trials = cd_ref.shape
    grow = trials.bit_length() - 1
    parity = row_half(cross_levels)
    square = (rows, LANES)
    lane, row = iota(square, 1), iota(square, 0)
    inner, outer = row & (SUBLANES - 1), row >> 3
    half = (rows // 2, LANES)
    lane_h, row_h = iota(half, 1), iota(half, 0)
    inner_h, outer_h = row_h & (SUBLANES - 1), (row_h >> 3) * 2 + parity

    at, to = iota(band_ref.shape, 0) - LANES, iota(band_ref.shape, 1)
    band = jnp.where(at == to, float(WINDOW), 0.0) - jnp.where(jnp.abs(at - to) <= HALF, 1.0, 0.0)
    band_ref[...] = band.astype(jnp.bfloat16)
    pick = lane == inner * trials + outer
    pick_h = lane_h == inner_h * trials + outer_h
    uses = []
    for bit in range(local_levels - grow):
        uses.append((lane_h == (inner_h >> (bit + 1)) * trials + outer_h) & (inner_h >> bit & 1 == 1))
    on, off = jnp.ones((LANES, LANES), jnp.bfloat16), jnp.zeros((LANES, LANES), jnp.bfloat16)
    ones = jnp.concatenate(
        [jnp.concatenate([on, off], axis=1), jnp.concatenate([off, on], axis=1)], axis=0
    )

    for copy in copies[:-1]:
        copy.wait()
    tail = jnp.zeros(half, jnp.int32)
    for bit, use in enumerate(uses):
        tail = tail + jnp.where(use, ld_ref[grow + bit : grow + bit + 1, :], 0)
    parts = [jnp.where(pick_h, ld_ref[m : m + 1, :], 0) for m in range(grow)]
    parts += [tail] + [jnp.zeros(half, jnp.int32)] * ((grow + 1) % 2)
    parts = [part.astype(jnp.float32).astype(jnp.bfloat16) for part in parts]
    pieces = [jnp.concatenate(parts[i : i + 2], axis=0) for i in range(0, len(parts), 2)]
    rest = bp_ref[...]
    for _ in range(3):
        part = rest.astype(jnp.bfloat16).astype(jnp.float32)
        rest = rest - part
        pieces.append(jnp.where(pick, part, 0.0).astype(jnp.bfloat16))
    pieces += [off] * (len(pieces) % 2)
    pairs = [jnp.concatenate(pieces[i : i + 2], axis=1) for i in range(0, len(pieces), 2)]
    spread = jnp.dot(jnp.concatenate(pairs, axis=0), ones, preferred_element_type=jnp.float32)
    spread = [
        spread[i // 2 * rows : (i // 2 + 1) * rows, i % 2 * LANES : (i % 2 + 1) * LANES]
        for i in range(len(pieces))
    ]
    count = len(parts) // 2
    for i in range(count):
        shifts_ref[i * rows : (i + 1) * rows, :] = spread[i].astype(jnp.int32)
    gain_ref[...] = (spread[count] + spread[count + 1] + spread[count + 2]) * (1.0 / WINDOW)
    kept = (SUBLANES, trials)
    kept = iota(kept, 1) == iota(kept, 0) * 2 + parity
    for l in range(cross_levels):
        step = jnp.sum(jnp.where(kept, cd_ref[l : l + 1, :].astype(jnp.float32), 0.0), axis=1, keepdims=True)
        step = jnp.broadcast_to(step, (SUBLANES, LANES)).astype(jnp.int32)
        steps_ref[l * SUBLANES : (l + 1) * SUBLANES, :] = step
    copies[-1].wait()
    window_sums(own_ref, band_ref, own_level_ref)


def window_sums(samples_ref, band_ref, level_ref):
    rows = samples_ref.shape[0]
    blocks = samples_ref.shape[1] // LANES
    for block in range(0, blocks, 2):
        low, high = max(block - 1, 0), min(block + 3, blocks)
        part = band_ref[(low - block + 1) * LANES : (high - block + 1) * LANES, :]
        got = jnp.dot(
            samples_ref[:, low * LANES : high * LANES], part, preferred_element_type=jnp.float32
        )
        level_ref[block * rows : (block + 1) * rows, :] = got[:, :LANES]
        level_ref[(block + 1) * rows : (block + 2) * rows, :] = got[:, LANES:]


def plane_kernel(trials, *refs):
    own_ref, other_ref, own_level_ref, shifts_ref, gain_ref, band_ref = refs[:6]
    out_ref, other_level_ref, seam_ref = refs[6:]
    rows, span = own_ref.shape
    grow = trials.bit_length() - 1
    per_span = span // LANES
    blocks = 2 * per_span
    first_span = lax.axis_index("tm") == 0
    own_first, own_last = own_ref[:, :LANES], own_ref[:, span - LANES :]
    none = jnp.zeros((rows, LANES), own_ref.dtype)
    other = [other_ref[:, start : start + LANES] for start in range(0, span, LANES)]
    about = [jnp.where(first_span, own_last, none), *other, jnp.where(first_span, none, own_first)]
    for block in range(0, per_span, 2):
        window = jnp.concatenate(about[block : block + 4], axis=1)
        got = jnp.dot(window, band_ref[...], preferred_element_type=jnp.float32)
        other_level_ref[block * rows : (block + 1) * rows, :] = got[:, :LANES]
        other_level_ref[(block + 1) * rows : (block + 2) * rows, :] = got[:, LANES:]

    after, before = band_ref[3 * LANES :, LANES:], band_ref[:LANES, :LANES]
    seam_ref[...] = jnp.dot(
        jnp.where(first_span, other[0], other[-1]),
        jnp.where(first_span, after, before),
        preferred_element_type=jnp.float32,
    )

    bands = []
    for e in range(trials):
        scale = gain_ref[e * SUBLANES : (e + 1) * SUBLANES, :]
        rows_of = lambda ref, block: ref[pl.ds(block * rows + e, SUBLANES, stride=trials), :]
        own = [rows_of(own_level_ref, block) for block in range(per_span)]
        other = [rows_of(other_level_ref, block) for block in range(per_span)]
        tiles = [jnp.where(first_span, a, b) for a, b in zip(own, other)]
        tiles += [jnp.where(first_span, b, a) for a, b in zip(own, other)]
        seam = rows_of(seam_ref, 0)
        tiles[per_span - 1] += jnp.where(first_span, seam, 0.0)
        tiles[per_span] += jnp.where(first_span, 0.0, seam)
        bands.append([tile * scale for tile in tiles])
    plane = [bands]

    def merged(low, high, at_row):
        moved = later(high, shifts_ref[at_row : at_row + SUBLANES, :], blocks)
        return [a + b for a, b in zip(low, moved)]

    for m in range(grow):
        old, plane = plane, []
        for c in range(2 if m else 1):
            for i, held in enumerate(old):
                j = c * len(old) + i
                starts = [m * rows // 2 + ((e << m) + j) * SUBLANES for e in range(len(held) // 2)]
                plane.append([merged(held[2 * e], held[2 * e + 1], start) for e, start in enumerate(starts)])
    for j, held in enumerate(plane):
        at_row = grow * rows // 2 + j * SUBLANES
        moved = later(held[0], shifts_ref[at_row : at_row + SUBLANES, :], blocks)
        out_ref[pl.ds(j, SUBLANES, stride=SUBLANES), :] = folded(moved)


def row_half(cross_levels):
    half = lax.axis_index("tm")
    for level in range(cross_levels):
        half = half ^ (lax.axis_index("sub") >> level & 1)
    return half


def tile_of(ref, block):
    return ref[block * SUBLANES : (block + 1) * SUBLANES, :]


def merge_kernel(level, scale, own_ref, there_ref, steps_ref, out_ref, send_ref=None):
    is_upper = lax.axis_index("sub") >> level & 1 == 1
    blocks = own_ref.shape[0] // SUBLANES
    lower, upper = [], []
    for block in range(blocks):
        own, there = tile_of(own_ref, block), tile_of(there_ref, block)
        lower.append(jnp.where(is_upper, there, own))
        upper.append(jnp.where(is_upper, own, there))
    moved = later(upper, tile_of(steps_ref, level), blocks)
    new = [a + b for a, b in zip(lower, moved)]
    if scale is None:
        for block in range(blocks):
            out_ref[block * SUBLANES : (block + 1) * SUBLANES, :] = new[block]
        return
    first_span = lax.axis_index("tm") == 0
    past = blocks // 2
    for block in range(past):
        early, late = new[block] * scale, new[block + past] * scale
        out_ref[block * SUBLANES : (block + 1) * SUBLANES, :] = jnp.where(first_span, early, late)
        send_ref[block * SUBLANES : (block + 1) * SUBLANES, :] = jnp.where(first_span, late, early)


def last_kernel(cross_levels, keep_ref, there_ref, out_ref):
    is_even = row_half(cross_levels) == 0
    row = iota((SUBLANES, LANES), 0)
    for block in range(keep_ref.shape[0] // SUBLANES):
        keep, there = tile_of(keep_ref, block), tile_of(there_ref, block)
        even, odd = jnp.where(is_even, keep, there), jnp.where(is_even, there, keep)
        for part in range(2):
            source = (row >> 1) + part * (SUBLANES // 2)
            new = jnp.where(row & 1 == 0, turned(even, source, 0), turned(odd, source, 0))
            out_ref[part * SUBLANES : (part + 1) * SUBLANES, block * LANES : (block + 1) * LANES] = new


def shards(filterbank, bandpass, local_delays, cross_delays):
    rows, span = filterbank.shape
    cross_levels, trials = cross_delays.shape
    subs, spans = lax.axis_size("sub"), lax.axis_size("tm")
    local_levels = local_delays.shape[0]
    shift_max = span // 16
    grow = trials.bit_length() - 1
    past = span // LANES
    assert rows == LANES == trials * SUBLANES and trials == 2 * SUBLANES
    assert spans * past == SUBLANES and (local_levels - grow) * shift_max < LANES

    vmem = pl.BlockSpec(memory_space=pltpu.VMEM)
    tiled = lambda count, kind=jnp.float32: jax.ShapeDtypeStruct((count * SUBLANES, LANES), kind)
    room = lambda size: pltpu.CompilerParams(vmem_limit_bytes=size << 20)
    call = functools.partial(pl.pallas_call, compiler_params=room(1))
    swap = [(0, 1), (1, 0)]
    other = lax.ppermute(filterbank, "tm", swap)
    args = (filterbank, bandpass[None, :], local_delays, cross_delays)
    own, own_level, shifts, gain, steps, band = pl.pallas_call(
        table_kernel,
        out_shape=(
            jax.ShapeDtypeStruct(filterbank.shape, filterbank.dtype),
            tiled(past * trials),
            tiled((grow + 2) // 2 * trials, jnp.int32),
            tiled(trials),
            tiled(cross_levels, jnp.int32),
            jax.ShapeDtypeStruct((4 * LANES, 2 * LANES), jnp.bfloat16),
        ),
        in_specs=[pl.BlockSpec(memory_space=pltpu.HBM)] * len(args),
        out_specs=(vmem,) * 6,
        scratch_shapes=[pltpu.VMEM(a.shape, a.dtype) for a in args[1:]]
        + [pltpu.SemaphoreType.DMA((len(args),))],
        compiler_params=room(4),
    )(*[pltpu.with_memory_space_constraint(a, pltpu.HBM) for a in args])
    plane = pl.pallas_call(
        functools.partial(plane_kernel, trials),
        out_shape=tiled(spans * past),
        in_specs=[vmem] * 6,
        out_specs=vmem,
        scratch_shapes=[
            pltpu.VMEM((rows * past, LANES), jnp.float32),
            pltpu.VMEM((rows, LANES), jnp.float32),
        ],
        compiler_params=room(6),
    )(own, other, own_level, shifts, gain, band)
    for level in range(cross_levels):
        last = level == cross_levels - 1
        mask = spans << level | 1
        there = lax.ppermute(plane, ("sub", "tm"), [(i, i ^ mask) for i in range(subs * spans)])
        scale = 1.0 / math.sqrt(rows * subs) if last else None
        plane = call(
            functools.partial(merge_kernel, level, scale),
            out_shape=(tiled(past),) * 2 if last else tiled(spans * past),
            in_specs=[vmem] * 3,
            out_specs=(vmem,) * 2 if last else vmem,
        )(plane, there, steps)
    keep, send = plane
    return call(
        functools.partial(last_kernel, cross_levels),
        out_shape=jax.ShapeDtypeStruct((trials, span), jnp.float32),
        in_specs=[vmem] * 2,
        out_specs=vmem,
    )(keep, lax.ppermute(send, "tm", swap))


def solution(mesh):
    return jax.shard_map(
        shards,
        mesh=mesh,
        in_specs=(P(("beam", "sub"), "tm"), P(("beam", "sub")), P(None, "sub"), P(None, "sub")),
        out_specs=P(("beam", "sub"), "tm"),
        check_vma=False,
    )
```

```python
import functools
import math

import jax
import jax.numpy as jnp
from jax import lax
from jax.experimental import pallas as pl
from jax.experimental.pallas import tpu as pltpu
from jax.sharding import PartitionSpec as P

LANES = 128
SUBLANES = 8
WINDOW = 31
HALF = WINDOW // 2


def iota(shape, axis):
    return lax.broadcasted_iota(jnp.int32, shape, axis)


def turned(x, index, axis):
    return jnp.take_along_axis(x, index, axis=axis, mode="promise_in_bounds")


def blocks_of(columns):
    return -(-columns // LANES)


def later(tiles, source, count):
    index = source & (LANES - 1)
    zero = jnp.zeros(source.shape, jnp.float32)
    spun = [zero] + [turned(tile, index, 1) for tile in tiles]
    return [jnp.where(source >= 0, spun[b + 1], spun[b]) for b in range(count)]


def folded(tiles):
    row = iota(tiles[0].shape, 0)
    reach = SUBLANES // 2
    while reach:
        first = row & reach == 0
        tiles = [
            jnp.where(first, a, b) + pltpu.roll(jnp.where(first, b, a), reach, 0)
            if 2 * reach == SUBLANES
            else jnp.where(first, a + pltpu.roll(a, SUBLANES - reach, 0), b + pltpu.roll(b, reach, 0))
            for a, b in zip(tiles[:reach], tiles[reach:])
        ]
        reach //= 2
    return tiles[0]


def table_kernel(*refs):
    fb_ref, *sources = refs[:4]
    own_ref, shifts_ref, gain_ref, steps_ref, band_ref = refs[4:9]
    held, sems = refs[9:12], refs[12]
    copies = [
        pltpu.make_async_copy(a, b, sems.at[i])
        for i, (a, b) in enumerate(zip([*sources, fb_ref], [*held, own_ref]))
    ]
    for copy in copies:
        copy.start()
    bp_ref, ld_ref, cd_ref = held
    rows = own_ref.shape[0]
    local_levels = ld_ref.shape[0]
    cross_levels, trials = cd_ref.shape
    grow = trials.bit_length() - 1
    parity = row_half(cross_levels)
    square = (rows, LANES)
    lane, row = iota(square, 1), iota(square, 0)
    inner, outer = row & (SUBLANES - 1), row >> 3
    half = (rows // 2, LANES)
    lane_h, row_h = iota(half, 1), iota(half, 0)
    inner_h, outer_h = row_h & (SUBLANES - 1), (row_h >> 3) * 2 + parity

    at, to = iota(band_ref.shape, 0) - LANES, iota(band_ref.shape, 1)
    band = jnp.where(at == to, float(WINDOW), 0.0) - jnp.where(jnp.abs(at - to) <= HALF, 1.0, 0.0)
    band_ref[...] = band.astype(jnp.bfloat16)
    pick = lane == inner * trials + outer
    pick_h = lane_h == inner_h * trials + outer_h
    uses = []
    for bit in range(local_levels - grow):
        uses.append((lane_h == (inner_h >> (bit + 1)) * trials + outer_h) & (inner_h >> bit & 1 == 1))
    on, off = jnp.ones((LANES, LANES), jnp.bfloat16), jnp.zeros((LANES, LANES), jnp.bfloat16)
    ones = jnp.concatenate(
        [jnp.concatenate([on, off], axis=1), jnp.concatenate([off, on], axis=1)], axis=0
    )

    for copy in copies[:-1]:
        copy.wait()
    tail = jnp.zeros(half, jnp.int32)
    for bit, use in enumerate(uses):
        tail = tail + jnp.where(use, ld_ref[grow + bit : grow + bit + 1, :], 0)
    parts = [jnp.where(pick_h, ld_ref[m : m + 1, :], 0) for m in range(grow)]
    parts += [tail] + [jnp.zeros(half, jnp.int32)] * ((grow + 1) % 2)
    parts = [part.astype(jnp.float32).astype(jnp.bfloat16) for part in parts]
    pieces = [jnp.concatenate(parts[i : i + 2], axis=0) for i in range(0, len(parts), 2)]
    rest = bp_ref[...]
    for _ in range(3):
        part = rest.astype(jnp.bfloat16).astype(jnp.float32)
        rest = rest - part
        pieces.append(jnp.where(pick, part, 0.0).astype(jnp.bfloat16))
    pieces += [off] * (len(pieces) % 2)
    pairs = [jnp.concatenate(pieces[i : i + 2], axis=1) for i in range(0, len(pieces), 2)]
    spread = jnp.dot(jnp.concatenate(pairs, axis=0), ones, preferred_element_type=jnp.float32)
    spread = [
        spread[i // 2 * rows : (i // 2 + 1) * rows, i % 2 * LANES : (i % 2 + 1) * LANES]
        for i in range(len(pieces))
    ]
    count = len(parts) // 2
    for i in range(count):
        shifts_ref[i * rows : (i + 1) * rows, :] = lane - spread[i].astype(jnp.int32)
    gain_ref[...] = (spread[count] + spread[count + 1] + spread[count + 2]) * (1.0 / WINDOW)
    kept = (SUBLANES, trials)
    kept = iota(kept, 1) == iota(kept, 0) * 2 + parity
    for l in range(cross_levels):
        step = jnp.sum(jnp.where(kept, cd_ref[l : l + 1, :].astype(jnp.float32), 0.0), axis=1, keepdims=True)
        step = jnp.broadcast_to(step, (SUBLANES, LANES)).astype(jnp.int32)
        steps_ref[l * SUBLANES : (l + 1) * SUBLANES, :] = iota(step.shape, 1) - step
    copies[-1].wait()


def plane_kernel(trials, own_ref, other_ref, shifts_ref, gain_ref, band_ref, out_ref, whole_ref, level_ref):
    rows, span = own_ref.shape
    grow = trials.bit_length() - 1
    columns = whole_ref.shape[1]
    blocks = columns // LANES
    first_span = lax.axis_index("tm") == 0

    @pl.when(first_span)
    def _():
        whole_ref[:, :span] = own_ref[...]
        whole_ref[:, span:] = other_ref[...]

    @pl.when(jnp.logical_not(first_span))
    def _():
        whole_ref[:, :span] = other_ref[...]
        whole_ref[:, span:] = own_ref[...]

    for block in range(0, blocks, 2):
        low, high = max(block - 1, 0), min(block + 3, blocks)
        part = band_ref[(low - block + 1) * LANES : (high - block + 1) * LANES, :]
        got = jnp.dot(
            whole_ref[:, low * LANES : high * LANES], part, preferred_element_type=jnp.float32
        )
        level_ref[block * rows : (block + 1) * rows, :] = got[:, :LANES]
        level_ref[(block + 1) * rows : (block + 2) * rows, :] = got[:, LANES:]

    bands = []
    for e in range(trials):
        scale = gain_ref[e * SUBLANES : (e + 1) * SUBLANES, :]
        bands.append(
            [level_ref[pl.ds(block * rows + e, SUBLANES, stride=trials), :] * scale for block in range(blocks)]
        )
    plane = [bands]

    def merged(low, high, at_row):
        moved = later(high, shifts_ref[at_row : at_row + SUBLANES, :], blocks)
        return [a + b for a, b in zip(low, moved)]

    for m in range(grow):
        old, plane = plane, []
        for c in range(2 if m else 1):
            for i, held in enumerate(old):
                j = c * len(old) + i
                starts = [m * rows // 2 + ((e << m) + j) * SUBLANES for e in range(len(held) // 2)]
                plane.append([merged(held[2 * e], held[2 * e + 1], start) for e, start in enumerate(starts)])
    for j, held in enumerate(plane):
        at_row = grow * rows // 2 + j * SUBLANES
        moved = later(held[0], shifts_ref[at_row : at_row + SUBLANES, :], blocks)
        out_ref[pl.ds(j, SUBLANES, stride=SUBLANES), :] = folded(moved)


def row_half(cross_levels):
    half = lax.axis_index("tm")
    for level in range(cross_levels):
        half = half ^ (lax.axis_index("sub") >> level & 1)
    return half


def tile_of(ref, block):
    return ref[block * SUBLANES : (block + 1) * SUBLANES, :]


def merge_kernel(level, scale, own_ref, there_ref, steps_ref, out_ref, send_ref=None):
    is_upper = lax.axis_index("sub") >> level & 1 == 1
    blocks = own_ref.shape[0] // SUBLANES
    lower, upper = [], []
    for block in range(blocks):
        own, there = tile_of(own_ref, block), tile_of(there_ref, block)
        lower.append(jnp.where(is_upper, there, own))
        upper.append(jnp.where(is_upper, own, there))
    moved = later(upper, tile_of(steps_ref, level), blocks)
    new = [a + b for a, b in zip(lower, moved)]
    if scale is None:
        for block in range(blocks):
            out_ref[block * SUBLANES : (block + 1) * SUBLANES, :] = new[block]
        return
    first_span = lax.axis_index("tm") == 0
    past = blocks // 2
    for block in range(past):
        early, late = new[block] * scale, new[block + past] * scale
        out_ref[block * SUBLANES : (block + 1) * SUBLANES, :] = jnp.where(first_span, early, late)
        send_ref[block * SUBLANES : (block + 1) * SUBLANES, :] = jnp.where(first_span, late, early)


def last_kernel(cross_levels, keep_ref, there_ref, out_ref):
    is_even = row_half(cross_levels) == 0
    row = iota((SUBLANES, LANES), 0)
    for block in range(keep_ref.shape[0] // SUBLANES):
        keep, there = tile_of(keep_ref, block), tile_of(there_ref, block)
        even, odd = jnp.where(is_even, keep, there), jnp.where(is_even, there, keep)
        for part in range(2):
            source = (row >> 1) + part * (SUBLANES // 2)
            new = jnp.where(row & 1 == 0, turned(even, source, 0), turned(odd, source, 0))
            out_ref[part * SUBLANES : (part + 1) * SUBLANES, block * LANES : (block + 1) * LANES] = new


def shards(filterbank, bandpass, local_delays, cross_delays):
    rows, span = filterbank.shape
    cross_levels, trials = cross_delays.shape
    subs, spans = lax.axis_size("sub"), lax.axis_size("tm")
    local_levels = local_delays.shape[0]
    shift_max = span // 16
    grow = trials.bit_length() - 1
    past = span // LANES
    assert rows == LANES == trials * SUBLANES and trials == 2 * SUBLANES
    assert spans * past == SUBLANES and (local_levels - grow) * shift_max < LANES

    vmem = pl.BlockSpec(memory_space=pltpu.VMEM)
    tiled = lambda count, kind=jnp.float32: jax.ShapeDtypeStruct((count * SUBLANES, LANES), kind)
    room = lambda size: pltpu.CompilerParams(vmem_limit_bytes=size << 20)
    call = functools.partial(pl.pallas_call, compiler_params=room(1))
    swap = [(0, 1), (1, 0)]
    other = lax.ppermute(filterbank, "tm", swap)
    args = (filterbank, bandpass[None, :], local_delays, cross_delays)
    own, shifts, gain, steps, band = pl.pallas_call(
        table_kernel,
        out_shape=(
            jax.ShapeDtypeStruct(filterbank.shape, filterbank.dtype),
            tiled((grow + 2) // 2 * trials, jnp.int32),
            tiled(trials),
            tiled(cross_levels, jnp.int32),
            jax.ShapeDtypeStruct((4 * LANES, 2 * LANES), jnp.bfloat16),
        ),
        in_specs=[pl.BlockSpec(memory_space=pltpu.HBM)] * len(args),
        out_specs=(vmem,) * 5,
        scratch_shapes=[pltpu.VMEM(a.shape, a.dtype) for a in args[1:]]
        + [pltpu.SemaphoreType.DMA((len(args),))],
        compiler_params=room(4),
    )(*[pltpu.with_memory_space_constraint(a, pltpu.HBM) for a in args])
    plane = pl.pallas_call(
        functools.partial(plane_kernel, trials),
        out_shape=tiled(spans * past),
        in_specs=[vmem] * 5,
        out_specs=vmem,
        scratch_shapes=[
            pltpu.VMEM((rows, spans * span), filterbank.dtype),
            pltpu.VMEM((rows * spans * past, LANES), jnp.float32),
        ],
        compiler_params=room(6),
    )(own, other, shifts, gain, band)
    for level in range(cross_levels):
        last = level == cross_levels - 1
        mask = spans << level | 1
        there = lax.ppermute(plane, ("sub", "tm"), [(i, i ^ mask) for i in range(subs * spans)])
        scale = 1.0 / math.sqrt(rows * subs) if last else None
        plane = call(
            functools.partial(merge_kernel, level, scale),
            out_shape=(tiled(past),) * 2 if last else tiled(spans * past),
            in_specs=[vmem] * 3,
            out_specs=(vmem,) * 2 if last else vmem,
        )(plane, there, steps)
    keep, send = plane
    return call(
        functools.partial(last_kernel, cross_levels),
        out_shape=jax.ShapeDtypeStruct((trials, span), jnp.float32),
        in_specs=[vmem] * 2,
        out_specs=vmem,
    )(keep, lax.ppermute(send, "tm", swap))


def solution(mesh):
    return jax.shard_map(
        shards,
        mesh=mesh,
        in_specs=(P(("beam", "sub"), "tm"), P(("beam", "sub")), P(None, "sub"), P(None, "sub")),
        out_specs=P(("beam", "sub"), "tm"),
        check_vma=False,
    )
```

```python
import functools
import math

import jax
import jax.numpy as jnp
from jax import lax
from jax.experimental import pallas as pl
from jax.experimental.pallas import tpu as pltpu
from jax.sharding import PartitionSpec as P

LANES = 128
SUBLANES = 8
WINDOW = 31
HALF = WINDOW // 2


def iota(shape, axis):
    return lax.broadcasted_iota(jnp.int32, shape, axis)


def turned(x, index, axis):
    return jnp.take_along_axis(x, index, axis=axis, mode="promise_in_bounds")


def blocks_of(columns):
    return -(-columns // LANES)


def later(tiles, shift, count):
    source = iota(shift.shape, 1) - shift
    index = source & (LANES - 1)
    zero = jnp.zeros(shift.shape, jnp.float32)
    spun = [zero] + [turned(tile, index, 1) for tile in tiles]
    return [jnp.where(source >= 0, spun[b + 1], spun[b]) for b in range(count)]


def folded(tiles):
    row = iota(tiles[0].shape, 0)
    reach = SUBLANES // 2
    while reach:
        first = row & reach == 0
        tiles = [
            jnp.where(
                first,
                a + pltpu.roll(a, SUBLANES - reach, 0),
                b + pltpu.roll(b, reach, 0),
            )
            for a, b in zip(tiles[:reach], tiles[reach:])
        ]
        reach //= 2
    return tiles[0]


def table_kernel(*refs):
    fb_ref, *sources = refs[:4]
    own_ref, shifts_ref, gain_ref, steps_ref, band_ref = refs[4:9]
    held, sems = refs[9:12], refs[12]
    copies = [
        pltpu.make_async_copy(a, b, sems.at[i])
        for i, (a, b) in enumerate(zip([*sources, fb_ref], [*held, own_ref]))
    ]
    for copy in copies:
        copy.start()
    bp_ref, ld_ref, cd_ref = held
    rows = own_ref.shape[0]
    local_levels = ld_ref.shape[0]
    cross_levels, trials = cd_ref.shape
    grow = trials.bit_length() - 1
    parity = row_half(cross_levels)
    square = (rows, LANES)
    lane, row = iota(square, 1), iota(square, 0)
    inner, outer = row & (SUBLANES - 1), row >> 3
    half = (rows // 2, LANES)
    lane_h, row_h = iota(half, 1), iota(half, 0)
    inner_h, outer_h = row_h & (SUBLANES - 1), (row_h >> 3) * 2 + parity

    at, to = iota(band_ref.shape, 0) - LANES, iota(band_ref.shape, 1)
    band = jnp.where(at == to, float(WINDOW), 0.0) - jnp.where(jnp.abs(at - to) <= HALF, 1.0, 0.0)
    band_ref[...] = band.astype(jnp.bfloat16)
    pick = lane == inner * trials + outer
    pick_h = lane_h == inner_h * trials + outer_h
    uses = []
    for bit in range(local_levels - grow):
        uses.append((lane_h == (inner_h >> (bit + 1)) * trials + outer_h) & (inner_h >> bit & 1 == 1))
    on, off = jnp.ones((LANES, LANES), jnp.bfloat16), jnp.zeros((LANES, LANES), jnp.bfloat16)
    ones = jnp.concatenate(
        [jnp.concatenate([on, off], axis=1), jnp.concatenate([off, on], axis=1)], axis=0
    )

    for copy in copies[:-1]:
        copy.wait()
    tail = jnp.zeros(half, jnp.int32)
    for bit, use in enumerate(uses):
        tail = tail + jnp.where(use, ld_ref[grow + bit : grow + bit + 1, :], 0)
    parts = [jnp.where(pick_h, ld_ref[m : m + 1, :], 0) for m in range(grow)]
    parts += [tail] + [jnp.zeros(half, jnp.int32)] * ((grow + 1) % 2)
    parts = [part.astype(jnp.float32).astype(jnp.bfloat16) for part in parts]
    pieces = [jnp.concatenate(parts[i : i + 2], axis=0) for i in range(0, len(parts), 2)]
    rest = bp_ref[...]
    for _ in range(3):
        part = rest.astype(jnp.bfloat16).astype(jnp.float32)
        rest = rest - part
        pieces.append(jnp.where(pick, part, 0.0).astype(jnp.bfloat16))
    pieces += [off] * (len(pieces) % 2)
    pairs = [jnp.concatenate(pieces[i : i + 2], axis=1) for i in range(0, len(pieces), 2)]
    spread = jnp.dot(jnp.concatenate(pairs, axis=0), ones, preferred_element_type=jnp.float32)
    spread = [
        spread[i // 2 * rows : (i // 2 + 1) * rows, i % 2 * LANES : (i % 2 + 1) * LANES]
        for i in range(len(pieces))
    ]
    count = len(parts) // 2
    for i in range(count):
        shifts_ref[i * rows : (i + 1) * rows, :] = spread[i].astype(jnp.int32)
    gain_ref[...] = (spread[count] + spread[count + 1] + spread[count + 2]) * (1.0 / WINDOW)
    kept = (SUBLANES, trials)
    kept = iota(kept, 1) == iota(kept, 0) * 2 + parity
    for l in range(cross_levels):
        step = jnp.sum(jnp.where(kept, cd_ref[l : l + 1, :].astype(jnp.float32), 0.0), axis=1, keepdims=True)
        step = jnp.broadcast_to(step, (SUBLANES, LANES)).astype(jnp.int32)
        steps_ref[l * SUBLANES : (l + 1) * SUBLANES, :] = step
    copies[-1].wait()


def plane_kernel(trials, own_ref, other_ref, shifts_ref, gain_ref, band_ref, out_ref, whole_ref, level_ref):
    rows, span = own_ref.shape
    grow = trials.bit_length() - 1
    columns = whole_ref.shape[1]
    blocks = columns // LANES
    first_span = lax.axis_index("tm") == 0

    @pl.when(first_span)
    def _():
        whole_ref[:, :span] = own_ref[...]
        whole_ref[:, span:] = other_ref[...]

    @pl.when(jnp.logical_not(first_span))
    def _():
        whole_ref[:, :span] = other_ref[...]
        whole_ref[:, span:] = own_ref[...]

    for block in range(0, blocks, 2):
        low, high = max(block - 1, 0), min(block + 3, blocks)
        part = band_ref[(low - block + 1) * LANES : (high - block + 1) * LANES, :]
        got = jnp.dot(
            whole_ref[:, low * LANES : high * LANES], part, preferred_element_type=jnp.float32
        )
        level_ref[block * rows : (block + 1) * rows, :] = got[:, :LANES]
        level_ref[(block + 1) * rows : (block + 2) * rows, :] = got[:, LANES:]

    def band(e):
        scale = gain_ref[e * SUBLANES : (e + 1) * SUBLANES, :]
        return [level_ref[pl.ds(block * rows + e, SUBLANES, stride=trials), :] * scale for block in range(blocks)]

    def merged(low, high, at_row):
        moved = later(high, shifts_ref[at_row : at_row + SUBLANES, :], blocks)
        return [a + b for a, b in zip(low, moved)]

    plane = [[merged(band(2 * e), band(2 * e + 1), e * SUBLANES) for e in range(trials // 2)]]
    for m in range(1, grow):
        old, plane = plane, []
        for c in range(2):
            for i, held in enumerate(old):
                j = c * len(old) + i
                starts = [m * rows // 2 + ((e << m) + j) * SUBLANES for e in range(len(held) // 2)]
                plane.append([merged(held[2 * e], held[2 * e + 1], start) for e, start in enumerate(starts)])
    for j, held in enumerate(plane):
        at_row = grow * rows // 2 + j * SUBLANES
        moved = later(held[0], shifts_ref[at_row : at_row + SUBLANES, :], blocks)
        out_ref[pl.ds(j, SUBLANES, stride=SUBLANES), :] = folded(moved)


def row_half(cross_levels):
    half = lax.axis_index("tm")
    for level in range(cross_levels):
        half = half ^ (lax.axis_index("sub") >> level & 1)
    return half


def tile_of(ref, block):
    return ref[block * SUBLANES : (block + 1) * SUBLANES, :]


def merge_kernel(level, scale, own_ref, there_ref, steps_ref, out_ref, send_ref=None):
    is_upper = lax.axis_index("sub") >> level & 1 == 1
    blocks = own_ref.shape[0] // SUBLANES
    lower, upper = [], []
    for block in range(blocks):
        own, there = tile_of(own_ref, block), tile_of(there_ref, block)
        lower.append(jnp.where(is_upper, there, own))
        upper.append(jnp.where(is_upper, own, there))
    moved = later(upper, tile_of(steps_ref, level), blocks)
    new = [a + b for a, b in zip(lower, moved)]
    if scale is None:
        for block in range(blocks):
            out_ref[block * SUBLANES : (block + 1) * SUBLANES, :] = new[block]
        return
    first_span = lax.axis_index("tm") == 0
    past = blocks // 2
    for block in range(past):
        early, late = new[block] * scale, new[block + past] * scale
        out_ref[block * SUBLANES : (block + 1) * SUBLANES, :] = jnp.where(first_span, early, late)
        send_ref[block * SUBLANES : (block + 1) * SUBLANES, :] = jnp.where(first_span, late, early)


def last_kernel(cross_levels, keep_ref, there_ref, out_ref):
    is_even = row_half(cross_levels) == 0
    row = iota((SUBLANES, LANES), 0)
    for block in range(keep_ref.shape[0] // SUBLANES):
        keep, there = tile_of(keep_ref, block), tile_of(there_ref, block)
        even, odd = jnp.where(is_even, keep, there), jnp.where(is_even, there, keep)
        for part in range(2):
            source = (row >> 1) + part * (SUBLANES // 2)
            new = jnp.where(row & 1 == 0, turned(even, source, 0), turned(odd, source, 0))
            out_ref[part * SUBLANES : (part + 1) * SUBLANES, block * LANES : (block + 1) * LANES] = new


def shards(filterbank, bandpass, local_delays, cross_delays):
    rows, span = filterbank.shape
    cross_levels, trials = cross_delays.shape
    subs, spans = lax.axis_size("sub"), lax.axis_size("tm")
    local_levels = local_delays.shape[0]
    shift_max = span // 16
    grow = trials.bit_length() - 1
    past = span // LANES
    assert rows == LANES == trials * SUBLANES and trials == 2 * SUBLANES
    assert spans * past == SUBLANES and (local_levels - grow) * shift_max < LANES

    vmem = pl.BlockSpec(memory_space=pltpu.VMEM)
    tiled = lambda count, kind=jnp.float32: jax.ShapeDtypeStruct((count * SUBLANES, LANES), kind)
    room = lambda size: pltpu.CompilerParams(vmem_limit_bytes=size << 20)
    call = functools.partial(pl.pallas_call, compiler_params=room(1))
    swap = [(0, 1), (1, 0)]
    other = lax.ppermute(filterbank, "tm", swap)
    args = (filterbank, bandpass[None, :], local_delays, cross_delays)
    own, shifts, gain, steps, band = pl.pallas_call(
        table_kernel,
        out_shape=(
            jax.ShapeDtypeStruct(filterbank.shape, filterbank.dtype),
            tiled((grow + 2) // 2 * trials, jnp.int32),
            tiled(trials),
            tiled(cross_levels, jnp.int32),
            jax.ShapeDtypeStruct((4 * LANES, 2 * LANES), jnp.bfloat16),
        ),
        in_specs=[pl.BlockSpec(memory_space=pltpu.HBM)] * len(args),
        out_specs=(vmem,) * 5,
        scratch_shapes=[pltpu.VMEM(a.shape, a.dtype) for a in args[1:]]
        + [pltpu.SemaphoreType.DMA((len(args),))],
        compiler_params=room(4),
    )(*[pltpu.with_memory_space_constraint(a, pltpu.HBM) for a in args])
    plane = pl.pallas_call(
        functools.partial(plane_kernel, trials),
        out_shape=tiled(spans * past),
        in_specs=[vmem] * 5,
        out_specs=vmem,
        scratch_shapes=[
            pltpu.VMEM((rows, spans * span), filterbank.dtype),
            pltpu.VMEM((rows * spans * past, LANES), jnp.float32),
        ],
        compiler_params=room(6),
    )(own, other, shifts, gain, band)
    for level in range(cross_levels):
        last = level == cross_levels - 1
        mask = spans << level | 1
        there = lax.ppermute(plane, ("sub", "tm"), [(i, i ^ mask) for i in range(subs * spans)])
        scale = 1.0 / math.sqrt(rows * subs) if last else None
        plane = call(
            functools.partial(merge_kernel, level, scale),
            out_shape=(tiled(past),) * 2 if last else tiled(spans * past),
            in_specs=[vmem] * 3,
            out_specs=(vmem,) * 2 if last else vmem,
        )(plane, there, steps)
    keep, send = plane
    return call(
        functools.partial(last_kernel, cross_levels),
        out_shape=jax.ShapeDtypeStruct((trials, span), jnp.float32),
        in_specs=[vmem] * 2,
        out_specs=vmem,
    )(keep, lax.ppermute(send, "tm", swap))


def solution(mesh):
    return jax.shard_map(
        shards,
        mesh=mesh,
        in_specs=(P(("beam", "sub"), "tm"), P(("beam", "sub")), P(None, "sub"), P(None, "sub")),
        out_specs=P(("beam", "sub"), "tm"),
        check_vma=False,
    )
```

```python
import functools
import math

import jax
import jax.numpy as jnp
from jax import lax
from jax.experimental import pallas as pl
from jax.experimental.pallas import tpu as pltpu
from jax.sharding import PartitionSpec as P

LANES = 128
SUBLANES = 8
WINDOW = 31
HALF = WINDOW // 2


def iota(shape, axis):
    return lax.broadcasted_iota(jnp.int32, shape, axis)


def turned(x, index, axis):
    return jnp.take_along_axis(x, index, axis=axis, mode="promise_in_bounds")


def blocks_of(columns):
    return -(-columns // LANES)


def later(tiles, shift, count):
    source = iota(shift.shape, 1) - shift
    index = source & (LANES - 1)
    zero = jnp.zeros(shift.shape, jnp.float32)
    spun = [zero] + [turned(tile, index, 1) for tile in tiles]
    return [jnp.where(source >= 0, spun[b + 1], spun[b]) for b in range(count)]


def folded(tiles):
    row = iota(tiles[0].shape, 0)
    reach = SUBLANES // 2
    while reach:
        first = row & reach == 0
        tiles = [
            jnp.where(
                first,
                a + pltpu.roll(a, SUBLANES - reach, 0),
                b + pltpu.roll(b, reach, 0),
            )
            for a, b in zip(tiles[:reach], tiles[reach:])
        ]
        reach //= 2
    return tiles[0]


def table_kernel(*refs):
    fb_ref, *sources = refs[:4]
    own_ref, shifts_ref, gain_ref, steps_ref, band_ref = refs[4:9]
    held, sems = refs[9:12], refs[12]
    copies = [
        pltpu.make_async_copy(a, b, sems.at[i])
        for i, (a, b) in enumerate(zip([*sources, fb_ref], [*held, own_ref]))
    ]
    for copy in copies:
        copy.start()
    bp_ref, ld_ref, cd_ref = held
    rows = own_ref.shape[0]
    local_levels = ld_ref.shape[0]
    cross_levels, trials = cd_ref.shape
    grow = trials.bit_length() - 1
    parity = row_half(cross_levels)
    square = (rows, LANES)
    lane, row = iota(square, 1), iota(square, 0)
    inner, outer = row & (SUBLANES - 1), row >> 3
    half = (rows // 2, LANES)
    lane_h, row_h = iota(half, 1), iota(half, 0)
    inner_h, outer_h = row_h & (SUBLANES - 1), (row_h >> 3) * 2 + parity

    at, to = iota(band_ref.shape, 0) - LANES, iota(band_ref.shape, 1)
    band = jnp.where(at == to, float(WINDOW), 0.0) - jnp.where(jnp.abs(at - to) <= HALF, 1.0, 0.0)
    band_ref[...] = band.astype(jnp.bfloat16)
    pick = lane == inner * trials + outer
    pick_h = lane_h == inner_h * trials + outer_h
    uses = []
    for bit in range(local_levels - grow):
        uses.append((lane_h == (inner_h >> (bit + 1)) * trials + outer_h) & (inner_h >> bit & 1 == 1))
    on, off = jnp.ones((LANES, LANES), jnp.bfloat16), jnp.zeros((LANES, LANES), jnp.bfloat16)
    ones = jnp.concatenate(
        [jnp.concatenate([on, off], axis=1), jnp.concatenate([off, on], axis=1)], axis=0
    )

    for copy in copies[:-1]:
        copy.wait()
    tail = jnp.zeros(half, jnp.int32)
    for bit, use in enumerate(uses):
        tail = tail + jnp.where(use, ld_ref[grow + bit : grow + bit + 1, :], 0)
    parts = [jnp.where(pick_h, ld_ref[m : m + 1, :], 0) for m in range(grow)]
    parts += [tail] + [jnp.zeros(half, jnp.int32)] * ((grow + 1) % 2)
    parts = [part.astype(jnp.float32).astype(jnp.bfloat16) for part in parts]
    pieces = [jnp.concatenate(parts[i : i + 2], axis=0) for i in range(0, len(parts), 2)]
    rest = bp_ref[...]
    for _ in range(3):
        part = rest.astype(jnp.bfloat16).astype(jnp.float32)
        rest = rest - part
        pieces.append(jnp.where(pick, part, 0.0).astype(jnp.bfloat16))
    pieces += [off] * (len(pieces) % 2)
    pairs = [jnp.concatenate(pieces[i : i + 2], axis=1) for i in range(0, len(pieces), 2)]
    spread = jnp.dot(jnp.concatenate(pairs, axis=0), ones, preferred_element_type=jnp.float32)
    spread = [
        spread[i // 2 * rows : (i // 2 + 1) * rows, i % 2 * LANES : (i % 2 + 1) * LANES]
        for i in range(len(pieces))
    ]
    count = len(parts) // 2
    for i in range(count):
        shifts_ref[i * rows : (i + 1) * rows, :] = spread[i].astype(jnp.int32)
    gain_ref[...] = (spread[count] + spread[count + 1] + spread[count + 2]) * (1.0 / WINDOW)
    kept = (SUBLANES, trials)
    kept = iota(kept, 1) == iota(kept, 0) * 2 + parity
    for l in range(cross_levels):
        step = jnp.sum(jnp.where(kept, cd_ref[l : l + 1, :].astype(jnp.float32), 0.0), axis=1, keepdims=True)
        step = jnp.broadcast_to(step, (SUBLANES, LANES)).astype(jnp.int32)
        steps_ref[l * SUBLANES : (l + 1) * SUBLANES, :] = step
    copies[-1].wait()


def plane_kernel(trials, own_ref, other_ref, shifts_ref, gain_ref, band_ref, out_ref, whole_ref, level_ref):
    rows, span = own_ref.shape
    grow = trials.bit_length() - 1
    columns = whole_ref.shape[1]
    blocks = columns // LANES
    first_span = lax.axis_index("tm") == 0

    @pl.when(first_span)
    def _():
        whole_ref[:, :span] = own_ref[...]
        whole_ref[:, span:] = other_ref[...]

    @pl.when(jnp.logical_not(first_span))
    def _():
        whole_ref[:, :span] = other_ref[...]
        whole_ref[:, span:] = own_ref[...]

    for block in range(0, blocks, 2):
        low, high = max(block - 1, 0), min(block + 3, blocks)
        part = band_ref[(low - block + 1) * LANES : (high - block + 1) * LANES, :]
        got = jnp.dot(
            whole_ref[:, low * LANES : high * LANES], part, preferred_element_type=jnp.float32
        )
        level_ref[block * rows : (block + 1) * rows, :] = got[:, :LANES]
        level_ref[(block + 1) * rows : (block + 2) * rows, :] = got[:, LANES:]

    def band(e):
        scale = gain_ref[e * SUBLANES : (e + 1) * SUBLANES, :]
        return [level_ref[pl.ds(block * rows + e, SUBLANES, stride=trials), :] * scale for block in range(blocks)]

    def merged(low, high, at_row):
        moved = later(high, shifts_ref[at_row : at_row + SUBLANES, :], blocks)
        return [a + b for a, b in zip(low, moved)]

    plane = [[merged(band(2 * e), band(2 * e + 1), e * SUBLANES) for e in range(trials // 2)]]
    for m in range(1, grow):
        old, plane = plane, []
        for c in range(2):
            for i, held in enumerate(old):
                j = c * len(old) + i
                starts = [m * rows // 2 + ((e << m) + j) * SUBLANES for e in range(len(held) // 2)]
                plane.append([merged(held[2 * e], held[2 * e + 1], start) for e, start in enumerate(starts)])
    for j, held in enumerate(plane):
        at_row = grow * rows // 2 + j * SUBLANES
        moved = later(held[0], shifts_ref[at_row : at_row + SUBLANES, :], blocks)
        out_ref[pl.ds(j, SUBLANES, stride=SUBLANES), :] = folded(moved)


def row_half(cross_levels):
    half = lax.axis_index("tm")
    for level in range(cross_levels - 1):
        half = half ^ (lax.axis_index("sub") >> level & 1)
    return half


def tile_of(ref, block):
    return ref[block * SUBLANES : (block + 1) * SUBLANES, :]


def merge_kernel(level, scale, own_ref, there_ref, steps_ref, out_ref, send_ref=None):
    is_upper = lax.axis_index("sub") >> level & 1 == 1
    blocks = own_ref.shape[0] // SUBLANES
    lower, upper = [], []
    for block in range(blocks):
        own, there = tile_of(own_ref, block), tile_of(there_ref, block)
        lower.append(jnp.where(is_upper, there, own))
        upper.append(jnp.where(is_upper, own, there))
    moved = later(upper, tile_of(steps_ref, level), blocks)
    new = [a + b for a, b in zip(lower, moved)]
    if scale is None:
        for block in range(blocks):
            out_ref[block * SUBLANES : (block + 1) * SUBLANES, :] = new[block]
        return
    first_span = lax.axis_index("tm") == 0
    past = blocks // 2
    for block in range(past):
        early, late = new[block] * scale, new[block + past] * scale
        out_ref[block * SUBLANES : (block + 1) * SUBLANES, :] = jnp.where(first_span, early, late)
        send_ref[block * SUBLANES : (block + 1) * SUBLANES, :] = jnp.where(first_span, late, early)


def last_kernel(cross_levels, keep_ref, there_ref, out_ref):
    is_even = row_half(cross_levels) == 0
    row = iota((SUBLANES, LANES), 0)
    for block in range(keep_ref.shape[0] // SUBLANES):
        keep, there = tile_of(keep_ref, block), tile_of(there_ref, block)
        even, odd = jnp.where(is_even, keep, there), jnp.where(is_even, there, keep)
        for part in range(2):
            source = (row >> 1) + part * (SUBLANES // 2)
            new = jnp.where(row & 1 == 0, turned(even, source, 0), turned(odd, source, 0))
            out_ref[part * SUBLANES : (part + 1) * SUBLANES, block * LANES : (block + 1) * LANES] = new


def shards(filterbank, bandpass, local_delays, cross_delays):
    rows, span = filterbank.shape
    cross_levels, trials = cross_delays.shape
    subs, spans = lax.axis_size("sub"), lax.axis_size("tm")
    local_levels = local_delays.shape[0]
    shift_max = span // 16
    grow = trials.bit_length() - 1
    past = span // LANES
    assert rows == LANES == trials * SUBLANES and trials == 2 * SUBLANES
    assert spans * past == SUBLANES and (local_levels - grow) * shift_max < LANES

    vmem = pl.BlockSpec(memory_space=pltpu.VMEM)
    tiled = lambda count, kind=jnp.float32: jax.ShapeDtypeStruct((count * SUBLANES, LANES), kind)
    room = lambda size: pltpu.CompilerParams(vmem_limit_bytes=size << 20)
    call = functools.partial(pl.pallas_call, compiler_params=room(1))
    swap = [(0, 1), (1, 0)]
    other = lax.ppermute(filterbank, "tm", swap)
    args = (filterbank, bandpass[None, :], local_delays, cross_delays)
    own, shifts, gain, steps, band = pl.pallas_call(
        table_kernel,
        out_shape=(
            jax.ShapeDtypeStruct(filterbank.shape, filterbank.dtype),
            tiled((grow + 2) // 2 * trials, jnp.int32),
            tiled(trials),
            tiled(cross_levels, jnp.int32),
            jax.ShapeDtypeStruct((4 * LANES, 2 * LANES), jnp.bfloat16),
        ),
        in_specs=[pl.BlockSpec(memory_space=pltpu.HBM)] * len(args),
        out_specs=(vmem,) * 5,
        scratch_shapes=[pltpu.VMEM(a.shape, a.dtype) for a in args[1:]]
        + [pltpu.SemaphoreType.DMA((len(args),))],
        compiler_params=room(4),
    )(*[pltpu.with_memory_space_constraint(a, pltpu.HBM) for a in args])
    plane = pl.pallas_call(
        functools.partial(plane_kernel, trials),
        out_shape=tiled(spans * past),
        in_specs=[vmem] * 5,
        out_specs=vmem,
        scratch_shapes=[
            pltpu.VMEM((rows, spans * span), filterbank.dtype),
            pltpu.VMEM((rows * spans * past, LANES), jnp.float32),
        ],
        compiler_params=room(6),
    )(own, other, shifts, gain, band)
    for level in range(cross_levels):
        last = level == cross_levels - 1
        mask = spans << level | (0 if last else 1)
        there = lax.ppermute(plane, ("sub", "tm"), [(i, i ^ mask) for i in range(subs * spans)])
        scale = 1.0 / math.sqrt(rows * subs) if last else None
        plane = call(
            functools.partial(merge_kernel, level, scale),
            out_shape=(tiled(past),) * 2 if last else tiled(spans * past),
            in_specs=[vmem] * 3,
            out_specs=(vmem,) * 2 if last else vmem,
        )(plane, there, steps)
    keep, send = plane
    return call(
        functools.partial(last_kernel, cross_levels),
        out_shape=jax.ShapeDtypeStruct((trials, span), jnp.float32),
        in_specs=[vmem] * 2,
        out_specs=vmem,
    )(keep, lax.ppermute(send, "tm", swap))


def solution(mesh):
    return jax.shard_map(
        shards,
        mesh=mesh,
        in_specs=(P(("beam", "sub"), "tm"), P(("beam", "sub")), P(None, "sub"), P(None, "sub")),
        out_specs=P(("beam", "sub"), "tm"),
        check_vma=False,
    )
```
